32 devices in a mesh: rows: 8 (over z, y), hid: 4 (over x, core).
Axes of the slice: x: 2, y: 2, z: 4, core: 2. Of those that a mesh axis runs over, the one named last changes fastest.
Arguments:
- features: bfloat16 [32768, 256], P(('rows', 'hid')), may hold values from -6 to 6
- w_expand: float32 [256, 16, 256], P('rows', None, 'hid'), may hold values from -0.375 to 0.375
- w_reduce: float32 [16, 256, 256], P(None, 'hid', 'rows'), may hold values from -1.5 to 1.5
- biases: float32 [2, 16, 256], P(None, None, 'hid'), may hold values from -1.8 to 1.8
- w_select: float32 [256, 60], P('rows'), may hold values from -0.1875 to 0.1875
- grad_mix: bfloat16 [32768, 3, 256], P(('rows', 'hid')), may hold values from -6 to 6
- m_expand: float32 [256, 16, 256], P('rows', None, 'hid'), may hold values from -271.529 to 271.529
- v_expand: float32 [256, 16, 256], P('rows', None, 'hid'), may hold values from 2048 to 8192
- m_reduce: float32 [16, 256, 256], P(None, 'hid', 'rows'), may hold values from -70.59754 to 70.59754
- v_reduce: float32 [16, 256, 256], P(None, 'hid', 'rows'), may hold values from 140.8 to 563.2
- m_biases: float32 [2, 16, 256], P(None, None, 'hid'), may hold values from -203.64676 to 203.64676
- v_biases: float32 [2, 16, 256], P(None, None, 'hid'), may hold values from 768 to 3072
- m_select: float32 [256, 60], P('rows'), may hold values from -4344.464 to 4344.464
- v_select: float32 [256, 60], P('rows'), may hold values from 524288 to 2097152
Outputs:
- mixed: bfloat16 [32768, 3, 256], P(('rows', 'hid'))
- grad_features: bfloat16 [32768, 256], P(('rows', 'hid'))
- mean_expand: float32 [256, 16, 256], P('rows', None, 'hid')
- square_expand: float32 [256, 16, 256], P('rows', None, 'hid')
- updated_expand: float32 [256, 16, 256], P('rows', None, 'hid')
- mean_reduce: float32 [16, 256, 256], P(None, 'hid', 'rows')
- square_reduce: float32 [16, 256, 256], P(None, 'hid', 'rows')
- updated_reduce: float32 [16, 256, 256], P(None, 'hid', 'rows')
- mean_biases: float32 [2, 16, 256], P(None, None, 'hid')
- square_biases: float32 [2, 16, 256], P(None, None, 'hid')
- updated_biases: float32 [2, 16, 256], P(None, None, 'hid')
- mean_select: float32 [256, 60], P('rows')
- square_select: float32 [256, 60], P('rows')
- updated_select: float32 [256, 60], P('rows')
The draws below stay inside these ranges and needn't reach their ends.
All inputs are finite; a program needn't handle non-finite values.
Results may differ from the reference program's by a relative error of at most 0.012.
Values may be sent and summed in bfloat16 or wider, within the bound.
No kernel may reach another device: no remote copies, remote signals or barrier semaphores. Data moves between devices by JAX's collectives and lax.ppermute only.
A program may use at most 256 MiB of HBM per device.

```python
import math
import jax
import jax.numpy as jnp
from jax import lax

D = 256
H = 256
TASKS = 3
SELECT = 4
BITS = 4
STEP = 5
TOK_DEV = 4096
EXPERTS = 16
GATES = 60
TOKENS = 32768


def level_of(key, shape, split, low, high):
    level, own = 1.0, jax.random.fold_in(key, 6)
    for dim, shards_of in split:
        steps = jnp.exp(jax.random.uniform(jax.random.fold_in(own, dim), (shards_of,), jnp.float32, low / len(split), high / len(split)))
        level = level * jnp.repeat(steps, shape[dim] // shards_of).reshape([-1 if axis == dim else 1 for axis in range(len(shape))])
    return level


def gaussian(own_key, extent, width, bound, pieces=(), kind=jnp.bfloat16):
    drawn = jax.random.normal(own_key, extent, jnp.float32) * width
    if len(pieces) > 0:
        drawn = level_of(own_key, extent, pieces, -0.22, 0.18) * drawn
    return jnp.clip(drawn, min=-bound, max=bound).astype(kind)


def setup_inputs(seed: int = 0) -> dict:
    streams_of = jax.random.split(jax.random.key(seed), 15)
    return {
        "features": gaussian(streams_of[0], (TOKENS, D), 1.0, 6.0, ((0, 32),)),
        "w_expand": gaussian(streams_of[1], (D, EXPERTS, H), D ** -0.5, 0.375, ((0, 8), (2, 4)), jnp.float32),
        "w_reduce": gaussian(streams_of[2], (EXPERTS, H, D), (H // 16) ** -0.5, 1.5, ((1, 4), (2, 8)), jnp.float32),
        "biases": gaussian(streams_of[3], (2, EXPERTS, D), 0.3, 1.8, ((2, 4),), jnp.float32),
        "w_select": gaussian(streams_of[4], (D, GATES), (D * 4) ** -0.5, 0.1875, ((0, 8),), jnp.float32),
        "grad_mix": gaussian(streams_of[5], (TOKENS, TASKS, D), 1.0, 6.0, ((0, 32),)),
        "m_expand": gaussian(streams_of[6], (D, EXPERTS, H), (4.0 * TOKENS ** 0.5 / EXPERTS), 271.529, ((0, 8), (2, 4)), jnp.float32),
        "v_expand": jnp.clip(jnp.exp(math.log(8192.0) - 1.3862944 * jax.random.uniform(streams_of[7], (D, EXPERTS, H), jnp.float32) ** level_of(streams_of[7], (D, EXPERTS, H), ((0, 8), (2, 4)), -0.2, 0.2)), 2048.0, 8192.0),
        "m_reduce": gaussian(streams_of[8], (EXPERTS, H, D), (1.04 * TOKENS ** 0.5 / EXPERTS), 70.59754, ((1, 4), (2, 8)), jnp.float32),
        "v_reduce": jnp.clip(jnp.exp(math.log(563.2) - 1.3862944 * jax.random.uniform(streams_of[9], (EXPERTS, H, D), jnp.float32) ** level_of(streams_of[9], (EXPERTS, H, D), ((1, 4), (2, 8)), -0.2, 0.2)), 140.8, 563.2),
        "m_biases": gaussian(streams_of[10], (2, EXPERTS, D), (3.0 * TOKENS ** 0.5 / EXPERTS), 203.64676, ((2, 4),), jnp.float32),
        "v_biases": jnp.clip(jnp.exp(math.log(3072.0) - 1.3862944 * jax.random.uniform(streams_of[11], (2, EXPERTS, D), jnp.float32) ** level_of(streams_of[11], (2, EXPERTS, D), ((2, 4),), -0.2, 0.2)), 768.0, 3072.0),
        "m_select": gaussian(streams_of[12], (D, GATES), (4.0 * TOKENS ** 0.5), 4344.464, ((0, 8),), jnp.float32),
        "v_select": jnp.clip(jnp.exp(math.log(2097152) - 1.3862944 * jax.random.uniform(streams_of[13], (D, GATES), jnp.float32) ** level_of(streams_of[13], (D, GATES), ((0, 8),), -0.2, 0.2)), 524288.0, 2097152),
    }


@jax.custom_vjp
def low(v):
    return lax.optimization_barrier(v.astype(jnp.bfloat16)).astype(jnp.float32)

@jax.custom_vjp
def low_back(v):
    return v

def low_keep(v):
    return (low(v), None)

def low_pass(kept, grad):
    return (grad,)

def back_keep(v):
    return (v, None)

def back_low(kept, grad):
    return (low(grad),)
low.defvjp(low_keep, low_pass)
low_back.defvjp(back_keep, back_low)
GAMMA = 2.0
RATE = 0.05
DECAY = 0.01
EPSILON = 1e-08
BETA_ONE = 0.5
BETA_TWO = 0.5

def selector_gate(logits_t, tasks, selectors, digits):
    count_rows = logits_t.shape[1]
    cut = tasks * selectors * digits
    zvals = logits_t[:cut].reshape(tasks, selectors, digits, count_rows)
    avals = logits_t[cut:].reshape(tasks, selectors, count_rows)
    clipped = jnp.clip(zvals, -0.5 * GAMMA, 0.5 * GAMMA)
    smooth = clipped * (1.5 / GAMMA - 2.0 / GAMMA ** 3 * clipped * clipped) + 0.5
    experts_n = 2 ** digits
    route = jnp.ones((tasks, selectors, experts_n, count_rows), jnp.float32)
    for digit in range(digits):
        code = (jnp.arange(experts_n) // 2 ** digit % 2).astype(jnp.float32)[:, None]
        chosen = smooth[:, :, digit, None, :]
        route = route * (code * chosen + (1.0 - code) * (1.0 - chosen))
    alpha = jax.nn.softmax(avals, axis=1)
    return lax.optimization_barrier(jnp.sum(alpha[:, :, None, :] * route, axis=1))

def forward(feat, w_expand, w_reduce, biases, w_select):
    count_rows = feat.shape[0]
    pre = jnp.dot(feat, low(w_expand).reshape(D, EXPERTS * H), precision=lax.Precision.HIGHEST) + biases[0].reshape(-1)
    pre = low_back(pre)
    hidden = low(jax.nn.silu(pre))
    logits_t = low_back(jnp.dot(low(w_select).T, feat.T, precision=lax.Precision.HIGHEST))
    gates = selector_gate(logits_t, TASKS, SELECT, BITS)
    gate_rows = jnp.transpose(gates, (2, 0, 1))
    weighted = low(hidden.reshape(count_rows, 1, EXPERTS, H) * gate_rows[:, :, :, None])
    weighted = weighted.reshape(count_rows * TASKS, EXPERTS * H)
    result = jnp.dot(weighted, low(w_reduce).reshape(EXPERTS * H, D), precision=lax.Precision.HIGHEST)
    result = result.reshape(count_rows, TASKS, D)
    return result + jnp.einsum('nte,ed->ntd', gate_rows, biases[1], precision=lax.Precision.HIGHEST)

def adamw(weight, grad, first, second):
    first = BETA_ONE * first + (1.0 - BETA_ONE) * grad
    second = BETA_TWO * second + (1.0 - BETA_TWO) * grad * grad
    mhat = first / (1.0 - BETA_ONE ** STEP)
    vhat = second / (1.0 - BETA_TWO ** STEP)
    weight = weight - RATE * (mhat / (jnp.sqrt(vhat) + EPSILON) + DECAY * weight)
    return (first, second, weight)

def reference(features, w_expand, w_reduce, biases, w_select, grad_mix, m_expand, v_expand, m_reduce, v_reduce, m_biases, v_biases, m_select, v_select):
    blocks = TOKENS // TOK_DEV
    feat = features.astype(jnp.float32).reshape(blocks, TOK_DEV, D)
    cotan = grad_mix.astype(jnp.float32).reshape(blocks, TOK_DEV, TASKS, D)
    params = (w_expand, w_reduce, biases, w_select)

    def one_block(carry, item):
        block_feat, block_cot = item
        result, pull = jax.vjp(forward, block_feat, *params)
        grads = pull(block_cot)
        carry = tuple((total + part for total, part in zip(carry, grads[1:])))
        return (carry, (result.astype(jnp.bfloat16), grads[0].astype(jnp.bfloat16)))
    zeros_init = tuple((jnp.zeros_like(param) for param in params))
    totals, (mixed, grad_feat) = lax.scan(one_block, zeros_init, (feat, cotan))
    mixed = mixed.reshape(TOKENS, TASKS, D)
    grad_feat = grad_feat.reshape(TOKENS, D)
    me, se, ue = adamw(w_expand, totals[0], m_expand, v_expand)
    mr, sr, ur = adamw(w_reduce, totals[1], m_reduce, v_reduce)
    mb, sb, ub = adamw(biases, totals[2], m_biases, v_biases)
    ms, ss, us = adamw(w_select, totals[3], m_select, v_select)
    return (mixed, grad_feat, me, se, ue, mr, sr, ur, mb, sb, ub, ms, ss, us)
```

```python
import functools

import jax
import jax.numpy as jnp
import numpy as np
from jax import lax
from jax.experimental import pallas as pl
from jax.experimental.pallas import tpu as pltpu
from jax.sharding import PartitionSpec as P

TASKS = 3
SELECT = 4
BITS = 4
STEP = 5
GAMMA = 2.0
RATE = 0.05
DECAY = 0.01
EPSILON = 1e-08
BETA_ONE = 0.5
BETA_TWO = 0.5

BF = jnp.bfloat16
F32 = jnp.float32
HIGHEST = lax.Precision.HIGHEST
TPAD = 8
GROUPS = BITS * SELECT + SELECT
GROWS = GROUPS * TPAD
ONES = 16
TILE = 512
MIB = 1 << 20


def dot(a, b, ca, cb, precision=None):
    return lax.dot_general(
        a, b, (((ca,), (cb,)), ((), ())), preferred_element_type=F32, precision=precision
    )


def params(mib):
    return pltpu.CompilerParams(
        vmem_limit_bytes=mib * MIB, dimension_semantics=("arbitrary",)
    )


VMEM = functools.partial(pl.BlockSpec, memory_space=pltpu.VMEM)


def gate_parts(z_of, a_of, high):
    smooth, clipped = {}, {}
    for k in range(SELECT):
        for b in range(BITS):
            v = jnp.clip(z_of(b, k), -0.5 * GAMMA, 0.5 * GAMMA)
            clipped[b, k] = v
            smooth[b, k] = v * (1.5 / GAMMA - 2.0 / GAMMA**3 * v * v) + 0.5
    a = [a_of(k) for k in range(SELECT)]
    top = functools.reduce(jnp.maximum, a)
    ex = [jnp.exp(v - top) for v in a]
    inv = 1.0 / functools.reduce(jnp.add, ex)
    alpha = [v * inv for v in ex]
    last = BITS - 1
    f_high = [
        high * smooth[last, k] + (1.0 - high) * (1.0 - smooth[last, k]) for k in range(SELECT)
    ]
    return alpha, smooth, clipped, f_high


def fac(smooth, b, k, bit):
    return smooth[b, k] if bit else 1.0 - smooth[b, k]


def prep_kernel(core, perm, order, sel, xo, xr, go, gr, xt, gt, cc, gates, logits, selp, gb1):
    i = pl.program_id(0)
    half = pl.num_programs(0) // 2
    own = i < half
    high = core[0].astype(F32)

    @pl.when(i == 0)
    def _():
        selp[...] = dot(order[...], sel[...], 1, 1).astype(BF)
        gb1[...] = jnp.zeros_like(gb1)

    x = jnp.where(own, xo[...], xr[...])
    x_t = dot(perm[...], x, 1, 1).astype(BF)
    width = x_t.shape[0]
    xt[0:width, :] = x_t
    xt[width : width + ONES, :] = jnp.ones((ONES, x_t.shape[1]), BF)
    lg = dot(selp[...], x_t, 1, 0)
    logits[...] = lg

    def z_of(b, k):
        at = (b * SELECT + k) * TPAD
        return lg[at : at + TPAD]

    def a_of(k):
        at = (BITS * SELECT + k) * TPAD
        return lg[at : at + TPAD]

    alpha, smooth, _, f_high = gate_parts(z_of, a_of, high)
    gate = [None] * 8
    for k in range(SELECT):
        base = alpha[k] * f_high[k]
        for e2 in range(2):
            w2 = base * fac(smooth, 2, k, e2)
            for e1 in range(2):
                w1 = w2 * fac(smooth, 1, k, e1)
                for e0 in range(2):
                    e = 4 * e2 + 2 * e1 + e0
                    w0 = w1 * fac(smooth, 0, k, e0)
                    gate[e] = w0 if gate[e] is None else gate[e] + w0
    g_t = []
    for t in range(TASKS):
        g = jnp.where(own, go[t], gr[t])
        g = dot(perm[...], g, 1, 1)
        gt[t] = g.astype(BF)
        g_t.append(g)
    ones = jnp.ones((8, x_t.shape[1]), BF)
    for e in range(8):
        gates[e] = gate[e]
        c = gate[e][0:1] * g_t[0]
        for t in range(1, TASKS):
            c = c + gate[e][t : t + 1] * g_t[t]
        c = c.astype(BF)
        cc[e] = c
        gb1[e] += dot(ones, c, 1, 1)


def prep(core, perm, order, sel, x_own, x_recv, g_own, g_recv):
    rows, width = x_own.shape
    total = 2 * rows
    steps = total // TILE
    half = steps // 2
    lo = lambda i: jnp.minimum(i, half - 1)
    hi = lambda i: jnp.maximum(i - half, 0)
    whole = lambda shape: VMEM(shape, lambda i: (0,) * len(shape))
    return pl.pallas_call(
        prep_kernel,
        grid=(steps,),
        out_shape=(
            jax.ShapeDtypeStruct((width + ONES, total), BF),
            jax.ShapeDtypeStruct((TASKS, width, total), BF),
            jax.ShapeDtypeStruct((8, width, total), BF),
            jax.ShapeDtypeStruct((8, TPAD, total), F32),
            jax.ShapeDtypeStruct((GROWS, total), F32),
            jax.ShapeDtypeStruct((GROWS, width), BF),
            jax.ShapeDtypeStruct((8, 8, width), F32),
        ),
        in_specs=[
            pl.BlockSpec(memory_space=pltpu.SMEM),
            whole(perm.shape),
            whole(order.shape),
            whole(sel.shape),
            VMEM((TILE, width), lambda i: (lo(i), 0)),
            VMEM((TILE, width), lambda i: (hi(i), 0)),
            VMEM((TASKS, TILE, width), lambda i: (0, lo(i), 0)),
            VMEM((TASKS, TILE, width), lambda i: (0, hi(i), 0)),
        ],
        out_specs=(
            VMEM((width + ONES, TILE), lambda i: (0, i)),
            VMEM((TASKS, width, TILE), lambda i: (0, 0, i)),
            VMEM((8, width, TILE), lambda i: (0, 0, i)),
            VMEM((8, TPAD, TILE), lambda i: (0, 0, i)),
            VMEM((GROWS, TILE), lambda i: (0, i)),
            whole((GROWS, width)),
            whole((8, 8, width)),
        ),
        compiler_params=params(48),
        cost_estimate=pl.CostEstimate(
            flops=2 * total * width * width * 5, bytes_accessed=18 * MIB, transcendentals=0
        ),
    )(core, perm, order, sel, x_own, x_recv, g_own, g_recv)


def critical_kernel(
    table, w_lo, w_hi, xt, cc, b0, g_lo, g_hi, hid, gp, wun, gb0, wbuf, gbuf
):
    e = pl.program_id(0)
    last = pl.num_programs(0) - 1
    blocks, _, _, depth, lanes = w_lo.shape
    width = depth * blocks
    total = xt.shape[1]

    @pl.when(e == 0)
    def _():
        wbuf[0:blocks] = w_lo[...]
        wbuf[blocks : 2 * blocks] = w_hi[...]

    for q in range(blocks):
        for side in range(2):
            at = table[2 * q + side]
            for which in range(2):
                wun[0, which, q * depth : (q + 1) * depth, side * lanes : (side + 1) * lanes] = (
                    wbuf[at, which, e]
                )
    e_t = (wun[0, 0] * 0.5).T
    r = (wun[0, 1] * 0.5).T
    bias = jnp.concatenate([b0[0]] * (TILE // b0.shape[2]), axis=1)
    for i in range(total // TILE):
        part = slice(i * TILE, (i + 1) * TILE)
        u = dot(e_t, xt[0:width, part], 1, 0) + bias
        t = jnp.tanh(u)
        plus = 1.0 + t
        h = u * plus
        hid[0, :, part] = h.astype(BF)
        gh = dot(r, cc[0, :, part], 1, 0)
        gp[0, :, part] = (gh * (plus + h * (1.0 - t))).astype(BF)
    g_e = dot(xt[...], gp[0], 1, 1)
    g_r = dot(cc[0], hid[0], 1, 1)
    gb0[0] = g_e[width : width + 8]
    for q in range(blocks):
        for side in range(2):
            at = table[2 * q + side]
            rows, cols = slice(q * depth, (q + 1) * depth), slice(side * lanes, (side + 1) * lanes)
            gbuf[at, 0, e] = g_e[rows, cols].astype(BF)
            gbuf[at, 1, e] = g_r[rows, cols].astype(BF)

    @pl.when(e == last)
    def _():
        g_lo[...] = gbuf[0:blocks]
        g_hi[...] = gbuf[blocks : 2 * blocks]


def critical(table, w_lo, w_hi, xt, cc, b0, first):
    blocks, _, chunk, depth, lanes = w_lo.shape
    width, total = blocks * depth, xt.shape[1]
    hidden = 2 * lanes
    whole = lambda shape: VMEM(shape, lambda e: (0,) * len(shape))
    per = lambda *shape: VMEM((1, *shape), lambda e: (e,) + (0,) * len(shape))
    at = lambda *shape: VMEM((1, *shape), lambda e: (e + first,) + (0,) * len(shape))
    return pl.pallas_call(
        critical_kernel,
        grid=(chunk,),
        out_shape=(
            jax.ShapeDtypeStruct(w_lo.shape, BF),
            jax.ShapeDtypeStruct(w_lo.shape, BF),
            jax.ShapeDtypeStruct((chunk, hidden, total), BF),
            jax.ShapeDtypeStruct((chunk, hidden, total), BF),
            jax.ShapeDtypeStruct((chunk, 2, width, hidden), BF),
            jax.ShapeDtypeStruct((chunk, 8, hidden), F32),
        ),
        in_specs=[
            pl.BlockSpec(memory_space=pltpu.SMEM),
            whole(w_lo.shape),
            whole(w_hi.shape),
            whole(xt.shape),
            at(width, total),
            at(hidden, b0.shape[2]),
        ],
        out_specs=(
            whole(w_lo.shape),
            whole(w_lo.shape),
            per(hidden, total),
            per(hidden, total),
            per(2, width, hidden),
            per(8, hidden),
        ),
        scratch_shapes=[
            pltpu.VMEM((2 * blocks, 2, chunk, depth, lanes), BF),
            pltpu.VMEM((2 * blocks, 2, chunk, depth, lanes), BF),
        ],
        compiler_params=params(48),
        cost_estimate=pl.CostEstimate(
            flops=8 * chunk * total * width * hidden,
            bytes_accessed=chunk * 4 * MIB,
            transcendentals=chunk * total * hidden,
        ),
    )(table, w_lo, w_hi, xt, cc, b0)


def rest_kernel(
    wun, hid, gp, gt, gates, b1, mix_in, gx_in, mix_own, mix_other, gx, gg, mix_acc, gx_acc, *, first
):
    e = pl.program_id(0)
    last = pl.num_programs(0) - 1
    width, total = gx_acc.shape
    rows = total // 2

    @pl.when(e == 0)
    def _():
        if first:
            mix_acc[...] = jnp.zeros_like(mix_acc)
            gx_acc[...] = jnp.zeros_like(gx_acc)
        else:
            mix_acc[...] = mix_in[...]
            gx_acc[...] = gx_in[...]

    gg[...] = jnp.zeros_like(gg)
    bias = jnp.concatenate([b1[0]] * (TILE // b1.shape[2]), axis=1)
    for i in range(total // TILE):
        part = slice(i * TILE, (i + 1) * TILE)
        y = dot(wun[0, 1], hid[0, :, part], 1, 0) + bias
        gx_acc[:, part] += dot(wun[0, 0], gp[0, :, part], 1, 0)
        for t in range(TASKS):
            mix_acc[t, :, part] += gates[0, t : t + 1, part] * y
            gg[0, t : t + 1, part] = jnp.sum(
                gt[t, :, part].astype(F32) * y, axis=0, keepdims=True
            )

    @pl.when(e == last)
    def _():
        mix_own[...] = mix_acc[:, :, 0:rows].astype(mix_own.dtype)
        mix_other[...] = mix_acc[:, :, rows:total].astype(mix_other.dtype)
        gx[...] = gx_acc[...]


def rest(wun, hid, gp, gt, gates, b1):
    count, _, width, hidden = wun.shape
    total = gt.shape[2]
    whole = lambda shape: VMEM(shape, lambda e: (0,) * len(shape))
    per = lambda *shape: VMEM((1, *shape), lambda e: (e,) + (0,) * len(shape))
    none = jnp.zeros((8, 128), F32)
    return pl.pallas_call(
        functools.partial(rest_kernel, first=True),
        grid=(count,),
        out_shape=(
            jax.ShapeDtypeStruct((TASKS, width, total // 2), BF),
            jax.ShapeDtypeStruct((TASKS, width, total // 2), BF),
            jax.ShapeDtypeStruct((width, total), F32),
            jax.ShapeDtypeStruct((count, TPAD, total), F32),
        ),
        in_specs=[
            per(2, width, hidden),
            per(hidden, total),
            per(hidden, total),
            whole(gt.shape),
            per(TPAD, total),
            per(width, b1.shape[2]),
            whole(none.shape),
            whole(none.shape),
        ],
        out_specs=(
            whole((TASKS, width, total // 2)),
            whole((TASKS, width, total // 2)),
            whole((width, total)),
            per(TPAD, total),
        ),
        scratch_shapes=[
            pltpu.VMEM((TASKS, width, total), F32),
            pltpu.VMEM((width, total), F32),
        ],
        compiler_params=params(56),
        cost_estimate=pl.CostEstimate(
            flops=4 * count * total * width * hidden,
            bytes_accessed=count * 3 * MIB,
            transcendentals=0,
        ),
    )(wun, hid, gp, gt, gates, b1, none, none)


def gate_back_kernel(core, order, selp, logits, gg, xo, xr, gx_in, gx, gsel, acc):
    i = pl.program_id(0)
    last = pl.num_programs(0) - 1
    own = i < pl.num_programs(0) // 2
    high = core[0].astype(F32)
    sign = 2.0 * high - 1.0

    def z_of(b, k):
        at = (b * SELECT + k) * TPAD
        return logits[at : at + TPAD]

    def a_of(k):
        at = (BITS * SELECT + k) * TPAD
        return logits[at : at + TPAD]

    alpha, smooth, clipped, f_high = gate_parts(z_of, a_of, high)
    out = [None] * GROUPS
    d_alpha = []
    for k in range(SELECT):
        f = [[fac(smooth, b, k, bit) for bit in range(2)] for b in range(BITS - 1)]
        t0 = d0 = d1 = d2 = None
        low = {}
        dif = {}
        for e2 in range(2):
            for e1 in range(2):
                p, q = gg[4 * e2 + 2 * e1], gg[4 * e2 + 2 * e1 + 1]
                low[e2, e1] = f[0][0] * p + f[0][1] * q
                dif[e2, e1] = q - p
        mid = [f[1][0] * low[e2, 0] + f[1][1] * low[e2, 1] for e2 in range(2)]
        mid1 = [low[e2, 1] - low[e2, 0] for e2 in range(2)]
        mid0 = [f[1][0] * dif[e2, 0] + f[1][1] * dif[e2, 1] for e2 in range(2)]
        t0 = f[2][0] * mid[0] + f[2][1] * mid[1]
        d2 = mid[1] - mid[0]
        d1 = f[2][0] * mid1[0] + f[2][1] * mid1[1]
        d0 = f[2][0] * mid0[0] + f[2][1] * mid0[1]
        d_alpha.append(f_high[k] * t0)
        scale = alpha[k] * f_high[k]
        for b, d in enumerate((scale * d0, scale * d1, scale * d2, alpha[k] * sign * t0)):
            v = clipped[b, k]
            out[b * SELECT + k] = d * (1.5 / GAMMA - 6.0 / GAMMA**3 * v * v)
    total = functools.reduce(jnp.add, [a * d for a, d in zip(alpha, d_alpha)])
    for k in range(SELECT):
        out[BITS * SELECT + k] = alpha[k] * (d_alpha[k] - total)
    gl = jnp.concatenate(out, axis=0).astype(BF)
    gx[...] = (gx_in[...] + dot(selp[...], gl, 0, 0)).astype(gx.dtype)

    @pl.when(i == 0)
    def _():
        acc[...] = jnp.zeros_like(acc)

    acc[...] += dot(gl, jnp.where(own, xo[...], xr[...]), 1, 0)

    @pl.when(i == last)
    def _():
        gsel[...] = dot(order[...].astype(F32), acc[...], 0, 0, HIGHEST)


def gate_back(core, order, selp, logits, gg, x_own, x_recv, gx):
    rows, width = x_own.shape
    total = 2 * rows
    steps = total // TILE
    half = steps // 2
    lo = lambda i: jnp.minimum(i, half - 1)
    hi = lambda i: jnp.maximum(i - half, 0)
    whole = lambda shape: VMEM(shape, lambda i: (0,) * len(shape))
    return pl.pallas_call(
        gate_back_kernel,
        grid=(steps,),
        out_shape=(
            jax.ShapeDtypeStruct((width, total), BF),
            jax.ShapeDtypeStruct((order.shape[1], width), F32),
        ),
        in_specs=[
            pl.BlockSpec(memory_space=pltpu.SMEM),
            whole(order.shape),
            whole(selp.shape),
            VMEM((GROWS, TILE), lambda i: (0, i)),
            VMEM((8, TPAD, TILE), lambda i: (0, 0, i)),
            VMEM((TILE, width), lambda i: (lo(i), 0)),
            VMEM((TILE, width), lambda i: (hi(i), 0)),
            VMEM((width, TILE), lambda i: (0, i)),
        ],
        out_specs=(
            VMEM((width, TILE), lambda i: (0, i)),
            whole((order.shape[1], width)),
        ),
        scratch_shapes=[pltpu.VMEM((GROWS, width), F32)],
        compiler_params=params(32),
        cost_estimate=pl.CostEstimate(
            flops=4 * total * width * GROWS, bytes_accessed=8 * MIB, transcendentals=0
        ),
    )(core, order, selp, logits, gg, x_own, x_recv, gx)


def final_kernel(perm, mo, mr, xo, xr, mixed, gf):
    for t in range(TASKS):
        s = (mo[t].astype(F32) + mr[t].astype(F32)).astype(BF)
        mixed[t] = dot(s, perm[...], 0, 0).astype(BF)
    s = (xo[...].astype(F32) + xr[...].astype(F32)).astype(BF)
    gf[...] = dot(s, perm[...], 0, 0).astype(BF)


def final(perm, mo, mr, xo, xr):
    width, rows = xo.shape
    whole = lambda shape: VMEM(shape, lambda i: (0,) * len(shape))
    tall = VMEM((width, TILE), lambda i: (0, i))
    deep = VMEM((TASKS, width, TILE), lambda i: (0, 0, i))
    return pl.pallas_call(
        final_kernel,
        grid=(rows // TILE,),
        out_shape=(
            jax.ShapeDtypeStruct((TASKS, rows, width), BF),
            jax.ShapeDtypeStruct((rows, width), BF),
        ),
        in_specs=[whole(perm.shape), deep, deep, tall, tall],
        out_specs=(
            VMEM((TASKS, TILE, width), lambda i: (0, i, 0)),
            VMEM((TILE, width), lambda i: (i, 0)),
        ),
        compiler_params=params(32),
        cost_estimate=pl.CostEstimate(
            flops=8 * rows * width * width, bytes_accessed=6 * MIB, transcendentals=0
        ),
    )(perm, mo, mr, xo, xr)


def adamw(weight, grad, first, second):
    first = BETA_ONE * first + (1.0 - BETA_ONE) * grad
    second = BETA_TWO * second + (1.0 - BETA_TWO) * grad * grad
    mhat = first / (1.0 - BETA_ONE**STEP)
    vhat = second / (1.0 - BETA_TWO**STEP)
    weight = weight - RATE * (mhat / (jnp.sqrt(vhat) + EPSILON) + DECAY * weight)
    return (first, second, weight)


def logit_order():
    order = np.zeros((GROWS, 64), np.float32)
    for t in range(TASKS):
        for k in range(SELECT):
            for b in range(BITS):
                order[(b * SELECT + k) * TPAD + t, (t * SELECT + k) * BITS + b] = 1.0
            at = (BITS * SELECT + k) * TPAD + t
            order[at, TASKS * SELECT * BITS + t * SELECT + k] = 1.0
    return order


def per_device(
    n_rows,
    n_hid,
    features,
    w_expand,
    w_reduce,
    biases,
    w_select,
    grad_mix,
    m_expand,
    v_expand,
    m_reduce,
    v_reduce,
    m_biases,
    v_biases,
    m_select,
    v_select,
):
    d_loc, experts, h_loc = w_expand.shape
    width = d_loc * n_rows
    mine_n = experts // 2
    chunk = mine_n // 2
    row = lax.axis_index("rows")
    hid_at = lax.axis_index("hid")
    core = hid_at % 2

    bits = n_rows.bit_length() - 1
    masks = [1, 2, 6] if n_rows == 8 else [1 << b for b in range(bits)]
    side = (0, 2)
    sibling = ((0, 1), (0, 1))
    dims = [side] + [(m, 0) for m in masks]
    if n_rows == 8:
        orders = [((0, 1, 2, 3), (2, 3, 0, 1)), ((1, 0, 3, 2), (3, 2, 1, 0))]
    else:
        orders = [(tuple(range(len(dims))),) * 2] * 2

    def swap(x, hops):
        pairs = []
        for r in range(n_rows):
            for h in range(n_hid):
                mr, mh = hops[h % 2]
                pairs.append((r * n_hid + h, (r ^ mr) * n_hid + (h ^ mh)))
        return lax.ppermute(x, ("rows", "hid"), pairs)

    def hops_of(c, step):
        return tuple(dims[orders[c][k][step]] for k in range(2))

    def table_of(c):
        if n_rows != 8:
            return jnp.arange(16, dtype=jnp.int32)
        both = []
        for k in range(2):
            order = orders[c][k]
            spots = []
            for q in range(8):
                for s in range(2):
                    on = [s] + [(q >> b) & 1 for b in range(3)]
                    spots.append(sum(on[d] << order.index(d) for d in range(4)))
            both.append(spots)
        both = np.asarray(both, np.int32)
        return jnp.where(core == 0, both[0], both[1])

    spot = np.arange(width)
    away = np.zeros(width, np.int32)
    for b, m in enumerate(masks):
        away ^= np.where((spot // d_loc >> b) & 1, m, 0).astype(np.int32)
    d_of = (row ^ jnp.asarray(away)) * d_loc + jnp.asarray(spot % d_loc, jnp.int32)
    perm32 = (d_of[:, None] == jnp.arange(width, dtype=jnp.int32)[None, :]).astype(F32)
    perm = perm32.astype(BF)
    q_of = (hid_at ^ jnp.asarray(spot // h_loc, jnp.int32)) * h_loc + jnp.asarray(
        spot % h_loc, jnp.int32
    )
    order = jnp.asarray(logit_order(), BF)
    core_arr = jnp.reshape(core, (1,)).astype(jnp.int32)

    def split_experts(x, axis):
        mine = lax.dynamic_slice_in_dim(x, core * mine_n, mine_n, axis)
        other = lax.dynamic_slice_in_dim(x, (1 - core) * mine_n, mine_n, axis)
        return mine, other

    w_pack = jnp.stack(
        [jnp.transpose(w_expand, (1, 0, 2)), jnp.transpose(w_reduce, (0, 2, 1))]
    ).astype(BF)
    w_mine, w_other = split_experts(w_pack, 1)
    w_recv = swap(w_other, sibling)
    chip = jnp.concatenate([w_mine, w_recv], axis=3)
    bufs = [chip[None, :, :chunk], chip[None, :, chunk:]]

    x_own = features
    g_own = jnp.transpose(grad_mix, (1, 0, 2))
    x_recv = swap(x_own, sibling)
    g_recv = swap(g_own, sibling)

    sel = w_select.astype(BF)
    for m in masks:
        sel = jnp.concatenate([sel, swap(sel, ((m, 0), (m, 0)))], axis=0)
    sel = jnp.pad(sel, ((0, 0), (0, order.shape[1] - sel.shape[1])))

    b_mine, b_other = split_experts(biases, 1)
    b_pair = jnp.stack([b_mine, swap(b_other, sibling)])
    b_all = jnp.stack([b_pair, swap(b_pair, (side, side))])
    b_all = jnp.transpose(b_all, (2, 3, 0, 1, 4)).reshape(2, mine_n, width)
    b0 = jnp.broadcast_to((0.5 * b_all[0])[:, :, None], (mine_n, width, 128))
    to_d = (d_of[:, None] == q_of[None, :]).astype(F32)
    b1 = dot(b_all[1], to_d, 1, 1, HIGHEST)
    b1 = jnp.broadcast_to(b1[:, :, None], (mine_n, width, 128))

    steps = len(dims)
    ends = []
    for step in range(steps):
        for c in range(2):
            got = swap(bufs[c], hops_of(c, step))
            if step + 1 < steps:
                bufs[c] = jnp.concatenate([bufs[c], got], axis=0)
            else:
                ends.append((bufs[c], got))

    xt, gt, cc, gates, logits, selp, gb1 = prep(
        core_arr, perm, order, sel, x_own, x_recv, g_own, g_recv
    )

    def canonical(lo, hi):
        if n_rows == 8:
            return lo, hi
        part = n_rows // 8
        w = jnp.concatenate([lo, hi], axis=0).reshape(8, part, 2, 2, chunk, d_loc, 2 * h_loc)
        w = jnp.transpose(w, (0, 2, 3, 4, 1, 5, 6)).reshape(16, 2, chunk, part * d_loc, 2 * h_loc)
        return w[:8], w[8:]

    def uncanonical(lo, hi):
        if n_rows == 8:
            return lo, hi
        part = n_rows // 8
        w = jnp.concatenate([lo, hi], axis=0).reshape(8, 2, 2, chunk, part, d_loc, 2 * h_loc)
        w = jnp.transpose(w, (0, 4, 1, 2, 3, 5, 6)).reshape(
            2 * n_rows, 2, chunk, d_loc, 2 * h_loc
        )
        return w[:n_rows], w[n_rows:]

    outs = []
    for c in range(2):
        lo, hi = canonical(*ends[c])
        outs.append(critical(table_of(c), lo, hi, xt, cc, b0, c * chunk))

    grads = [uncanonical(o[0], o[1]) for o in outs]
    for step in reversed(range(steps)):
        for c in range(2):
            lo, hi = grads[c]
            got = swap(hi, hops_of(c, step))
            half = lo.shape[0] // 2
            if step > 0:
                add = lambda a, b: (a.astype(F32) + b.astype(F32)).astype(BF)
                grads[c] = (add(lo[:half], got[:half]), add(lo[half:], got[half:]))
            else:
                grads[c] = lo[0].astype(F32) + got[0].astype(F32)
    g_chip = jnp.concatenate(grads, axis=1)
    g_recv_w = swap(g_chip[..., h_loc:].astype(BF), sibling).astype(F32)
    g_mine = g_chip[..., :h_loc]
    g_w = jnp.where(
        core == 0,
        jnp.concatenate([g_mine, g_recv_w], axis=1),
        jnp.concatenate([g_recv_w, g_mine], axis=1),
    )
    total_expand = jnp.transpose(g_w[0], (1, 0, 2))
    total_reduce = jnp.transpose(g_w[1], (0, 2, 1))

    cat = lambda k: jnp.concatenate([outs[0][k], outs[1][k]], axis=0)
    mix_own, mix_other, gx, gg = rest(cat(4), cat(2), cat(3), gt, gates, b1)
    gx, gsel = gate_back(core_arr, order, selp, logits, gg, x_own, x_recv, gx)
    rows_n = x_own.shape[0]
    mix_recv = swap(mix_other, sibling)
    gx_recv = swap(gx[:, rows_n:], sibling)
    mixed, grad_features = final(perm, mix_own, mix_recv, gx[:, :rows_n], gx_recv)
    mixed = jnp.transpose(mixed, (1, 0, 2))

    to_q = (q_of[:, None] == jnp.arange(width, dtype=jnp.int32)[None, :]).astype(F32)
    gb0_abs = dot(cat(5)[:, 0], to_q, 1, 0, HIGHEST)
    gb1_abs = dot(gb1[:, 0], perm32, 1, 0, HIGHEST)
    small = jnp.concatenate([gsel, gb0_abs, gb1_abs], axis=0)
    for d in dims:
        small = small + swap(small, (d, d))
    small_recv = swap(small, sibling)
    n_sel = gsel.shape[0]
    gsel = small[:n_sel] + small_recv[:n_sel]
    total_select = jnp.transpose(
        lax.dynamic_slice_in_dim(gsel[: w_select.shape[1]], row * d_loc, d_loc, 1)
    )
    both = [
        lax.dynamic_slice_in_dim(s[n_sel:].reshape(2, mine_n, width), hid_at * h_loc, h_loc, 2)
        for s in (small, small_recv)
    ]
    total_biases = jnp.where(
        core == 0, jnp.concatenate(both, axis=1), jnp.concatenate(both[::-1], axis=1)
    )

    mean_e, square_e, new_e = adamw(w_expand, total_expand, m_expand, v_expand)
    mean_r, square_r, new_r = adamw(w_reduce, total_reduce, m_reduce, v_reduce)
    mean_b, square_b, new_b = adamw(biases, total_biases, m_biases, v_biases)
    mean_s, square_s, new_s = adamw(w_select, total_select, m_select, v_select)
    return (
        mixed,
        grad_features,
        mean_e,
        square_e,
        new_e,
        mean_r,
        square_r,
        new_r,
        mean_b,
        square_b,
        new_b,
        mean_s,
        square_s,
        new_s,
    )


def solution(mesh):
    row_split = P(("rows", "hid"), None)
    task_split = P(("rows", "hid"), None, None)
    expand = P("rows", None, "hid")
    reduce = P(None, "hid", "rows")
    bias = P(None, None, "hid")
    select = P("rows", None)
    return jax.shard_map(
        functools.partial(per_device, mesh.shape["rows"], mesh.shape["hid"]),
        mesh=mesh,
        in_specs=(
            row_split, expand, reduce, bias, select, task_split,
            expand, expand, reduce, reduce, bias, bias, select, select,
        ),
        out_specs=(
            task_split, row_split,
            expand, expand, expand,
            reduce, reduce, reduce,
            bias, bias, bias,
            select, select, select,
        ),
        check_vma=False,
    )
```

```python
import functools

import jax
import jax.numpy as jnp
import numpy as np
from jax import lax
from jax.experimental import pallas as pl
from jax.experimental.pallas import tpu as pltpu
from jax.sharding import PartitionSpec as P

TASKS = 3
SELECT = 4
BITS = 4
STEP = 5
GAMMA = 2.0
RATE = 0.05
DECAY = 0.01
EPSILON = 1e-08
BETA_ONE = 0.5
BETA_TWO = 0.5

BF = jnp.bfloat16
F32 = jnp.float32
HIGHEST = lax.Precision.HIGHEST
TPAD = 8
GROUPS = BITS * SELECT + SELECT
GROWS = GROUPS * TPAD
ONES = 16
TILE = 512
WIDE = 1024
MIB = 1 << 20
FLOPS_MICRO = 1.2e10


def dot(a, b, ca, cb, precision=None):
    return lax.dot_general(
        a, b, (((ca,), (cb,)), ((), ())), preferred_element_type=F32, precision=precision
    )


def params(mib):
    return pltpu.CompilerParams(vmem_limit_bytes=mib * MIB)


def kernel_call(body, outs, scratch, mib, micros, smem, *args, after=()):
    in_vmem = pl.BlockSpec(memory_space=pltpu.VMEM)
    in_smem = pl.BlockSpec(memory_space=pltpu.SMEM)
    anywhere = pl.BlockSpec(memory_space=pl.ANY)
    n_in, n_after = len(args), len(after)

    def kernel(*refs):
        body(*refs[:n_in], *refs[n_in + n_after :])

    return pl.pallas_call(
        kernel,
        out_shape=tuple(jax.ShapeDtypeStruct(shape, kind) for shape, kind in outs),
        in_specs=[in_smem] * smem + [in_vmem] * (len(args) - smem) + [anywhere] * len(after),
        out_specs=(in_vmem,) * len(outs),
        scratch_shapes=[pltpu.VMEM(shape, kind) for shape, kind in scratch],
        compiler_params=params(mib),
        cost_estimate=pl.CostEstimate(
            flops=int(micros * FLOPS_MICRO), bytes_accessed=0, transcendentals=0
        ),
    )(*args, *after)


def gate_parts(z_of, a_of, high):
    smooth, clipped = {}, {}
    for k in range(SELECT):
        for b in range(BITS):
            v = jnp.clip(z_of(b, k), -0.5 * GAMMA, 0.5 * GAMMA)
            clipped[b, k] = v
            smooth[b, k] = v * (1.5 / GAMMA - 2.0 / GAMMA**3 * v * v) + 0.5
    a = [a_of(k) for k in range(SELECT)]
    top = functools.reduce(jnp.maximum, a)
    ex = [jnp.exp(v - top) for v in a]
    inv = 1.0 / functools.reduce(jnp.add, ex)
    alpha = [v * inv for v in ex]
    last = BITS - 1
    f_high = [
        high * smooth[last, k] + (1.0 - high) * (1.0 - smooth[last, k]) for k in range(SELECT)
    ]
    return alpha, smooth, clipped, f_high


def fac(smooth, b, k, bit):
    return smooth[b, k] if bit else 1.0 - smooth[b, k]


def part_of(i, tile):
    return pl.ds(pl.multiple_of(i * tile, tile), tile)


def prep_kernel(
    masks, at, order, sel, b_own, b_side, xo, xr, go, gr,
    xt, gt, cc_a, cc_b, gates, logits, selp, gb1, perm, to_q, b0, b1, mul,
):
    core, row, hid = at[0], at[1], at[2]
    high = core.astype(F32)
    rows, width = xo.shape
    tile = min(WIDE, rows)
    steps = rows // tile

    depth = width // (1 << len(masks))
    square = (width, width)
    up = lax.broadcasted_iota(jnp.int32, square, 0)
    across = lax.broadcasted_iota(jnp.int32, square, 1)

    def d_of(spot):
        block, out = spot // depth, row
        for b, m in enumerate(masks):
            out = out ^ (((block >> b) & 1) * m)
        return out * depth + spot % depth

    def q_of(spot):
        lanes = width // 4
        return (hid ^ (spot // lanes)) * lanes + spot % lanes

    one = lambda same: same.astype(F32)
    perm[...] = one(d_of(up) == across).astype(BF)
    to_q[...] = one(q_of(up) == across).astype(BF)
    pieces = []
    for ref in (b_own, b_side):
        for k in range(2):
            block = ref[k * 32 : (k + 1) * 32, :].astype(F32)
            block = block[:, :64] + block[:, 64:]
            pieces.append(block)
    take = lambda x, k: jnp.where(core == 0, x[16 * k : 16 * k + 8], x[16 * k + 8 : 16 * k + 16])
    bias = [jnp.concatenate([take(x, k) for x in pieces], axis=1) for k in range(2)]
    b0[...] = dot(one(up == across), 0.5 * bias[0], 1, 1, HIGHEST)
    b1[...] = dot(one(d_of(up) == q_of(across)), bias[1], 1, 1, HIGHEST)

    selp[...] = dot(order[...], sel[...], 1, 1).astype(BF)
    gb1[...] = jnp.zeros_like(gb1)
    xt[width : width + ONES, :] = jnp.ones((ONES, xt.shape[1]), BF)

    def step(i, x_ref, g_ref, first):
        here, out = part_of(i, tile), part_of(i + first, tile)
        x_t = dot(perm[...], x_ref[here, :], 1, 1).astype(BF)
        xt[0:width, out] = x_t
        lg = dot(selp[...], x_t, 1, 0)
        logits[:, out] = lg

        def z_of(b, k):
            at = (b * SELECT + k) * TPAD
            return lg[at : at + TPAD]

        def a_of(k):
            at = (BITS * SELECT + k) * TPAD
            return lg[at : at + TPAD]

        alpha, smooth, _, f_high = gate_parts(z_of, a_of, high)
        gate = [None] * 8
        for k in range(SELECT):
            base = alpha[k] * f_high[k]
            for e2 in range(2):
                w2 = base * fac(smooth, 2, k, e2)
                for e1 in range(2):
                    w1 = w2 * fac(smooth, 1, k, e1)
                    for e0 in range(2):
                        e = 4 * e2 + 2 * e1 + e0
                        w0 = w1 * fac(smooth, 0, k, e0)
                        gate[e] = w0 if gate[e] is None else gate[e] + w0
        g_t = []
        for t in range(TASKS):
            g = dot(perm[...], g_ref[t, here, :], 1, 1)
            gt[t, :, out] = g.astype(BF)
            g_t.append(g)
        ones = jnp.ones((8, tile), BF)
        for e in range(8):
            gates[e, :, out] = gate[e]
            c = gate[e][0:1] * g_t[0]
            for t in range(1, TASKS):
                c = c + gate[e][t : t + 1] * g_t[t]
            c = c.astype(BF)
            cc = cc_a if e < 4 else cc_b
            cc[e % 4, :, out] = c
            gb1[e] += dot(ones, c, 1, 1)

    @pl.loop(0, steps)
    def _(i):
        step(i, xo, go, 0)

    @pl.loop(0, steps)
    def _(i):
        step(i, xr, gr, steps)


def prep(masks, at, order, sel, b_own, b_side, x_own, x_recv, g_own, g_recv, after):
    rows, width = x_own.shape
    total = 2 * rows
    return kernel_call(
        functools.partial(prep_kernel, masks),
        (
            ((width + ONES, total), BF),
            ((TASKS, width, total), BF),
            ((4, width, total), BF),
            ((4, width, total), BF),
            ((8, TPAD, total), F32),
            ((GROWS, total), F32),
            ((GROWS, width), BF),
            ((8, 8, width), F32),
            ((width, width), BF),
            ((width, width), BF),
            ((width, 8), F32),
            ((width, 8), F32),
        ),
        (((8, 128), F32),),
        16,
        7.5,
        1,
        at, order, sel, b_own, b_side, x_own, x_recv, g_own, g_recv,
        after=after,
    )


def lanes_out(x):
    return jnp.concatenate([x[:, :128], x[:, 128:]], axis=0)


def lanes_in(x):
    rows = x.shape[0] // 2
    return jnp.concatenate([x[:rows], x[rows:]], axis=1)


def critical_kernel(second, spots, back, *refs):
    if second:
        (at_core, w_lo, w_hi, xt, cc, b0, gb0_a, gb1, to_q, perm,
         g_lo, g_hi, hid, gp, e_all, r_all, acc_e, acc_r) = refs
    else:
        (at_core, w_lo, w_hi, xt, cc, b0,
         g_lo, g_hi, hid, gp, e_all, r_all, gb0, acc_e, acc_r) = refs
    core = at_core[0]
    chunk, width, total = cc.shape
    lanes = w_lo.shape[1]
    hidden = 2 * lanes
    blocks = 8
    depth = width // blocks
    first = chunk if second else 0

    def each_block(table, lo, hi, visit):
        for q in range(blocks):
            for side in range(2):
                at = jnp.where(core == 0, table[0][2 * q + side], table[1][2 * q + side])
                rows = slice(q * depth, (q + 1) * depth)

                def cols(e, side=side):
                    return slice(e * hidden + side * lanes, e * hidden + (side + 1) * lanes)

                @pl.when(at < blocks)
                def _():
                    visit(lo, at, rows, cols)

                @pl.when(at >= blocks)
                def _():
                    visit(hi, at - blocks, rows, cols)

    def unpack(ref, at, rows, cols):
        for e in range(chunk):
            for which, out in ((0, e_all), (1, r_all)):
                spot = pl.multiple_of(((at * 2 + which) * chunk + e) * depth, depth)
                out[rows, cols(e)] = ref[pl.ds(spot, depth), :]

    each_block(spots, w_lo, w_hi, unpack)

    sums = []
    for e in range(chunk):
        cols = slice(e * hidden, (e + 1) * hidden)
        e_t = (e_all[:, cols] * 0.5).T
        r = (r_all[:, cols] * 0.5).T
        add = b0[:, first + e : first + e + 1]
        for i in range(total // TILE):
            part = slice(i * TILE, (i + 1) * TILE)
            u = dot(e_t, xt[0:width, part], 1, 0) + add
            t = jnp.tanh(u)
            plus = 1.0 + t
            h = u * plus
            hid[e, :, part] = h.astype(BF)
            gh = dot(r, cc[e, :, part], 1, 0)
            gp[e, :, part] = (gh * (plus + h * (1.0 - t))).astype(BF)
        acc_e[:, cols] = dot(xt[...], gp[e], 1, 1)
        acc_r[:, cols] = dot(cc[e], hid[e], 1, 1)
        sums.append(acc_e[width : width + 1, cols])

    def pack(ref, at, rows, cols):
        for e in range(chunk):
            ref[pl.ds(pl.multiple_of((at * 2 * chunk + e) * depth, depth), depth), :] = acc_e[
                rows, cols(e)
            ].astype(BF)
            ref[
                pl.ds(pl.multiple_of(((at * 2 + 1) * chunk + e) * depth, depth), depth), :
            ] = acc_r[rows, cols(e)].astype(BF)

    each_block(back, g_lo, g_hi, pack)
    sums = jnp.concatenate(sums, axis=0)
    if second:
        mine = jnp.concatenate([gb0_a[...], sums], axis=0).astype(BF)
        outer = jnp.concatenate([gb1[e, 0:1] for e in range(2 * chunk)], axis=0).astype(BF)
        both = jnp.concatenate(
            [dot(mine, to_q[...], 1, 0), dot(outer, perm[...], 1, 0)], axis=0
        ).astype(BF)
        g_hi[2 * chunk * width :, :] = lanes_out(both)
    else:
        gb0[...] = sums


def critical(spots, back, at, w_lo, w_hi, xt, cc, b0, after, more=None):
    chunk, width, total = cc.shape
    rows, lanes = w_lo.shape
    hidden = 2 * lanes
    outs = [
        ((rows, lanes), BF),
        ((rows + (8 * chunk if more else 0), lanes), BF),
        ((chunk, hidden, total), BF),
        ((chunk, hidden, total), BF),
        ((width, chunk * hidden), BF),
        ((width, chunk * hidden), BF),
    ]
    if not more:
        outs.append(((chunk, hidden), F32))
    return kernel_call(
        functools.partial(critical_kernel, more is not None, spots, back),
        tuple(outs),
        (((width + ONES, chunk * hidden), F32), ((width, chunk * hidden), F32)),
        16,
        7.6,
        1,
        at, w_lo, w_hi, xt, cc, b0, *(more or ()),
        after=after,
    )


def add_low(a, b):
    return (a.astype(F32) + b.astype(F32)).astype(BF)


def fold_kernel(n_small, *refs):
    lo, sent, got, *more, keep, msg = refs
    rows = lo.shape[0]
    half = rows // 2
    keep[...] = add_low(lo[0:half, :], got[0:half, :])
    msg[0:half, :] = add_low(lo[half:rows, :], got[half:rows, :])
    small = sent.shape[0] - rows
    if small:
        msg[half : half + small, :] = add_low(sent[rows:, :], got[rows:, :])
    if n_small:
        msg[half + small :, :] = add_low(more[0][...], more[1][...])


def fold(lo, sent, got, more=(), after=()):
    rows, lanes = lo.shape
    small = sent.shape[0] - rows + (more[0].shape[0] if more else 0)
    return kernel_call(
        functools.partial(fold_kernel, len(more)),
        (((rows // 2, lanes), BF), ((rows // 2 + small, lanes), BF)),
        (),
        8,
        0.3,
        0,
        lo, sent, got, *more,
        after=after,
    )


def append_kernel(msg, one, two, out):
    rows = msg.shape[0]
    out[0:rows, :] = msg[...]
    out[rows:, :] = add_low(one[...], two[...])


def append(msg, one, two, after):
    rows, lanes = msg.shape
    (out,) = kernel_call(
        append_kernel,
        (((rows + one.shape[0], lanes), BF),),
        (),
        8,
        0.3,
        0,
        msg, one, two,
        after=after,
    )
    return out


def last_fold_kernel(a_lo, a_got, b_lo, b_sent, b_got, own, msg):
    half = a_lo.shape[1] // 2
    rows = a_lo.shape[0] // 2
    for i, (lo, got) in enumerate(((a_lo, a_got), (b_lo, b_got))):
        e = lo[0:rows, :].astype(F32) + got[0:rows, :].astype(F32)
        r = lo[rows : 2 * rows, :].astype(F32) + got[rows : 2 * rows, :].astype(F32)
        here = slice(i * rows, (i + 1) * rows)
        own[here, :] = jnp.concatenate([e[:, :half], r[:, :half]], axis=1)
        msg[here, :] = jnp.concatenate([e[:, half:], r[:, half:]], axis=1).astype(BF)
    msg[2 * rows :, :] = add_low(b_sent[2 * rows :, :], b_got[2 * rows :, :])


def last_fold(a_lo, a_got, b_lo, b_sent, b_got):
    rows, lanes = a_lo.shape
    small = b_sent.shape[0] - rows
    return kernel_call(
        last_fold_kernel,
        (((rows, lanes), F32), ((rows + small, lanes), BF)),
        (),
        8,
        0.3,
        0,
        a_lo, a_got, b_lo, b_sent, b_got,
    )


def outer_kernel(start, *refs):
    if start:
        at_core, order, r_a, hid_a, r_b, hid_b, gt, logits, b1, x, acc_in, ys, gls, gsel, acc = refs
        acc[...] = acc_in[...]
    else:
        at_core, order, r_a, hid_a, r_b, hid_b, gt, logits, b1, x, ys, gls, acc = refs
        acc[...] = jnp.zeros_like(acc)
    high = at_core[0].astype(F32)
    sign = 2.0 * high - 1.0
    rows, width = x.shape
    chunk, hidden, _ = hid_a.shape
    tile = min(WIDE, rows)

    @pl.loop(0, rows // tile)
    def _(i):
        here, part = part_of(i, tile), part_of(i + start // tile, tile)
        gg = []
        wide = [gt[t, :, part].astype(F32) for t in range(TASKS)]
        for e in range(2 * chunk):
            r_all, hid = (r_a, hid_a) if e < chunk else (r_b, hid_b)
            at = e % chunk
            y = dot(r_all[:, at * hidden : (at + 1) * hidden], hid[at, :, part], 1, 0)
            y = y + b1[:, e : e + 1]
            ys[e, :, here] = y.astype(BF)
            sums = [jnp.sum(wide[t] * y, axis=0, keepdims=True) for t in range(TASKS)]
            gg.append(jnp.concatenate(sums + [jnp.zeros((TPAD - TASKS, tile), F32)], axis=0))
        gl = gate_back(
            lambda b, k: logits[(b * SELECT + k) * TPAD : (b * SELECT + k + 1) * TPAD, part],
            lambda k: logits[
                (BITS * SELECT + k) * TPAD : (BITS * SELECT + k + 1) * TPAD, part
            ],
            gg, high, sign,
        ).astype(BF)
        gls[:, here] = gl
        acc[...] += dot(gl, x[here, :], 1, 0)

    if start:
        gsel[...] = lanes_out(dot(order[:, 0:64], acc[...].astype(BF), 0, 0)).astype(BF)


def outer(start, at, order, first, second, gt, logits, b1, x, acc=None, after=()):
    rows, width = x.shape
    (r_a, hid_a), (r_b, hid_b) = first, second
    chunk, hidden, _ = hid_a.shape
    outs = [((2 * chunk, width, rows), BF), ((GROWS, rows), BF)]
    scratch = ()
    if start:
        outs.append(((order.shape[1], 128), BF))
        scratch = (((GROWS, width), F32),)
    else:
        outs.append(((GROWS, width), F32))
    return kernel_call(
        functools.partial(outer_kernel, start),
        tuple(outs),
        scratch,
        16,
        4.3,
        1,
        at, order, r_a, hid_a, r_b, hid_b, gt, logits, b1, x, *((acc,) if start else ()),
        after=after,
    )


def mix_kernel(start, e_a, gp_a, e_b, gp_b, selp, ys, gls, gates, out):
    count, width, rows = ys.shape
    chunk, hidden, _ = gp_a.shape
    tile, depth = 256, 32

    @pl.loop(0, rows // tile)
    def _(i):
        here, part = part_of(i, tile), part_of(i + start // tile, tile)
        v = dot(e_a[...], gp_a[:, :, part].reshape(chunk * hidden, tile), 1, 0)
        v = v + dot(e_b[...], gp_b[:, :, part].reshape(chunk * hidden, tile), 1, 0)
        out[TASKS, :, here] = (v + dot(selp[...], gls[:, here], 0, 0)).astype(BF)
        for d in range(width // depth):
            block = slice(d * depth, (d + 1) * depth)
            sums = [None] * TASKS
            for e in range(count):
                y = ys[e, block, here].astype(F32)
                for t in range(TASKS):
                    m = gates[e, t : t + 1, part] * y
                    sums[t] = m if e == 0 else sums[t] + m
            for t in range(TASKS):
                out[t, block, here] = sums[t].astype(BF)


def mix(start, first, second, selp, ys, gls, gates, after):
    (e_a, gp_a), (e_b, gp_b) = first, second
    count, width, rows = ys.shape
    chunk, hidden, _ = gp_a.shape
    (out,) = kernel_call(
        functools.partial(mix_kernel, start),
        (((TASKS + 1, width, rows), BF),),
        (),
        16,
        4.0,
        0,
        e_a, gp_a, e_b, gp_b, selp, ys, gls, gates,
        after=after,
    )
    return out


def gate_back(z_of, a_of, gg, high, sign):
    alpha, smooth, clipped, f_high = gate_parts(z_of, a_of, high)
    out = [None] * GROUPS
    d_alpha = []
    for k in range(SELECT):
        f = [[fac(smooth, b, k, bit) for bit in range(2)] for b in range(BITS - 1)]
        low, dif = {}, {}
        for e2 in range(2):
            for e1 in range(2):
                p, q = gg[4 * e2 + 2 * e1], gg[4 * e2 + 2 * e1 + 1]
                low[e2, e1] = f[0][0] * p + f[0][1] * q
                dif[e2, e1] = q - p
        mid = [f[1][0] * low[e2, 0] + f[1][1] * low[e2, 1] for e2 in range(2)]
        mid1 = [low[e2, 1] - low[e2, 0] for e2 in range(2)]
        mid0 = [f[1][0] * dif[e2, 0] + f[1][1] * dif[e2, 1] for e2 in range(2)]
        t0 = f[2][0] * mid[0] + f[2][1] * mid[1]
        d2 = mid[1] - mid[0]
        d1 = f[2][0] * mid1[0] + f[2][1] * mid1[1]
        d0 = f[2][0] * mid0[0] + f[2][1] * mid0[1]
        d_alpha.append(f_high[k] * t0)
        scale = alpha[k] * f_high[k]
        for b, d in enumerate((scale * d0, scale * d1, scale * d2, alpha[k] * sign * t0)):
            v = clipped[b, k]
            out[b * SELECT + k] = d * (1.5 / GAMMA - 6.0 / GAMMA**3 * v * v)
    total = functools.reduce(jnp.add, [a * d for a, d in zip(alpha, d_alpha)])
    for k in range(SELECT):
        out[BITS * SELECT + k] = alpha[k] * (d_alpha[k] - total)
    return jnp.concatenate(out, axis=0)


def final_kernel(perm, own, recv, mixed, gf):
    for t in range(TASKS + 1):
        s = (own[t].astype(F32) + recv[t].astype(F32)).astype(BF)
        rows = dot(s, perm[...], 0, 0).astype(BF)
        if t < TASKS:
            mixed[t] = rows
        else:
            gf[...] = rows


def final(perm, own, recv, after):
    _, width, rows = own.shape
    return kernel_call(
        final_kernel,
        (((TASKS, rows, width), BF), ((rows, width), BF)),
        (),
        16,
        2.7,
        0,
        perm, own, recv,
        after=after,
    )


def adamw(weight, grad, first, second):
    first = BETA_ONE * first + (1.0 - BETA_ONE) * grad
    second = BETA_TWO * second + (1.0 - BETA_TWO) * grad * grad
    mhat = first / (1.0 - BETA_ONE**STEP)
    vhat = second / (1.0 - BETA_TWO**STEP)
    weight = weight - RATE * (mhat / (jnp.sqrt(vhat) + EPSILON) + DECAY * weight)
    return (first, second, weight)


def pack_kernel(with_w, core, w_e, w_r, w_b, w_s, sel, bias, *refs):
    first = core[0] == 0
    sel[...] = jnp.zeros_like(sel)
    sel[:, 0 : w_s.shape[1]] = w_s[...].astype(BF)
    experts, lanes = w_b.shape[1:]
    for k in range(2):
        high = w_b[k].astype(BF)
        low = (w_b[k] - high.astype(F32)).astype(BF)
        bias[k * experts : (k + 1) * experts, :] = jnp.concatenate(
            [high.astype(F32), low.astype(F32)], axis=1
        ).astype(BF)
    if with_w:
        mine, other = refs
        count = experts // 2
        for e in range(count):
            for which in range(2):
                lo, hi = (
                    (w_r[e], w_r[e + count]) if which else (w_e[:, e, :], w_e[:, e + count, :])
                )
                mine[which, e] = jnp.where(first, lo, hi).astype(BF)
                other[which, e] = jnp.where(first, hi, lo).astype(BF)


def pack(core, w_e, w_r, w_b, w_s, with_w):
    experts, depth, lanes = w_r.shape
    half = (2, experts // 2, depth, lanes)
    outs = [((depth, 2 * lanes), BF), ((2 * experts, 2 * lanes), BF)]
    if with_w:
        outs += [(half, BF), (half, BF)]
    block = lambda shape: pl.BlockSpec(shape, lambda i: (0,) * len(shape))
    return pl.pallas_call(
        functools.partial(pack_kernel, with_w),
        grid=(1,),
        out_shape=tuple(jax.ShapeDtypeStruct(shape, kind) for shape, kind in outs),
        in_specs=[pl.BlockSpec(memory_space=pltpu.SMEM)]
        + [block(x.shape) for x in (w_e, w_r, w_b, w_s)],
        out_specs=tuple(block(shape) for shape, _ in outs),
        compiler_params=params(8),
    )(core, w_e, w_r, w_b, w_s)


def join_kernel(plan, n_in, *refs):
    ins, outs = refs[:n_in], refs[n_in:]
    for out, pieces in zip(outs, plan):
        to = 0
        for k, start, rows in pieces:
            out[to : to + rows, :] = ins[k][start : start + rows, :]
            to += rows


def join(plan, *ins, after=()):
    lanes = ins[0].shape[1]
    return kernel_call(
        functools.partial(join_kernel, plan, len(ins)),
        tuple(((sum(p[2] for p in pieces), lanes), BF) for pieces in plan),
        (),
        8,
        0.3,
        0,
        *ins,
        after=after,
    )


def chip_kernel(mine, recv, sel, msg):
    _, count, depth, lanes = mine.shape
    for which in range(2):
        for e in range(count):
            to = (which * count + e) * depth
            msg[to : to + depth, :] = jnp.concatenate([mine[which, e], recv[which, e]], axis=1)
    msg[2 * count * depth :, :] = sel[...]


def chip_message(mine, recv, sel):
    _, count, depth, lanes = mine.shape
    rows = 2 * count * depth
    (msg,) = kernel_call(
        chip_kernel, (((rows + sel.shape[0], 2 * lanes), BF),), (), 8, 0.3, 0,
        mine, recv, sel,
    )
    return msg


def update_kernel(
    at, own, sent, got, w_e, m_e, v_e, w_r, m_r, v_r, w_b, m_b, v_b, w_s, m_s, v_s, *refs
):
    outs, (g_e,) = refs[:-1], refs[-1:]
    core, row, hid = at[0], at[1], at[2]
    first = core == 0
    experts, depth, lanes = w_r.shape
    count = experts // 2
    n_own = own.shape[0]
    theirs = got[0:n_own, :].astype(F32)
    halves = (jnp.where(first, own[...], theirs), jnp.where(first, theirs, own[...]))

    def store(k, new):
        for ref, value in zip(outs[3 * k : 3 * k + 3], new):
            ref[...] = value

    parts = []
    for half in halves:
        for e in range(count):
            rows = half[e * depth : (e + 1) * depth]
            g_e[:, len(parts), :] = rows[:, :lanes]
            parts.append(rows[:, lanes:])
    store(0, adamw(w_e[...], g_e[...], m_e[...], v_e[...]))
    store(1, adamw(w_r[...], jnp.stack(parts), m_r[...], v_r[...]))

    n_bias = 8 * count // 2
    small, small_got = sent[n_own:, :], got[n_own:, :]
    bias = [lanes_in(x[0:n_bias]) for x in (small, small_got)]
    width = bias[0].shape[1]
    spot = lax.broadcasted_iota(jnp.int32, (width, lanes), 0)
    lane = lax.broadcasted_iota(jnp.int32, (width, lanes), 1)
    pick = (spot == hid * lanes + lane).astype(F32).astype(BF)
    mine, other = [dot(x, pick, 1, 0) for x in bias]
    lo, hi = jnp.where(first, mine, other), jnp.where(first, other, mine)
    g_b = jnp.stack(
        [jnp.concatenate([x[k * count : (k + 1) * count] for x in (lo, hi)], axis=0) for k in range(2)]
    )
    store(2, adamw(w_b[...], g_b, m_b[...], v_b[...]))

    g_s = lanes_in(add_low(small[n_bias:], small_got[n_bias:]))
    spot = lax.broadcasted_iota(jnp.int32, (depth, width), 0)
    lane = lax.broadcasted_iota(jnp.int32, (depth, width), 1)
    pick = (lane == row * depth + spot).astype(F32).astype(BF)
    g_s = dot(pick, g_s, 1, 1)[:, : w_s.shape[1]]
    store(3, adamw(w_s[...], g_s, m_s[...], v_s[...]))


def update(at, own, sent, got, *params):
    outs = []
    for k in range(4):
        outs += [(params[3 * k].shape, F32)] * 3
    return kernel_call(
        update_kernel,
        tuple(outs),
        ((params[0].shape, F32),),
        16,
        2.4,
        1,
        at, own, sent, got, *params,
    )


def logit_order():
    order = np.zeros((GROWS, 128), np.float32)
    for t in range(TASKS):
        for k in range(SELECT):
            for b in range(BITS):
                order[(b * SELECT + k) * TPAD + t, (t * SELECT + k) * BITS + b] = 1.0
            at = (BITS * SELECT + k) * TPAD + t
            order[at, TASKS * SELECT * BITS + t * SELECT + k] = 1.0
    return order


def per_device(
    n_rows,
    n_hid,
    features,
    w_expand,
    w_reduce,
    biases,
    w_select,
    grad_mix,
    m_expand,
    v_expand,
    m_reduce,
    v_reduce,
    m_biases,
    v_biases,
    m_select,
    v_select,
):
    d_loc, experts, h_loc = w_expand.shape
    width = d_loc * n_rows
    mine_n = experts // 2
    chunk = mine_n // 2
    row = lax.axis_index("rows")
    hid_at = lax.axis_index("hid")
    core = hid_at % 2

    bits = n_rows.bit_length() - 1
    masks = [1 << b for b in range(bits)]
    side = (0, 2)
    sibling = ((0, 1), (0, 1))
    dims = [side] + [(m, 0) for m in masks]
    if n_rows == 8:
        way = ((3, 2, 0, 1), (1, 3, 2, 0))
    else:
        way = (tuple(range(len(dims))),) * 2

    def swap(x, hops):
        pairs = []
        for r in range(n_rows):
            for h in range(n_hid):
                mr, mh = hops[h % 2]
                pairs.append((r * n_hid + h, (r ^ mr) * n_hid + (h ^ mh)))
        return lax.ppermute(x, ("rows", "hid"), pairs)

    def hops(step):
        return tuple(dims[way[k][step]] for k in range(2))

    def table_of(pair):
        if n_rows != 8:
            return (tuple(range(16)),) * 2
        both = []
        for order in pair:
            spots = []
            for q in range(8):
                for s in range(2):
                    on = [s] + [(q >> b) & 1 for b in range(3)]
                    spots.append(sum(on[d] << order.index(d) for d in range(4)))
            both.append(tuple(spots))
        return tuple(both)

    order = jnp.asarray(logit_order(), BF)
    at = jnp.stack([core, row, hid_at]).astype(jnp.int32)

    def split_experts(x, axis):
        mine = lax.dynamic_slice_in_dim(x, core * mine_n, mine_n, axis)
        other = lax.dynamic_slice_in_dim(x, (1 - core) * mine_n, mine_n, axis)
        return mine, other

    def tie(x, *after):
        return lax.optimization_barrier((x, after))[0]

    part = n_rows // 8

    def canonical(lo, hi):
        w = jnp.concatenate([lo, hi], axis=0).reshape(8, part, 2, 2, chunk, d_loc, 2 * h_loc)
        w = jnp.transpose(w, (0, 2, 3, 4, 1, 5, 6)).reshape(2, -1, 2 * h_loc)
        return w[0], w[1]

    def uncanonical(lo, hi):
        if n_rows == 8:
            return lo, hi
        w = jnp.concatenate([lo, hi], axis=0).reshape(8, 2, 2, chunk, part, d_loc, 2 * h_loc)
        w = jnp.transpose(w, (0, 4, 1, 2, 3, 5, 6)).reshape(2, -1, 2 * h_loc)
        return w[0], w[1]

    w_r_view = jnp.transpose(w_reduce, (0, 2, 1))
    packed = pack(at, w_expand, w_r_view, biases, w_select, d_loc % 16 == 0)
    sel, b_own = packed[:2]
    if d_loc % 16 == 0:
        w_mine, w_other = packed[2:]
    else:
        w_mine, w_other = split_experts(
            jnp.stack([jnp.transpose(w_expand, (1, 0, 2)), w_r_view]).astype(BF), 1
        )
    w_recv = swap(w_other, sibling)
    b_own = jnp.concatenate([b_own, swap(b_own, sibling)], axis=0)
    x_own = features
    g_own = jnp.transpose(grad_mix, (1, 0, 2))
    x_recv = swap(x_own, sibling)
    g_recv = swap(g_own, sibling)

    steps = len(dims)
    ride = n_rows == 8
    if ride:
        whole = 2 * mine_n * d_loc
        msg = chip_message(w_mine, w_recv, sel)
        got = swap(msg, hops(0))
        (msg,) = join(
            (((0, 0, whole), (1, 0, whole), (0, whole, d_loc), (1, whole, d_loc)),), msg, got
        )
        got = swap(msg, hops(1))
        half = whole // 2
        group = chunk * d_loc
        pieces = [
            tuple((k, (2 * j + c) * group, group) for k in range(2) for j in range(4))
            for c in range(2)
        ]
        tail = tuple((k, 2 * whole, 2 * d_loc) for k in range(2)) + ((2, 0, 4 * experts),)
        a_msg, b_msg = join((pieces[0] + tail, pieces[1]), msg, got, b_own)
        a_got = swap(a_msg, hops(2))
        n = 8 * group
        a_lo, riders = join(
            (
                ((0, 0, n), (1, 0, n)),
                ((0, n, 4 * d_loc), (1, n, 4 * d_loc), (1, n + 4 * d_loc, 4 * experts)),
            ),
            a_msg, a_got,
        )
        a_hi = swap(a_lo, hops(3))
        turned = swap(riders, sibling)
        b_got = swap(tie(b_msg, a_lo), hops(2))
        last = a_lo
        sel = jnp.where(core == 1, riders[:width], turned[:width])
        sel = jnp.transpose(sel.reshape(2, 2, 2, d_loc, 2 * h_loc), (1, 0, 2, 3, 4))
        sel = sel.reshape(width, 2 * h_loc)
        n_b = 2 * experts
        turned = jnp.concatenate([turned[width + n_b :], turned[width : width + n_b]], axis=0)
        b_side = jnp.where(core == 0, riders[width:], turned)
    else:
        chip = jnp.concatenate([w_mine, w_recv], axis=3)
        bufs = [chip[None, :, :chunk], chip[None, :, chunk:]]
        for step in range(steps):
            gots = [swap(buf, hops(step)) for buf in bufs]
            if step + 1 < steps:
                bufs = [jnp.concatenate(pair, axis=0) for pair in zip(bufs, gots)]
        for m in masks:
            sel = jnp.concatenate([sel, swap(sel, ((m, 0), (m, 0)))], axis=0)
        b_side = swap(b_own, (side, side))
        (a_lo, a_hi), (b_lo, b_hi) = [canonical(*pair) for pair in zip(bufs, gots)]
        last = a_lo

    xt, gt, cc_a, cc_b, gates, logits, selp, gb1, perm, to_q, b0, b1 = prep(
        masks, at, order, sel, b_own, b_side, x_own, x_recv, g_own, g_recv, (last,)
    )

    spots = table_of(way)
    if ride:
        (b_lo,) = join((((0, 0, n), (1, 0, n)),), b_msg, b_got, after=(b0,))
        b_hi = swap(b_lo, hops(3))
    first = critical(spots, spots, at, a_lo, a_hi, xt, cc_a, b0, (b_lo,))
    a_lo, a_msg = uncanonical(first[0], first[1])
    a_got = swap(a_msg, hops(steps - 1))
    second = critical(
        spots, spots, at, b_lo, b_hi, xt, cc_b, b0, (first[0],), (first[6], gb1, to_q, perm)
    )
    b_lo, b_msg = second[:2]
    if not ride:
        n = b_lo.shape[0]
        b_lo, b_msg = uncanonical(b_lo, b_msg[:n])
        b_msg = jnp.concatenate([b_msg, second[1][n:]], axis=0)
    b_got = swap(b_msg, hops(steps - 1))
    inner = ((first[5], first[2]), (second[5], second[2]))
    ends = ((first[4], first[3]), (second[4], second[3]))
    n_own = x_own.shape[0]
    ys_own, gl_own, acc = outer(0, at, order, *inner, gt, logits, b1, x_own)

    def next_a(step, lo, sent, got, after=()):
        keep, msg = fold(lo, sent, got, (), after)
        return keep, msg, swap(msg, hops(step))

    a_lo, a_msg, a_got = next_a(steps - 2, a_lo, a_msg, a_got, (b_lo,))
    ys_other, gl_other, gsel = outer(
        n_own, at, order, *inner, gt, logits, b1, x_recv, acc, (a_lo,)
    )
    gsel_got = swap(gsel, hops(steps - 1))
    b_lo, b_msg = fold(b_lo, b_msg, b_got)
    a_lo, a_msg, a_got = next_a(steps - 3, a_lo, a_msg, a_got)
    mix_other = mix(n_own, *ends, selp, ys_other, gl_other, gates, (a_lo, b_lo))
    mix_recv = swap(mix_other, sibling)
    b_msg = append(b_msg, gsel, gsel_got, (mix_other,))
    b_got = swap(b_msg, hops(steps - 2))
    mix_own = mix(0, *ends, selp, ys_own, gl_own, gates, (b_msg,))
    for step in reversed(range(steps - 3)):
        a_lo, a_msg, a_got = next_a(step, a_lo, a_msg, a_got)
    mixed, grad_features = final(perm, mix_own, mix_recv, (a_lo,))
    for step in reversed(range(steps - 2)):
        b_lo, b_msg = fold(b_lo, b_msg, b_got, (), (grad_features,))
        b_got = swap(b_msg, hops(step))
    own, msg = last_fold(a_lo, a_got, b_lo, b_msg, b_got)
    got = swap(msg, sibling)
    mixed = jnp.transpose(mixed, (1, 0, 2))

    flip = lambda x: jnp.transpose(x, (0, 2, 1))
    new = list(
        update(
            at, own, msg, got,
            w_expand, m_expand, v_expand,
            w_r_view, flip(m_reduce), flip(v_reduce),
            biases, m_biases, v_biases,
            w_select, m_select, v_select,
        )
    )
    new[3:6] = [flip(x) for x in new[3:6]]
    return (mixed, grad_features, *new)


def solution(mesh):
    row_split = P(("rows", "hid"), None)
    task_split = P(("rows", "hid"), None, None)
    expand = P("rows", None, "hid")
    reduce = P(None, "hid", "rows")
    bias = P(None, None, "hid")
    select = P("rows", None)
    return jax.shard_map(
        functools.partial(per_device, mesh.shape["rows"], mesh.shape["hid"]),
        mesh=mesh,
        in_specs=(
            row_split, expand, reduce, bias, select, task_split,
            expand, expand, reduce, reduce, bias, bias, select, select,
        ),
        out_specs=(
            task_split, row_split,
            expand, expand, expand,
            reduce, reduce, reduce,
            bias, bias, bias,
            select, select, select,
        ),
        check_vma=False,
    )
```

```python
import functools

import jax
import jax.numpy as jnp
import numpy as np
from jax import lax
from jax.experimental import pallas as pl
from jax.experimental.pallas import tpu as pltpu
from jax.sharding import PartitionSpec as P

TASKS = 3
SELECT = 4
BITS = 4
STEP = 5
GAMMA = 2.0
RATE = 0.05
DECAY = 0.01
EPSILON = 1e-08
BETA_ONE = 0.5
BETA_TWO = 0.5

BF = jnp.bfloat16
F32 = jnp.float32
HIGHEST = lax.Precision.HIGHEST
TPAD = 8
GROUPS = BITS * SELECT + SELECT
GROWS = GROUPS * TPAD
ONES = 16
TILE = 256
WIDE = 1024
MIB = 1 << 20
FLOPS_MICRO = 1.2e10


def dot(a, b, ca, cb, precision=None):
    return lax.dot_general(
        a, b, (((ca,), (cb,)), ((), ())), preferred_element_type=F32, precision=precision
    )


def params(mib):
    return pltpu.CompilerParams(vmem_limit_bytes=mib * MIB)


def kernel_call(body, outs, scratch, mib, micros, smem, *args, after=()):
    in_vmem = pl.BlockSpec(memory_space=pltpu.VMEM)
    in_smem = pl.BlockSpec(memory_space=pltpu.SMEM)
    anywhere = pl.BlockSpec(memory_space=pl.ANY)
    n_in, n_after = len(args), len(after)

    def kernel(*refs):
        body(*refs[:n_in], *refs[n_in + n_after :])

    return pl.pallas_call(
        kernel,
        out_shape=tuple(jax.ShapeDtypeStruct(shape, kind) for shape, kind in outs),
        in_specs=[in_smem] * smem + [in_vmem] * (len(args) - smem) + [anywhere] * len(after),
        out_specs=(in_vmem,) * len(outs),
        scratch_shapes=[pltpu.VMEM(shape, kind) for shape, kind in scratch],
        compiler_params=params(mib),
        cost_estimate=pl.CostEstimate(
            flops=int(micros * FLOPS_MICRO), bytes_accessed=0, transcendentals=0
        ),
    )(*args, *after)


def gate_parts(z_of, a_of, high):
    smooth, clipped = {}, {}
    for k in range(SELECT):
        for b in range(BITS):
            v = jnp.clip(z_of(b, k), -0.5 * GAMMA, 0.5 * GAMMA)
            clipped[b, k] = v
            smooth[b, k] = v * (1.5 / GAMMA - 2.0 / GAMMA**3 * v * v) + 0.5
    a = [a_of(k) for k in range(SELECT)]
    top = functools.reduce(jnp.maximum, a)
    ex = [jnp.exp(v - top) for v in a]
    inv = 1.0 / functools.reduce(jnp.add, ex)
    alpha = [v * inv for v in ex]
    last = BITS - 1
    f_high = [
        high * smooth[last, k] + (1.0 - high) * (1.0 - smooth[last, k]) for k in range(SELECT)
    ]
    return alpha, smooth, clipped, f_high


def fac(smooth, b, k, bit):
    return smooth[b, k] if bit else 1.0 - smooth[b, k]


def part_of(i, tile):
    return pl.ds(pl.multiple_of(i * tile, tile), tile)


def places(masks, at, width):
    row, hid = at[1], at[2]
    depth = width // (1 << len(masks))

    def d_of(spot):
        block, out = spot // depth, row
        for b, m in enumerate(masks):
            out = out ^ (((block >> b) & 1) * m)
        return out * depth + spot % depth

    def q_of(spot):
        lanes = width // 4
        return (hid ^ (spot // lanes)) * lanes + spot % lanes

    return d_of, q_of


def turn_kernel(masks, at, xo, xr, go, gr, xt, gt, perm, to_q):
    rows, width = xo.shape
    d_of, q_of = places(masks, at, width)
    up = lax.broadcasted_iota(jnp.int32, (width, width), 0)
    across = lax.broadcasted_iota(jnp.int32, (width, width), 1)
    perm[...] = (d_of(up) == across).astype(F32).astype(BF)
    to_q[...] = (q_of(up) == across).astype(F32).astype(BF)
    xt[width : width + ONES, :] = jnp.ones((ONES, xt.shape[1]), BF)
    tile = min(WIDE, rows)
    for x, g, start in ((xo, go, 0), (xr, gr, rows)):
        for i in range(rows // tile):
            here = slice(i * tile, (i + 1) * tile)
            out = slice(start + i * tile, start + (i + 1) * tile)
            xt[0:width, out] = dot(perm[...], x[here, :], 1, 1).astype(BF)
            for t in range(TASKS):
                gt[t, :, out] = dot(perm[...], g[t, here, :], 1, 1).astype(BF)


def turn(masks, at, x_own, x_recv, g_own, g_recv, after):
    rows, width = x_own.shape
    total = 2 * rows
    return kernel_call(
        functools.partial(turn_kernel, masks),
        (
            ((width + ONES, total), BF),
            ((TASKS, width, total), BF),
            ((width, width), BF),
            ((width, width), BF),
        ),
        (),
        12,
        3.5,
        1,
        at, x_own, x_recv, g_own, g_recv,
        after=after,
    )


def prep_kernel(
    masks, ride, at, order, riders, turned, b_own, xt, gt,
    cc_a, cc_b, gates, logits, selp, gb1, b0, b1, sel,
):
    core = at[0]
    high = core.astype(F32)
    _, width, total = gt.shape
    tile = min(WIDE, total)
    d_of, q_of = places(masks, at, width)
    up = lax.broadcasted_iota(jnp.int32, (width, width), 0)
    across = lax.broadcasted_iota(jnp.int32, (width, width), 1)
    one = lambda same: same.astype(F32)
    n_b = b_own.shape[0] // 2
    if ride:
        depth = width // 8
        for q in range(8):
            spot = (q & 1) + 2 * (q >> 2) + 4 * (q >> 1 & 1)
            rows = slice(spot * depth, (spot + 1) * depth)
            sel[q * depth : (q + 1) * depth, :] = jnp.where(core == 1, riders[rows, :], turned[rows, :])
        side = [
            jnp.where(
                core == 0,
                riders[width + k * n_b : width + (k + 1) * n_b, :],
                turned[width + (1 - k) * n_b : width + (2 - k) * n_b, :],
            )
            for k in range(2)
        ]
    else:
        sel[...] = riders[0:width, :]
        side = [riders[width + k * n_b : width + (k + 1) * n_b, :] for k in range(2)]
    pieces = []
    for block in [b_own[k * n_b : (k + 1) * n_b, :] for k in range(2)] + side:
        block = block.astype(F32)
        pieces.append(block[:, : width // 4] + block[:, width // 4 :])
    take = lambda x, k: jnp.where(core == 0, x[16 * k : 16 * k + 8], x[16 * k + 8 : 16 * k + 16])
    bias = [jnp.concatenate([take(x, k) for x in pieces], axis=1) for k in range(2)]
    b0[...] = dot(one(up == across), 0.5 * bias[0], 1, 1, HIGHEST)
    b1[...] = dot(one(d_of(up) == q_of(across)), bias[1], 1, 1, HIGHEST)
    selp[...] = dot(order[...], sel[...], 1, 1).astype(BF)
    gb1[...] = jnp.zeros_like(gb1)

    @pl.loop(0, total // tile)
    def _(i):
        part = part_of(i, tile)
        lg = dot(selp[...], xt[0:width, part], 1, 0)
        logits[:, part] = lg

        def z_of(b, k):
            at = (b * SELECT + k) * TPAD
            return lg[at : at + TPAD]

        def a_of(k):
            at = (BITS * SELECT + k) * TPAD
            return lg[at : at + TPAD]

        alpha, smooth, _, f_high = gate_parts(z_of, a_of, high)
        gate = [None] * 8
        for k in range(SELECT):
            base = alpha[k] * f_high[k]
            for e2 in range(2):
                w2 = base * fac(smooth, 2, k, e2)
                for e1 in range(2):
                    w1 = w2 * fac(smooth, 1, k, e1)
                    for e0 in range(2):
                        e = 4 * e2 + 2 * e1 + e0
                        w0 = w1 * fac(smooth, 0, k, e0)
                        gate[e] = w0 if gate[e] is None else gate[e] + w0
        for e in range(8):
            gates[e, :, part] = gate[e]
        ones = jnp.ones((8, tile), BF)
        g_t = [gt[t, :, part].astype(F32) for t in range(TASKS)]
        for e in range(8):
            c = gate[e][0:1] * g_t[0]
            for t in range(1, TASKS):
                c = c + gate[e][t : t + 1] * g_t[t]
            c = c.astype(BF)
            cc = cc_a if e < 4 else cc_b
            cc[e % 4, :, part] = c
            gb1[e] += dot(ones, c, 1, 1)


def prep(masks, ride, at, order, riders, turned, b_own, xt, gt):
    _, width, total = gt.shape
    return kernel_call(
        functools.partial(prep_kernel, masks, ride),
        (
            ((4, width, total), BF),
            ((4, width, total), BF),
            ((8, TPAD, total), F32),
            ((GROWS, total), F32),
            ((GROWS, width), BF),
            ((8, 8, width), F32),
            ((width, 8), F32),
            ((width, 8), F32),
        ),
        (((width, 128), BF),),
        14,
        5.0,
        1,
        at, order, riders, turned, b_own, xt, gt,
    )


def lanes_out(x):
    return jnp.concatenate([x[:, :128], x[:, 128:]], axis=0)


def lanes_in(x):
    rows = x.shape[0] // 2
    return jnp.concatenate([x[:rows], x[rows:]], axis=1)


def critical_kernel(second, spots, back, *refs):
    if second:
        (at_core, w_lo, w_hi, xt, cc, b0, gb0_a, gb1, to_q, perm,
         g_lo, g_hi, hid, gp, e_all, r_all, acc_e, acc_r) = refs
    else:
        (at_core, w_lo, w_hi, xt, cc, b0,
         g_lo, g_hi, hid, gp, e_all, r_all, gb0, acc_e, acc_r) = refs
    core = at_core[0]
    chunk, width, total = cc.shape
    lanes = w_lo.shape[1]
    hidden = 2 * lanes
    blocks = 8
    depth = width // blocks
    first = chunk if second else 0

    def each_block(table, lo, hi, visit):
        for q in range(blocks):
            for side in range(2):
                at = jnp.where(core == 0, table[0][2 * q + side], table[1][2 * q + side])
                rows = slice(q * depth, (q + 1) * depth)

                def cols(e, side=side):
                    return slice(e * hidden + side * lanes, e * hidden + (side + 1) * lanes)

                @pl.when(at < blocks)
                def _():
                    visit(lo, at, rows, cols)

                @pl.when(at >= blocks)
                def _():
                    visit(hi, at - blocks, rows, cols)

    def unpack(ref, at, rows, cols):
        for e in range(chunk):
            for which, out in ((0, e_all), (1, r_all)):
                spot = pl.multiple_of(((at * 2 + which) * chunk + e) * depth, depth)
                out[rows, cols(e)] = ref[pl.ds(spot, depth), :]

    each_block(spots, w_lo, w_hi, unpack)

    e_t = [(e_all[:, e * hidden : (e + 1) * hidden] * 0.5).T for e in range(chunk)]
    r = [(r_all[:, e * hidden : (e + 1) * hidden] * 0.5).T for e in range(chunk)]
    parts = [slice(i, i + TILE) for i in range(0, total, TILE)]

    def products(e, part):
        return dot(e_t[e], xt[0:width, part], 1, 0), dot(r[e], cc[e, :, part], 1, 0)

    def finish(e, part, u, gh):
        u = u + b0[:, first + e : first + e + 1]
        t = jnp.tanh(u)
        plus = 1.0 + t
        h = u * plus
        hid[e, :, part] = h.astype(BF)
        gp[e, :, part] = (gh * (plus + h * (1.0 - t))).astype(BF)
        if part is parts[-1]:
            cols = slice(e * hidden, (e + 1) * hidden)
            acc_e[:, cols] = dot(xt[...], gp[e], 1, 1)
            acc_r[:, cols] = dot(cc[e], hid[e], 1, 1)

    held = None
    for e in range(chunk):
        for part in parts:
            ready = (e, part, *products(e, part))
            if held:
                finish(*held)
            held = ready
    finish(*held)
    sums = [acc_e[width : width + 1, e * hidden : (e + 1) * hidden] for e in range(chunk)]

    def pack(ref, at, rows, cols):
        for e in range(chunk):
            ref[pl.ds(pl.multiple_of((at * 2 * chunk + e) * depth, depth), depth), :] = acc_e[
                rows, cols(e)
            ].astype(BF)
            ref[
                pl.ds(pl.multiple_of(((at * 2 + 1) * chunk + e) * depth, depth), depth), :
            ] = acc_r[rows, cols(e)].astype(BF)

    each_block(back, g_lo, g_hi, pack)
    sums = jnp.concatenate(sums, axis=0)
    if second:
        mine = jnp.concatenate([gb0_a[...], sums], axis=0).astype(BF)
        outer = jnp.concatenate([gb1[e, 0:1] for e in range(2 * chunk)], axis=0).astype(BF)
        both = jnp.concatenate(
            [dot(mine, to_q[...], 1, 0), dot(outer, perm[...], 1, 0)], axis=0
        ).astype(BF)
        g_hi[2 * chunk * width :, :] = lanes_out(both)
    else:
        gb0[...] = sums


def critical(spots, back, at, w_lo, w_hi, xt, cc, b0, after, more=None):
    chunk, width, total = cc.shape
    rows, lanes = w_lo.shape
    hidden = 2 * lanes
    outs = [
        ((rows, lanes), BF),
        ((rows + (8 * chunk if more else 0), lanes), BF),
        ((chunk, hidden, total), BF),
        ((chunk, hidden, total), BF),
        ((width, chunk * hidden), BF),
        ((width, chunk * hidden), BF),
    ]
    if not more:
        outs.append(((chunk, hidden), F32))
    return kernel_call(
        functools.partial(critical_kernel, more is not None, spots, back),
        tuple(outs),
        (((width + ONES, chunk * hidden), F32), ((width, chunk * hidden), F32)),
        16,
        7.6,
        1,
        at, w_lo, w_hi, xt, cc, b0, *(more or ()),
        after=after,
    )


def add_low(a, b):
    return (a.astype(F32) + b.astype(F32)).astype(BF)


def fold_kernel(lo, sent, got, *refs):
    *tail, keep, msg = refs
    rows = lo.shape[0]
    half = rows // 2
    end = sent.shape[0] - half
    keep[...] = add_low(lo[0:half, :], got[0:half, :])
    msg[0:half, :] = add_low(lo[half:rows, :], got[half:rows, :])
    if end > half:
        msg[half:end, :] = add_low(sent[rows:, :], got[rows:, :])
    if tail:
        msg[end:, :] = tail[0][...]


def fold(lo, sent, got, after=(), tail=()):
    rows, lanes = lo.shape
    half = rows // 2
    end = sent.shape[0] - half + sum(x.shape[0] for x in tail)
    return kernel_call(
        fold_kernel,
        (((half, lanes), BF), ((end, lanes), BF)),
        (),
        8,
        0.3,
        0,
        lo, sent, got, *tail,
        after=after,
    )


def append_kernel(msg, one, two, out):
    rows = msg.shape[0]
    out[0:rows, :] = msg[...]
    out[rows:, :] = add_low(one[...], two[...])


def append(msg, one, two, after):
    rows, lanes = msg.shape
    (out,) = kernel_call(
        append_kernel,
        (((rows + one.shape[0], lanes), BF),),
        (),
        8,
        0.3,
        0,
        msg, one, two,
        after=after,
    )
    return out


def plus_kernel(one, two, out):
    out[...] = add_low(one[...], two[...])


def plus(one, two, after):
    (out,) = kernel_call(plus_kernel, ((one.shape, BF),), (), 8, 0.3, 0, one, two, after=after)
    return out


def last_fold_kernel(a_lo, b_lo, sent, got, own, msg):
    half = a_lo.shape[1] // 2
    size = a_lo.shape[0]
    rows = size // 2
    a_at = sent.shape[0] - size
    for i, (lo, at) in enumerate(((a_lo, a_at), (b_lo, 0))):
        e = lo[0:rows, :].astype(F32) + got[at : at + rows, :].astype(F32)
        r = lo[rows:size, :].astype(F32) + got[at + rows : at + size, :].astype(F32)
        here = slice(i * rows, (i + 1) * rows)
        own[here, :] = jnp.concatenate([e[:, :half], r[:, :half]], axis=1)
        msg[here, :] = jnp.concatenate([e[:, half:], r[:, half:]], axis=1).astype(BF)
    msg[size:, :] = add_low(sent[size:a_at, :], got[size:a_at, :])


def last_fold(a_lo, b_lo, sent, got):
    rows, lanes = a_lo.shape
    small = sent.shape[0] - 2 * rows
    return kernel_call(
        last_fold_kernel,
        (((rows, lanes), F32), ((rows + small, lanes), BF)),
        (),
        8,
        0.3,
        0,
        a_lo, b_lo, sent, got,
    )


def outer_kernel(start, *refs):
    if start:
        at_core, order, r_a, hid_a, r_b, hid_b, gt, logits, b1, xt, perm, acc_in, ys, gls, gsel, acc = refs
        acc[...] = acc_in[...]
    else:
        at_core, order, r_a, hid_a, r_b, hid_b, gt, logits, b1, xt, ys, gls, acc = refs
        acc[...] = jnp.zeros_like(acc)
    high = at_core[0].astype(F32)
    sign = 2.0 * high - 1.0
    _, width, rows = ys.shape
    chunk, hidden, _ = hid_a.shape
    tile = min(WIDE, rows)

    @pl.loop(0, rows // tile)
    def _(i):
        here, part = part_of(i, tile), part_of(i + start // tile, tile)
        gg = []
        wide = [gt[t, :, part].astype(F32) for t in range(TASKS)]
        for e in range(2 * chunk):
            r_all, hid = (r_a, hid_a) if e < chunk else (r_b, hid_b)
            at = e % chunk
            y = dot(r_all[:, at * hidden : (at + 1) * hidden], hid[at, :, part], 1, 0)
            y = y + b1[:, e : e + 1]
            ys[e, :, here] = y.astype(BF)
            sums = [jnp.sum(wide[t] * y, axis=0, keepdims=True) for t in range(TASKS)]
            gg.append(jnp.concatenate(sums + [jnp.zeros((TPAD - TASKS, tile), F32)], axis=0))
        gl = gate_back(
            lambda b, k: logits[(b * SELECT + k) * TPAD : (b * SELECT + k + 1) * TPAD, part],
            lambda k: logits[
                (BITS * SELECT + k) * TPAD : (BITS * SELECT + k + 1) * TPAD, part
            ],
            gg, high, sign,
        ).astype(BF)
        gls[:, here] = gl
        acc[...] += dot(gl, xt[0:width, part], 1, 1)

    if start:
        turned = dot(order[:, 0:64], acc[...].astype(BF), 0, 0).astype(BF)
        gsel[...] = lanes_out(dot(turned, perm[...], 1, 0)).astype(BF)


def outer(start, rows, at, order, first, second, gt, logits, b1, xt, more=(), after=()):
    width = gt.shape[1]
    (r_a, hid_a), (r_b, hid_b) = first, second
    chunk, hidden, _ = hid_a.shape
    outs = [((2 * chunk, width, rows), BF), ((GROWS, rows), BF)]
    scratch = ()
    if start:
        outs.append(((order.shape[1], 128), BF))
        scratch = (((GROWS, width), F32),)
    else:
        outs.append(((GROWS, width), F32))
    return kernel_call(
        functools.partial(outer_kernel, start),
        tuple(outs),
        scratch,
        16,
        4.3,
        1,
        at, order, r_a, hid_a, r_b, hid_b, gt, logits, b1, xt, *more,
        after=after,
    )


def mix_kernel(start, e_a, gp_a, e_b, gp_b, selp, ys, gls, gates, out):
    count, width, rows = ys.shape
    chunk, hidden, _ = gp_a.shape
    tile, depth = 512, 16

    @pl.loop(0, rows // tile)
    def _(i):
        here, part = part_of(i, tile), part_of(i + start // tile, tile)
        v = dot(e_a[...], gp_a[:, :, part].reshape(chunk * hidden, tile), 1, 0)
        v = v + dot(e_b[...], gp_b[:, :, part].reshape(chunk * hidden, tile), 1, 0)
        out[TASKS, :, here] = (v + dot(selp[...], gls[:, here], 0, 0)).astype(BF)
        for d in range(width // depth):
            block = slice(d * depth, (d + 1) * depth)
            sums = [None] * TASKS
            for e in range(count):
                y = ys[e, block, here].astype(F32)
                for t in range(TASKS):
                    m = gates[e, t : t + 1, part] * y
                    sums[t] = m if e == 0 else sums[t] + m
            for t in range(TASKS):
                out[t, block, here] = sums[t].astype(BF)


def mix(start, first, second, selp, ys, gls, gates, after):
    (e_a, gp_a), (e_b, gp_b) = first, second
    count, width, rows = ys.shape
    chunk, hidden, _ = gp_a.shape
    (out,) = kernel_call(
        functools.partial(mix_kernel, start),
        (((TASKS + 1, width, rows), BF),),
        (),
        16,
        4.0,
        0,
        e_a, gp_a, e_b, gp_b, selp, ys, gls, gates,
        after=after,
    )
    return out


def gate_back(z_of, a_of, gg, high, sign):
    alpha, smooth, clipped, f_high = gate_parts(z_of, a_of, high)
    out = [None] * GROUPS
    d_alpha = []
    for k in range(SELECT):
        f = [[fac(smooth, b, k, bit) for bit in range(2)] for b in range(BITS - 1)]
        low, dif = {}, {}
        for e2 in range(2):
            for e1 in range(2):
                p, q = gg[4 * e2 + 2 * e1], gg[4 * e2 + 2 * e1 + 1]
                low[e2, e1] = f[0][0] * p + f[0][1] * q
                dif[e2, e1] = q - p
        mid = [f[1][0] * low[e2, 0] + f[1][1] * low[e2, 1] for e2 in range(2)]
        mid1 = [low[e2, 1] - low[e2, 0] for e2 in range(2)]
        mid0 = [f[1][0] * dif[e2, 0] + f[1][1] * dif[e2, 1] for e2 in range(2)]
        t0 = f[2][0] * mid[0] + f[2][1] * mid[1]
        d2 = mid[1] - mid[0]
        d1 = f[2][0] * mid1[0] + f[2][1] * mid1[1]
        d0 = f[2][0] * mid0[0] + f[2][1] * mid0[1]
        d_alpha.append(f_high[k] * t0)
        scale = alpha[k] * f_high[k]
        for b, d in enumerate((scale * d0, scale * d1, scale * d2, alpha[k] * sign * t0)):
            v = clipped[b, k]
            out[b * SELECT + k] = d * (1.5 / GAMMA - 6.0 / GAMMA**3 * v * v)
    total = functools.reduce(jnp.add, [a * d for a, d in zip(alpha, d_alpha)])
    for k in range(SELECT):
        out[BITS * SELECT + k] = alpha[k] * (d_alpha[k] - total)
    return jnp.concatenate(out, axis=0)


def final_kernel(masks, at, own, recv, mixed, gf, token):
    token[...] = jnp.zeros_like(token)
    width = gf.shape[1]
    d_of, _ = places(masks, at, width)
    up = lax.broadcasted_iota(jnp.int32, (width, width), 0)
    across = lax.broadcasted_iota(jnp.int32, (width, width), 1)
    perm = (d_of(up) == across).astype(F32).astype(BF)
    for t in range(TASKS + 1):
        s = (own[t].astype(F32) + recv[t].astype(F32)).astype(BF)
        rows = dot(s, perm, 0, 0).astype(BF)
        if t < TASKS:
            mixed[t] = rows
        else:
            gf[...] = rows


def final(masks, at, own, recv, after):
    _, width, rows = own.shape
    return kernel_call(
        functools.partial(final_kernel, masks),
        (((TASKS, rows, width), BF), ((rows, width), BF), ((8, 128), F32)),
        (),
        16,
        2.7,
        1,
        at, own, recv,
        after=after,
    )


def adamw(weight, grad, first, second):
    first = BETA_ONE * first + (1.0 - BETA_ONE) * grad
    second = BETA_TWO * second + (1.0 - BETA_TWO) * grad * grad
    mhat = first / (1.0 - BETA_ONE**STEP)
    vhat = second / (1.0 - BETA_TWO**STEP)
    weight = weight - RATE * (mhat / (jnp.sqrt(vhat) + EPSILON) + DECAY * weight)
    return (first, second, weight)


def pack_kernel(with_w, core, w_e, w_r, w_b, w_s, sel, bias, *refs):
    first = core[0] == 0
    sel[...] = jnp.zeros_like(sel)
    sel[:, 0 : w_s.shape[1]] = w_s[...].astype(BF)
    experts, lanes = w_b.shape[1:]
    for k in range(2):
        high = w_b[k].astype(BF)
        low = (w_b[k] - high.astype(F32)).astype(BF)
        bias[k * experts : (k + 1) * experts, :] = jnp.concatenate(
            [high.astype(F32), low.astype(F32)], axis=1
        ).astype(BF)
    if with_w:
        mine, other = refs
        count = experts // 2
        for e in range(count):
            for which in range(2):
                lo, hi = (
                    (w_r[e], w_r[e + count]) if which else (w_e[:, e, :], w_e[:, e + count, :])
                )
                mine[which, e] = jnp.where(first, lo, hi).astype(BF)
                other[which, e] = jnp.where(first, hi, lo).astype(BF)


def pack(core, w_e, w_r, w_b, w_s, with_w):
    experts, depth, lanes = w_r.shape
    half = (2, experts // 2, depth, lanes)
    outs = [((depth, 2 * lanes), BF), ((2 * experts, 2 * lanes), BF)]
    if with_w:
        outs += [(half, BF), (half, BF)]
    block = lambda shape: pl.BlockSpec(shape, lambda i: (0,) * len(shape))
    return pl.pallas_call(
        functools.partial(pack_kernel, with_w),
        grid=(1,),
        out_shape=tuple(jax.ShapeDtypeStruct(shape, kind) for shape, kind in outs),
        in_specs=[pl.BlockSpec(memory_space=pltpu.SMEM)]
        + [block(x.shape) for x in (w_e, w_r, w_b, w_s)],
        out_specs=tuple(block(shape) for shape, _ in outs),
        compiler_params=params(8),
    )(core, *(pltpu.with_memory_space_constraint(x, pltpu.HBM) for x in (w_e, w_r, w_b, w_s)))


def join_kernel(plan, n_in, *refs):
    ins, outs = refs[:n_in], refs[n_in:]
    for out, pieces in zip(outs, plan):
        to = 0
        for k, start, rows in pieces:
            out[to : to + rows, :] = ins[k][start : start + rows, :]
            to += rows


def join(plan, *ins, after=()):
    lanes = ins[0].shape[1]
    return kernel_call(
        functools.partial(join_kernel, plan, len(ins)),
        tuple(((sum(p[2] for p in pieces), lanes), BF) for pieces in plan),
        (),
        8,
        0.3,
        0,
        *ins,
        after=after,
    )


def chip_kernel(mine, recv, sel, msg):
    _, count, depth, lanes = mine.shape
    for which in range(2):
        for e in range(count):
            to = (which * count + e) * depth
            msg[to : to + depth, :] = jnp.concatenate([mine[which, e], recv[which, e]], axis=1)
    msg[2 * count * depth :, :] = sel[...]


def chip_message(mine, recv, sel):
    _, count, depth, lanes = mine.shape
    rows = 2 * count * depth
    (msg,) = kernel_call(
        chip_kernel, (((rows + sel.shape[0], 2 * lanes), BF),), (), 8, 0.3, 0,
        mine, recv, sel,
    )
    return msg


def update_kernel(
    at, own, sent, got, w_e, m_e, v_e, w_r, m_r, v_r, w_b, m_b, v_b, w_s, m_s, v_s, *refs
):
    outs, (g_e,) = refs[:-1], refs[-1:]
    core, row, hid = at[0], at[1], at[2]
    first = core == 0
    experts, depth, lanes = w_r.shape
    count = experts // 2
    n_own = own.shape[0]
    theirs = got[0:n_own, :].astype(F32)
    halves = (jnp.where(first, own[...], theirs), jnp.where(first, theirs, own[...]))

    def store(k, new):
        for ref, value in zip(outs[3 * k : 3 * k + 3], new):
            ref[...] = value

    parts = []
    for half in halves:
        for e in range(count):
            rows = half[e * depth : (e + 1) * depth]
            g_e[:, len(parts), :] = rows[:, :lanes]
            parts.append(rows[:, lanes:])
    store(0, adamw(w_e[...], g_e[...], m_e[...], v_e[...]))
    store(1, adamw(w_r[...], jnp.stack(parts), m_r[...], v_r[...]))

    n_bias = 8 * count // 2
    small, small_got = sent[n_own:, :], got[n_own:, :]
    bias = [lanes_in(x[0:n_bias]) for x in (small, small_got)]
    width = bias[0].shape[1]
    spot = lax.broadcasted_iota(jnp.int32, (width, lanes), 0)
    lane = lax.broadcasted_iota(jnp.int32, (width, lanes), 1)
    pick = (spot == hid * lanes + lane).astype(F32).astype(BF)
    mine, other = [dot(x, pick, 1, 0) for x in bias]
    lo, hi = jnp.where(first, mine, other), jnp.where(first, other, mine)
    g_b = jnp.stack(
        [jnp.concatenate([x[k * count : (k + 1) * count] for x in (lo, hi)], axis=0) for k in range(2)]
    )
    store(2, adamw(w_b[...], g_b, m_b[...], v_b[...]))

    g_s = lanes_in(add_low(small[n_bias:], small_got[n_bias:]))
    spot = lax.broadcasted_iota(jnp.int32, (depth, width), 0)
    lane = lax.broadcasted_iota(jnp.int32, (depth, width), 1)
    pick = (lane == row * depth + spot).astype(F32).astype(BF)
    g_s = dot(pick, g_s, 1, 1)[:, : w_s.shape[1]]
    store(3, adamw(w_s[...], g_s, m_s[...], v_s[...]))


def update(at, own, sent, got, *params):
    outs = []
    for k in range(4):
        outs += [(params[3 * k].shape, F32)] * 3
    return kernel_call(
        update_kernel,
        tuple(outs),
        ((params[0].shape, F32),),
        16,
        2.4,
        1,
        at, own, sent, got, *params,
    )


def logit_order():
    order = np.zeros((GROWS, 128), np.float32)
    for t in range(TASKS):
        for k in range(SELECT):
            for b in range(BITS):
                order[(b * SELECT + k) * TPAD + t, (t * SELECT + k) * BITS + b] = 1.0
            at = (BITS * SELECT + k) * TPAD + t
            order[at, TASKS * SELECT * BITS + t * SELECT + k] = 1.0
    return order


def per_device(
    n_rows,
    n_hid,
    features,
    w_expand,
    w_reduce,
    biases,
    w_select,
    grad_mix,
    m_expand,
    v_expand,
    m_reduce,
    v_reduce,
    m_biases,
    v_biases,
    m_select,
    v_select,
):
    d_loc, experts, h_loc = w_expand.shape
    width = d_loc * n_rows
    mine_n = experts // 2
    chunk = mine_n // 2
    row = lax.axis_index("rows")
    hid_at = lax.axis_index("hid")
    core = hid_at % 2

    bits = n_rows.bit_length() - 1
    masks = [1 << b for b in range(bits)]
    side = (0, 2)
    sibling = ((0, 1), (0, 1))
    dims = [side] + [(m, 0) for m in masks]
    if n_rows == 8:
        way = ((3, 2, 0, 1), (1, 3, 2, 0))
        back_way = ((2, 3, 0, 1), (1, 2, 3, 0))
    else:
        way = back_way = (tuple(range(len(dims))),) * 2

    def swap(x, hops):
        pairs = []
        for r in range(n_rows):
            for h in range(n_hid):
                mr, mh = hops[h % 2]
                pairs.append((r * n_hid + h, (r ^ mr) * n_hid + (h ^ mh)))
        return lax.ppermute(x, ("rows", "hid"), pairs)

    def hops(step):
        return tuple(dims[way[k][step]] for k in range(2))

    def back_hops(step):
        return tuple(dims[back_way[k][step]] for k in range(2))

    def table_of(pair):
        if n_rows != 8:
            return (tuple(range(16)),) * 2
        both = []
        for order in pair:
            spots = []
            for q in range(8):
                for s in range(2):
                    on = [s] + [(q >> b) & 1 for b in range(3)]
                    spots.append(sum(on[d] << order.index(d) for d in range(4)))
            both.append(tuple(spots))
        return tuple(both)

    order = jnp.asarray(logit_order(), BF)
    at = jnp.stack([core, row, hid_at]).astype(jnp.int32)

    def split_experts(x, axis):
        mine = lax.dynamic_slice_in_dim(x, core * mine_n, mine_n, axis)
        other = lax.dynamic_slice_in_dim(x, (1 - core) * mine_n, mine_n, axis)
        return mine, other

    def tie(x, *after):
        return lax.optimization_barrier((x, after))[0]

    part = n_rows // 8

    def canonical(lo, hi):
        w = jnp.concatenate([lo, hi], axis=0).reshape(8, part, 2, 2, chunk, d_loc, 2 * h_loc)
        w = jnp.transpose(w, (0, 2, 3, 4, 1, 5, 6)).reshape(2, -1, 2 * h_loc)
        return w[0], w[1]

    def uncanonical(lo, hi):
        if n_rows == 8:
            return lo, hi
        w = jnp.concatenate([lo, hi], axis=0).reshape(8, 2, 2, chunk, part, d_loc, 2 * h_loc)
        w = jnp.transpose(w, (0, 4, 1, 2, 3, 5, 6)).reshape(2, -1, 2 * h_loc)
        return w[0], w[1]

    w_r_view = jnp.transpose(w_reduce, (0, 2, 1))
    packed = pack(at, w_expand, w_r_view, biases, w_select, d_loc % 16 == 0)
    sel, b_own = packed[:2]
    if d_loc % 16 == 0:
        w_mine, w_other = packed[2:]
    else:
        w_mine, w_other = split_experts(
            jnp.stack([jnp.transpose(w_expand, (1, 0, 2)), w_r_view]).astype(BF), 1
        )
    w_recv = swap(w_other, sibling)
    b_own = jnp.concatenate([b_own, swap(b_own, sibling)], axis=0)
    x_own = features
    g_own = jnp.transpose(grad_mix, (1, 0, 2))
    x_recv = swap(tie(x_own, w_recv), sibling)
    g_recv = swap(tie(g_own, w_recv), sibling)

    steps = len(dims)
    ride = n_rows == 8
    if ride:
        whole = 2 * mine_n * d_loc
        msg = chip_message(w_mine, w_recv, sel)
        got = swap(msg, hops(0))
        (msg,) = join(
            (((0, 0, whole), (1, 0, whole), (0, whole, d_loc), (1, whole, d_loc)),), msg, got
        )
        got = swap(msg, hops(1))
        xt, gt, perm, to_q = turn(masks, at, x_own, x_recv, g_own, g_recv, (msg,))
        half = whole // 2
        group = chunk * d_loc
        pieces = [
            tuple((k, (2 * j + c) * group, group) for k in range(2) for j in range(4))
            for c in range(2)
        ]
        tail = tuple((k, 2 * whole, 2 * d_loc) for k in range(2)) + ((2, 0, 4 * experts),)
        a_msg, b_msg = join((pieces[0] + tail, pieces[1]), msg, got, b_own, after=(perm,))
        a_got = swap(a_msg, hops(2))
        n = 8 * group
        a_lo, riders = join(
            (
                ((0, 0, n), (1, 0, n)),
                ((0, n, 4 * d_loc), (1, n, 4 * d_loc), (1, n + 4 * d_loc, 4 * experts)),
            ),
            a_msg, a_got,
        )
        a_hi = swap(a_lo, hops(3))
        turned = swap(riders, sibling)
        b_got = swap(b_msg, hops(2))
    else:
        xt, gt, perm, to_q = turn(masks, at, x_own, x_recv, g_own, g_recv, (sel,))
        chip = jnp.concatenate([w_mine, w_recv], axis=3)
        bufs = [chip[None, :, :chunk], chip[None, :, chunk:]]
        for step in range(steps):
            gots = [swap(buf, hops(step)) for buf in bufs]
            if step + 1 < steps:
                bufs = [jnp.concatenate(pair, axis=0) for pair in zip(bufs, gots)]
        for m in masks:
            sel = jnp.concatenate([sel, swap(sel, ((m, 0), (m, 0)))], axis=0)
        riders = turned = jnp.concatenate([sel, swap(b_own, (side, side))], axis=0)
        (a_lo, a_hi), (b_lo, b_hi) = [canonical(*pair) for pair in zip(bufs, gots)]

    cc_a, cc_b, gates, logits, selp, gb1, b0, b1 = prep(
        masks, ride, at, order, riders, turned, b_own, xt, gt
    )

    spots, back = table_of(way), table_of(back_way)
    if ride:
        (b_lo,) = join((((0, 0, n), (1, 0, n)),), b_msg, b_got, after=(b0,))
        b_hi = swap(b_lo, hops(3))
    first = critical(spots, back, at, a_lo, a_hi, xt, cc_a, b0, (b_lo,))
    a_lo, a_msg = uncanonical(first[0], first[1])
    a_got = swap(a_msg, back_hops(steps - 1))
    second = critical(
        spots, back, at, b_lo, b_hi, xt, cc_b, b0, (first[0],), (first[6], gb1, to_q, perm)
    )
    b_lo, b_msg = second[:2]
    if not ride:
        n = b_lo.shape[0]
        b_lo, b_msg = uncanonical(b_lo, b_msg[:n])
        b_msg = jnp.concatenate([b_msg, second[1][n:]], axis=0)
    b_got = swap(b_msg, back_hops(steps - 1))
    inner = ((first[5], first[2]), (second[5], second[2]))
    ends = ((first[4], first[3]), (second[4], second[3]))
    n_own = x_own.shape[0]
    ys_own, gl_own, acc = outer(0, n_own, at, order, *inner, gt, logits, b1, xt)

    def next_a(step, lo, sent, got, after=()):
        keep, msg = fold(lo, sent, got, after)
        return keep, msg, swap(msg, back_hops(step))

    a_lo, a_msg, a_got = next_a(steps - 2, a_lo, a_msg, a_got, (b_lo,))
    ys_other, gl_other, gsel = outer(
        n_own, n_own, at, order, *inner, gt, logits, b1, xt, (perm, acc), (a_lo,)
    )
    gsel_got = swap(gsel, back_hops(steps - 1))
    b_lo, b_msg = fold(b_lo, b_msg, b_got)
    b_got = swap(b_msg, back_hops(steps - 2))
    a_lo, a_msg, a_got = next_a(steps - 3, a_lo, a_msg, a_got, (b_lo,))
    mix_other = mix(n_own, *ends, selp, ys_other, gl_other, gates, (a_lo, b_lo))
    mix_recv = swap(mix_other, sibling)
    gsel = plus(gsel, gsel_got, (mix_other,))
    gsel_got = swap(gsel, back_hops(steps - 2))
    b_lo, b_msg = fold(b_lo, b_msg, b_got, (mix_other,))
    b_msg = append(b_msg, gsel, gsel_got, (b_lo,))
    b_got = swap(b_msg, back_hops(steps - 3))
    mix_own = mix(0, *ends, selp, ys_own, gl_own, gates, (b_msg,))
    for step in reversed(range(1, steps - 3)):
        a_lo, a_msg, a_got = next_a(step, a_lo, a_msg, a_got, (mix_own,))
    a_lo, a_msg = fold(a_lo, a_msg, a_got, (mix_own,))
    mixed, grad_features, token = final(masks, at, mix_own, mix_recv, (a_lo, b_msg))
    for step in reversed(range(steps - 3)):
        tail = () if step else (a_msg,)
        b_lo, b_msg = fold(b_lo, b_msg, b_got, (token,), tail)
        b_got = swap(b_msg, back_hops(step))
    own, msg = last_fold(a_lo, b_lo, b_msg, b_got)
    got = swap(msg, sibling)
    mixed = jnp.transpose(mixed, (1, 0, 2))

    flip = lambda x: jnp.transpose(x, (0, 2, 1))
    new = list(
        update(
            at, own, msg, got,
            w_expand, m_expand, v_expand,
            w_r_view, flip(m_reduce), flip(v_reduce),
            biases, m_biases, v_biases,
            w_select, m_select, v_select,
        )
    )
    new[3:6] = [flip(x) for x in new[3:6]]
    return (mixed, grad_features, *new)


def solution(mesh):
    row_split = P(("rows", "hid"), None)
    task_split = P(("rows", "hid"), None, None)
    expand = P("rows", None, "hid")
    reduce = P(None, "hid", "rows")
    bias = P(None, None, "hid")
    select = P("rows", None)
    return jax.shard_map(
        functools.partial(per_device, mesh.shape["rows"], mesh.shape["hid"]),
        mesh=mesh,
        in_specs=(
            row_split, expand, reduce, bias, select, task_split,
            expand, expand, reduce, reduce, bias, bias, select, select,
        ),
        out_specs=(
            task_split, row_split,
            expand, expand, expand,
            reduce, reduce, reduce,
            bias, bias, bias,
            select, select, select,
        ),
        check_vma=False,
    )
```

```python
import functools

import jax
import jax.numpy as jnp
import numpy as np
from jax import lax
from jax.experimental import pallas as pl
from jax.experimental.pallas import tpu as pltpu
from jax.sharding import PartitionSpec as P

TASKS = 3
SELECT = 4
BITS = 4
STEP = 5
GAMMA = 2.0
RATE = 0.05
DECAY = 0.01
EPSILON = 1e-08
BETA_ONE = 0.5
BETA_TWO = 0.5

BF = jnp.bfloat16
F32 = jnp.float32
HIGHEST = lax.Precision.HIGHEST
TPAD = 8
GROUPS = BITS * SELECT + SELECT
GROWS = GROUPS * TPAD
ONES = 16
TILE = 256
WIDE = 1024
MIB = 1 << 20
FLOPS_MICRO = 1.2e10


def dot(a, b, ca, cb, precision=None):
    return lax.dot_general(
        a, b, (((ca,), (cb,)), ((), ())), preferred_element_type=F32, precision=precision
    )


def params(mib):
    return pltpu.CompilerParams(vmem_limit_bytes=mib * MIB)


def kernel_call(body, outs, scratch, mib, micros, smem, *args, after=(), far=0, sems=0):
    in_vmem = pl.BlockSpec(memory_space=pltpu.VMEM)
    in_smem = pl.BlockSpec(memory_space=pltpu.SMEM)
    anywhere = pl.BlockSpec(memory_space=pl.ANY)
    n_in, n_after = len(args), len(after)

    def kernel(*refs):
        body(*refs[:n_in], *refs[n_in + n_after :])

    return pl.pallas_call(
        kernel,
        out_shape=tuple(jax.ShapeDtypeStruct(shape, kind) for shape, kind in outs),
        in_specs=[in_smem] * smem + [in_vmem] * (len(args) - smem) + [anywhere] * len(after),
        out_specs=(anywhere,) * far + (in_vmem,) * (len(outs) - far),
        scratch_shapes=[pltpu.VMEM(shape, kind) for shape, kind in scratch]
        + ([pltpu.SemaphoreType.DMA((sems or far,))] if far else []),
        compiler_params=params(mib),
        cost_estimate=pl.CostEstimate(
            flops=int(micros * FLOPS_MICRO), bytes_accessed=0, transcendentals=0
        ),
    )(*args, *after)


def gate_parts(z_of, a_of, high):
    smooth, clipped = {}, {}
    for k in range(SELECT):
        for b in range(BITS):
            v = jnp.clip(z_of(b, k), -0.5 * GAMMA, 0.5 * GAMMA)
            clipped[b, k] = v
            smooth[b, k] = v * (1.5 / GAMMA - 2.0 / GAMMA**3 * v * v) + 0.5
    a = [a_of(k) for k in range(SELECT)]
    top = functools.reduce(jnp.maximum, a)
    ex = [jnp.exp(v - top) for v in a]
    inv = 1.0 / functools.reduce(jnp.add, ex)
    alpha = [v * inv for v in ex]
    last = BITS - 1
    f_high = [
        high * smooth[last, k] + (1.0 - high) * (1.0 - smooth[last, k]) for k in range(SELECT)
    ]
    return alpha, smooth, clipped, f_high


def fac(smooth, b, k, bit):
    return smooth[b, k] if bit else 1.0 - smooth[b, k]


def part_of(i, tile):
    return pl.ds(pl.multiple_of(i * tile, tile), tile)


def places(masks, at, width):
    row, hid = at[1], at[2]
    depth = width // (1 << len(masks))

    def d_of(spot):
        block, out = spot // depth, row
        for b, m in enumerate(masks):
            out = out ^ (((block >> b) & 1) * m)
        return out * depth + spot % depth

    def q_of(spot):
        lanes = width // 4
        return (hid ^ (spot // lanes)) * lanes + spot % lanes

    return d_of, q_of


def turn_kernel(masks, at, xo, xr, go, gr, xt, gt, perm, to_q):
    rows, width = xo.shape
    d_of, q_of = places(masks, at, width)
    up = lax.broadcasted_iota(jnp.int32, (width, width), 0)
    across = lax.broadcasted_iota(jnp.int32, (width, width), 1)
    perm[...] = (d_of(up) == across).astype(F32).astype(BF)
    to_q[...] = (q_of(up) == across).astype(F32).astype(BF)
    xt[width : width + ONES, :] = jnp.ones((ONES, xt.shape[1]), BF)
    tile = min(WIDE, rows)
    for x, g, start in ((xo, go, 0), (xr, gr, rows)):
        for i in range(rows // tile):
            here = slice(i * tile, (i + 1) * tile)
            out = slice(start + i * tile, start + (i + 1) * tile)
            xt[0:width, out] = dot(perm[...], x[here, :], 1, 1).astype(BF)
            for t in range(TASKS):
                gt[t, :, out] = dot(perm[...], g[t, here, :], 1, 1).astype(BF)


def turn(masks, at, x_own, x_recv, g_own, g_recv, after):
    rows, width = x_own.shape
    total = 2 * rows
    return kernel_call(
        functools.partial(turn_kernel, masks),
        (
            ((width + ONES, total), BF),
            ((TASKS, width, total), BF),
            ((width, width), BF),
            ((width, width), BF),
        ),
        (),
        12,
        3.5,
        1,
        at, x_own, x_recv, g_own, g_recv,
        after=after,
    )


def prep_kernel(
    masks, ride, at, order, riders, turned, b_own, xt, gt,
    cc_a, gates, logits, selp, gb1, b0, b1, sel,
):
    core = at[0]
    high = core.astype(F32)
    _, width, total = gt.shape
    tile = min(WIDE, total)
    d_of, q_of = places(masks, at, width)
    up = lax.broadcasted_iota(jnp.int32, (width, width), 0)
    across = lax.broadcasted_iota(jnp.int32, (width, width), 1)
    one = lambda same: same.astype(F32)
    n_b = b_own.shape[0] // 2
    if ride:
        depth = width // 8
        for q in range(8):
            spot = (q >> 2) + 2 * (q >> 1 & 1) + 4 * (q & 1)
            rows = slice(spot * depth, (spot + 1) * depth)
            sel[q * depth : (q + 1) * depth, :] = jnp.where(core == 1, riders[rows, :], turned[rows, :])
        side = [
            jnp.where(
                core == 0,
                riders[width + k * n_b : width + (k + 1) * n_b, :],
                turned[width + (1 - k) * n_b : width + (2 - k) * n_b, :],
            )
            for k in range(2)
        ]
    else:
        sel[...] = riders[0:width, :]
        side = [riders[width + k * n_b : width + (k + 1) * n_b, :] for k in range(2)]
    pieces = []
    for block in [b_own[k * n_b : (k + 1) * n_b, :] for k in range(2)] + side:
        block = block.astype(F32)
        pieces.append(block[:, : width // 4] + block[:, width // 4 :])
    take = lambda x, k: jnp.where(core == 0, x[16 * k : 16 * k + 8], x[16 * k + 8 : 16 * k + 16])
    bias = [jnp.concatenate([take(x, k) for x in pieces], axis=1) for k in range(2)]
    b0[...] = dot(one(up == across), 0.5 * bias[0], 1, 1, HIGHEST)
    b1[...] = dot(one(d_of(up) == q_of(across)), bias[1], 1, 1, HIGHEST)
    selp[...] = dot(order[...], sel[...], 1, 1).astype(BF)
    gb1[...] = jnp.zeros_like(gb1)

    @pl.loop(0, total // tile)
    def _(i):
        part = part_of(i, tile)
        lg = dot(selp[...], xt[0:width, part], 1, 0)
        logits[:, part] = lg

        def z_of(b, k):
            at = (b * SELECT + k) * TPAD
            return lg[at : at + TPAD]

        def a_of(k):
            at = (BITS * SELECT + k) * TPAD
            return lg[at : at + TPAD]

        alpha, smooth, _, f_high = gate_parts(z_of, a_of, high)
        gate = [None] * 8
        for k in range(SELECT):
            base = alpha[k] * f_high[k]
            for e2 in range(2):
                w2 = base * fac(smooth, 2, k, e2)
                for e1 in range(2):
                    w1 = w2 * fac(smooth, 1, k, e1)
                    for e0 in range(2):
                        e = 4 * e2 + 2 * e1 + e0
                        w0 = w1 * fac(smooth, 0, k, e0)
                        gate[e] = w0 if gate[e] is None else gate[e] + w0
        for e in range(8):
            gates[e, :, part] = gate[e]
        combine(gate[0:4], gt, part, cc_a, gb1)


def combine(gate, gt, part, cc, gb1):
    ones = jnp.ones((8, part.size), BF)
    low = [[g[t : t + 1].astype(BF) for t in range(TASKS)] for g in gate]
    for e in range(4):
        c = low[e][0] * gt[0, :, part]
        for t in range(1, TASKS):
            c = c + low[e][t] * gt[t, :, part]
        cc[e, :, part] = c
        gb1[e] += dot(ones, c, 1, 1)


def late_kernel(gates, gt, cc, gb1):
    total = gt.shape[2]
    tile = min(WIDE, total)
    gb1[...] = jnp.zeros_like(gb1)

    @pl.loop(0, total // tile)
    def _(i):
        part = part_of(i, tile)
        combine([gates[4 + e, :, part] for e in range(4)], gt, part, cc, gb1)


def late(gates, gt, after):
    _, width, total = gt.shape
    return kernel_call(
        late_kernel,
        (((4, width, total), BF), ((4, 8, width), F32)),
        (),
        12,
        2.0,
        0,
        gates, gt,
        after=after,
    )


def prep(masks, ride, at, order, riders, turned, b_own, xt, gt):
    _, width, total = gt.shape
    return kernel_call(
        functools.partial(prep_kernel, masks, ride),
        (
            ((4, width, total), BF),
            ((8, TPAD, total), F32),
            ((GROWS, total), F32),
            ((GROWS, width), BF),
            ((4, 8, width), F32),
            ((width, 8), F32),
            ((width, 8), F32),
        ),
        (((width, 128), BF),),
        14,
        5.0,
        1,
        at, order, riders, turned, b_own, xt, gt,
    )


def lanes_out(x):
    return jnp.concatenate([x[:, :128], x[:, 128:]], axis=0)


def lanes_in(x):
    rows = x.shape[0] // 2
    return jnp.concatenate([x[:rows], x[rows:]], axis=1)


def critical_kernel(second, spots, back, *refs):
    if second:
        (at_core, w_lo, w_hi, xt, cc, b0, gb0_a, gb1_a, gb1_b, to_q, perm,
         g_lo, g_hi, hid, gp, e_all, r_all, acc_e, acc_r) = refs
    else:
        (at_core, w_lo, w_hi, xt, cc, b0,
         g_lo, g_hi, hid, gp, e_all, r_all, gb0, acc_e, acc_r) = refs
    core = at_core[0]
    chunk, width, total = cc.shape
    lanes = w_lo.shape[1]
    hidden = 2 * lanes
    blocks = 8
    depth = width // blocks
    first = chunk if second else 0

    def each_block(table, lo, hi, visit):
        for q in range(blocks):
            for side in range(2):
                at = jnp.where(core == 0, table[0][2 * q + side], table[1][2 * q + side])
                rows = slice(q * depth, (q + 1) * depth)

                def cols(e, side=side):
                    return slice(e * hidden + side * lanes, e * hidden + (side + 1) * lanes)

                @pl.when(at < blocks)
                def _():
                    visit(lo, at, rows, cols)

                @pl.when(at >= blocks)
                def _():
                    visit(hi, at - blocks, rows, cols)

    def unpack(ref, at, rows, cols):
        for e in range(chunk):
            for which, out in ((0, e_all), (1, r_all)):
                spot = pl.multiple_of(((at * 2 + which) * chunk + e) * depth, depth)
                out[rows, cols(e)] = ref[pl.ds(spot, depth), :]

    each_block(spots, w_lo, w_hi, unpack)

    e_t = [(e_all[:, e * hidden : (e + 1) * hidden] * 0.5).T for e in range(chunk)]
    r = [(r_all[:, e * hidden : (e + 1) * hidden] * 0.5).T for e in range(chunk)]
    parts = [slice(i, i + TILE) for i in range(0, total, TILE)]

    def products(e, part):
        return dot(e_t[e], xt[0:width, part], 1, 0), dot(r[e], cc[e, :, part], 1, 0)

    def finish(e, part, u, gh):
        u = u + b0[:, first + e : first + e + 1]
        t = jnp.tanh(u)
        plus = 1.0 + t
        h = u * plus
        hid[e, :, part] = h.astype(BF)
        gp[e, :, part] = (gh * (plus + h * (1.0 - t))).astype(BF)
        if part is parts[-1]:
            cols = slice(e * hidden, (e + 1) * hidden)
            acc_e[:, cols] = dot(xt[...], gp[e], 1, 1)
            acc_r[:, cols] = dot(cc[e], hid[e], 1, 1)

    held = None
    for e in range(chunk):
        for part in parts:
            ready = (e, part, *products(e, part))
            if held:
                finish(*held)
            held = ready
    finish(*held)
    sums = [acc_e[width : width + 1, e * hidden : (e + 1) * hidden] for e in range(chunk)]

    def pack(ref, at, rows, cols):
        for e in range(chunk):
            ref[pl.ds(pl.multiple_of((at * 2 * chunk + e) * depth, depth), depth), :] = acc_e[
                rows, cols(e)
            ].astype(BF)
            ref[
                pl.ds(pl.multiple_of(((at * 2 + 1) * chunk + e) * depth, depth), depth), :
            ] = acc_r[rows, cols(e)].astype(BF)

    each_block(back, g_lo, g_hi, pack)
    sums = jnp.concatenate(sums, axis=0)
    if second:
        mine = jnp.concatenate([gb0_a[...], sums], axis=0).astype(BF)
        outer = jnp.concatenate(
            [x[e, 0:1] for x in (gb1_a, gb1_b) for e in range(chunk)], axis=0
        ).astype(BF)
        both = jnp.concatenate(
            [dot(mine, to_q[...], 1, 0), dot(outer, perm[...], 1, 0)], axis=0
        ).astype(BF)
        g_hi[2 * chunk * width :, :] = lanes_out(both)
    else:
        gb0[...] = sums


def critical(spots, back, at, w_lo, w_hi, xt, cc, b0, after, more=None):
    chunk, width, total = cc.shape
    rows, lanes = w_lo.shape
    hidden = 2 * lanes
    outs = [
        ((rows, lanes), BF),
        ((rows + (8 * chunk if more else 0), lanes), BF),
        ((chunk, hidden, total), BF),
        ((chunk, hidden, total), BF),
        ((width, chunk * hidden), BF),
        ((width, chunk * hidden), BF),
    ]
    if not more:
        outs.append(((chunk, hidden), F32))
    return kernel_call(
        functools.partial(critical_kernel, more is not None, spots, back),
        tuple(outs),
        (((width + ONES, chunk * hidden), F32), ((width, chunk * hidden), F32)),
        16,
        7.6,
        1,
        at, w_lo, w_hi, xt, cc, b0, *(more or ()),
        after=after,
    )


def add_low(a, b):
    return (a.astype(F32) + b.astype(F32)).astype(BF)


def fold_kernel(rows, n_small, n_tail, lo, sent, got, *refs):
    small, tail, (keep, msg) = refs[:n_small], refs[n_small : n_small + n_tail], refs[-2:]
    at = to = 0
    for size in rows:
        half = size // 2
        keep[to : to + half, :] = add_low(lo[at : at + half, :], got[at : at + half, :])
        msg[to : to + half, :] = add_low(lo[at + half : at + size, :], got[at + half : at + size, :])
        at, to = at + size, to + half
    more = sent.shape[0] - at
    if more:
        msg[to : to + more, :] = add_low(sent[at:, :], got[at:, :])
        to += more
    if small:
        msg[to:, :] = add_low(small[0][...], small[1][...])


def fold(rows, lo, sent, got, small=(), after=()):
    total = sum(rows)
    end = sent.shape[0] - total // 2 + (small[0].shape[0] if small else 0)
    return kernel_call(
        functools.partial(fold_kernel, rows, len(small), 0),
        (((total // 2, lo.shape[1]), BF), ((end, lo.shape[1]), BF)),
        (),
        8,
        0.3,
        0,
        lo, sent, got, *small,
        after=after,
    )


def pair_fold_kernel(a_lo, a_got, b_lo, b_sent, b_got, a_sent, keep, msg):
    half_b, half_a = b_lo.shape[0] // 2, a_lo.shape[0] // 2
    both = ((b_lo, b_got, half_b, 0), (a_lo, a_got, half_a, half_b))
    for lo, got, half, to in both:
        keep[to : to + half, :] = add_low(lo[0:half, :], got[0:half, :])
        msg[to : to + half, :] = add_low(lo[half : 2 * half, :], got[half : 2 * half, :])
    msg[half_a + half_b :, :] = add_low(b_sent[2 * half_b :, :], b_got[2 * half_b :, :])


def pair_fold(a_lo, a_sent, a_got, b_lo, b_sent, b_got, after=()):
    rows, lanes = a_lo.shape
    return kernel_call(
        pair_fold_kernel,
        (((rows, lanes), BF), ((b_sent.shape[0], lanes), BF)),
        (),
        8,
        0.3,
        0,
        a_lo, a_got, b_lo, b_sent, b_got, a_sent,
        after=after,
    )


def last_fold_kernel(lo, sent, got, own, msg):
    half = lo.shape[1] // 2
    size = lo.shape[0] // 2
    rows = size // 2
    for i, at in enumerate((size, 0)):
        e, r = [
            lo[k : k + rows, :].astype(F32) + got[k : k + rows, :].astype(F32)
            for k in (at, at + rows)
        ]
        here = slice(i * rows, (i + 1) * rows)
        own[here, :] = jnp.concatenate([e[:, :half], r[:, :half]], axis=1)
        msg[here, :] = jnp.concatenate([e[:, half:], r[:, half:]], axis=1).astype(BF)
    msg[size:, :] = add_low(sent[2 * size :, :], got[2 * size :, :])


def last_fold(lo, sent, got):
    rows, lanes = lo.shape
    small = sent.shape[0] - rows
    return kernel_call(
        last_fold_kernel,
        (((rows // 2, lanes), F32), ((rows // 2 + small, lanes), BF)),
        (),
        8,
        0.3,
        0,
        lo, sent, got,
    )


def outer_kernel(chunk_at, *refs):
    if chunk_at:
        at_core, order, r_all, hid, gt, logits, b1, gl_in, xt, perm, ys, gls, gsel, acc = refs
        acc[...] = jnp.zeros_like(acc)
    else:
        at_core, r_all, hid, gt, logits, b1, ys, gls = refs
    high = at_core[0].astype(F32)
    sign = 2.0 * high - 1.0
    count, hidden, total = hid.shape
    width = gt.shape[1]
    tile = min(WIDE, total)

    @pl.loop(0, total // tile)
    def _(i):
        part = part_of(i, tile)
        gg = []
        for e in range(count):
            y = dot(r_all[:, e * hidden : (e + 1) * hidden], hid[e, :, part], 1, 0)
            at = chunk_at * count + e
            y = y + b1[:, at : at + 1]
            low = y.astype(BF)
            ys[e, :, part] = low
            sums = []
            for t in range(TASKS):
                p = None
                for d in range(0, width, 32):
                    q = gt[t, d : d + 32, part] * low[d : d + 32]
                    p = q if p is None else p + q
                sums.append(jnp.sum(p.astype(F32), axis=0, keepdims=True))
            gg.append(jnp.concatenate(sums + [jnp.zeros((TPAD - TASKS, tile), F32)], axis=0))
        gl = gate_back(
            lambda b, k: logits[(b * SELECT + k) * TPAD : (b * SELECT + k + 1) * TPAD, part],
            lambda k: logits[
                (BITS * SELECT + k) * TPAD : (BITS * SELECT + k + 1) * TPAD, part
            ],
            gg, chunk_at, high, sign,
        )
        if chunk_at:
            gl = (gl + gl_in[:, part]).astype(BF)
            acc[...] += dot(gl, xt[0:width, part], 1, 1)
        gls[:, part] = gl

    if chunk_at:
        turned = dot(order[:, 0:64], acc[...].astype(BF), 0, 0).astype(BF)
        gsel[...] = lanes_out(dot(turned, perm[...], 1, 0)).astype(BF)


def outer(chunk_at, at, r_all, hid, gt, logits, b1, order=None, more=(), after=()):
    count, _, total = hid.shape
    width = gt.shape[1]
    outs = [((count, width, total), BF), ((GROWS, total), BF if chunk_at else F32)]
    if chunk_at:
        outs.append(((order.shape[1], 128), BF))
        args = (at, order, r_all, hid, gt, logits, b1, *more)
    else:
        args = (at, r_all, hid, gt, logits, b1)
    return kernel_call(
        functools.partial(outer_kernel, chunk_at),
        tuple(outs),
        (((GROWS, width), F32),) if chunk_at else (),
        16,
        4.3,
        1,
        *args,
        after=after,
    )


def mix_kernel(start, e_a, gp_a, y_a, e_b, gp_b, y_b, selp, gls, gates, out):
    chunk, hidden, _ = gp_a.shape
    _, width, rows = out.shape
    tile, depth = 512, 16

    @pl.loop(0, rows // tile)
    def _(i):
        here, part = part_of(i, tile), part_of(i + start // tile, tile)
        v = dot(e_a[...], gp_a[:, :, part].reshape(chunk * hidden, tile), 1, 0)
        v = v + dot(e_b[...], gp_b[:, :, part].reshape(chunk * hidden, tile), 1, 0)
        out[TASKS, :, here] = (v + dot(selp[...], gls[:, part], 0, 0)).astype(BF)
        for d in range(width // depth):
            block = slice(d * depth, (d + 1) * depth)
            sums = [None] * TASKS
            for e in range(2 * chunk):
                y = (y_a if e < chunk else y_b)[e % chunk, block, part].astype(F32)
                for t in range(TASKS):
                    m = gates[e, t : t + 1, part] * y
                    sums[t] = m if e == 0 else sums[t] + m
            for t in range(TASKS):
                out[t, block, here] = sums[t].astype(BF)


def mix(start, rows, first, second, selp, gls, gates, after):
    chunk, width, total = first[2].shape
    (out,) = kernel_call(
        functools.partial(mix_kernel, start),
        (((TASKS + 1, width, rows), BF),),
        (),
        16,
        4.0,
        0,
        *first, *second, selp, gls, gates,
        after=after,
    )
    return out


def gate_back(z_of, a_of, gg, e2, high, sign):
    alpha, smooth, clipped, f_high = gate_parts(z_of, a_of, high)
    out = [None] * GROUPS
    d_alpha = []
    for k in range(SELECT):
        f = [[fac(smooth, b, k, bit) for bit in range(2)] for b in range(BITS - 1)]
        low = [f[0][0] * gg[2 * e1] + f[0][1] * gg[2 * e1 + 1] for e1 in range(2)]
        dif = [gg[2 * e1 + 1] - gg[2 * e1] for e1 in range(2)]
        mid = f[1][0] * low[0] + f[1][1] * low[1]
        t0 = f[2][e2] * mid
        d2 = mid if e2 else -mid
        d1 = f[2][e2] * (low[1] - low[0])
        d0 = f[2][e2] * (f[1][0] * dif[0] + f[1][1] * dif[1])
        d_alpha.append(f_high[k] * t0)
        scale = alpha[k] * f_high[k]
        for b, d in enumerate((scale * d0, scale * d1, scale * d2, alpha[k] * sign * t0)):
            v = clipped[b, k]
            out[b * SELECT + k] = d * (1.5 / GAMMA - 6.0 / GAMMA**3 * v * v)
    total = functools.reduce(jnp.add, [a * d for a, d in zip(alpha, d_alpha)])
    for k in range(SELECT):
        out[BITS * SELECT + k] = alpha[k] * (d_alpha[k] - total)
    return jnp.concatenate(out, axis=0)


def final_kernel(masks, at, own, recv, mixed, gf, token, buf, sems):
    token[...] = jnp.zeros_like(token)
    width = buf.shape[2]
    d_of, _ = places(masks, at, width)
    up = lax.broadcasted_iota(jnp.int32, (width, width), 0)
    across = lax.broadcasted_iota(jnp.int32, (width, width), 1)
    perm = (d_of(up) == across).astype(F32).astype(BF)
    copies = []
    for t in range(TASKS + 1):
        s = (own[t].astype(F32) + recv[t].astype(F32)).astype(BF)
        buf[t] = dot(s, perm, 0, 0).astype(BF)
        to = mixed.at[t] if t < TASKS else gf
        copies.append(pltpu.make_async_copy(buf.at[t], to, sems.at[t]))
        copies[-1].start()
    for copy in copies:
        copy.wait()


def final(masks, at, own, recv, after):
    _, width, rows = own.shape
    return kernel_call(
        functools.partial(final_kernel, masks),
        (((TASKS, rows, width), BF), ((rows, width), BF), ((8, 128), F32)),
        (((TASKS + 1, rows, width), BF),),
        16,
        0.1,
        1,
        at, own, recv,
        after=after,
        far=2,
        sems=TASKS + 1,
    )


def adamw(weight, grad, first, second):
    first = BETA_ONE * first + (1.0 - BETA_ONE) * grad
    second = BETA_TWO * second + (1.0 - BETA_TWO) * grad * grad
    mhat = first / (1.0 - BETA_ONE**STEP)
    vhat = second / (1.0 - BETA_TWO**STEP)
    weight = weight - RATE * (mhat / (jnp.sqrt(vhat) + EPSILON) + DECAY * weight)
    return (first, second, weight)


def pack_kernel(with_w, core, w_e, w_r, w_b, w_s, sel, bias, *refs):
    first = core[0] == 0
    sel[...] = jnp.zeros_like(sel)
    sel[:, 0 : w_s.shape[1]] = w_s[...].astype(BF)
    experts, lanes = w_b.shape[1:]
    for k in range(2):
        high = w_b[k].astype(BF)
        low = (w_b[k] - high.astype(F32)).astype(BF)
        bias[k * experts : (k + 1) * experts, :] = jnp.concatenate(
            [high.astype(F32), low.astype(F32)], axis=1
        ).astype(BF)
    if with_w:
        mine, other = refs
        count = experts // 2
        for e in range(count):
            for which in range(2):
                lo, hi = (
                    (w_r[e], w_r[e + count]) if which else (w_e[:, e, :], w_e[:, e + count, :])
                )
                mine[which, e] = jnp.where(first, lo, hi).astype(BF)
                other[which, e] = jnp.where(first, hi, lo).astype(BF)


def pack(core, w_e, w_r, w_b, w_s, with_w):
    experts, depth, lanes = w_r.shape
    half = (2, experts // 2, depth, lanes)
    outs = [((depth, 2 * lanes), BF), ((2 * experts, 2 * lanes), BF)]
    if with_w:
        outs += [(half, BF), (half, BF)]
    block = lambda shape: pl.BlockSpec(shape, lambda i: (0,) * len(shape))
    return pl.pallas_call(
        functools.partial(pack_kernel, with_w),
        grid=(1,),
        out_shape=tuple(jax.ShapeDtypeStruct(shape, kind) for shape, kind in outs),
        in_specs=[pl.BlockSpec(memory_space=pltpu.SMEM)]
        + [block(x.shape) for x in (w_e, w_r, w_b, w_s)],
        out_specs=tuple(block(shape) for shape, _ in outs),
        compiler_params=params(8),
    )(core, *(pltpu.with_memory_space_constraint(x, pltpu.HBM) for x in (w_e, w_r, w_b, w_s)))


def join_kernel(plan, n_in, *refs):
    ins, outs = refs[:n_in], refs[n_in:]
    for out, pieces in zip(outs, plan):
        to = 0
        for k, start, rows in pieces:
            out[to : to + rows, :] = ins[k][start : start + rows, :]
            to += rows


def join(plan, *ins, after=()):
    lanes = ins[0].shape[1]
    return kernel_call(
        functools.partial(join_kernel, plan, len(ins)),
        tuple(((sum(p[2] for p in pieces), lanes), BF) for pieces in plan),
        (),
        8,
        0.3,
        0,
        *ins,
        after=after,
    )


def chip_kernel(mine, recv, sel, a_msg, b_msg):
    _, count, depth, lanes = mine.shape
    half = count // 2
    for which in range(2):
        for e in range(count):
            msg = a_msg if e < half else b_msg
            to = (which * half + e % half) * depth
            msg[to : to + depth, :] = jnp.concatenate([mine[which, e], recv[which, e]], axis=1)
    a_msg[2 * half * depth :, :] = sel[...]


def chip_messages(mine, recv, sel):
    _, count, depth, lanes = mine.shape
    rows = count * depth
    return kernel_call(
        chip_kernel,
        (((rows + sel.shape[0], 2 * lanes), BF), ((rows, 2 * lanes), BF)),
        (),
        8,
        0.3,
        0,
        mine, recv, sel,
    )


def update_kernel(
    at, own, sent, got, w_e, m_e, v_e, w_r, m_r, v_r, w_b, m_b, v_b, w_s, m_s, v_s, *refs
):
    outs, (g_e,) = refs[:-1], refs[-1:]
    core, row, hid = at[0], at[1], at[2]
    first = core == 0
    experts, depth, lanes = w_r.shape
    count = experts // 2
    n_own = own.shape[0]
    theirs = got[0:n_own, :].astype(F32)
    halves = (jnp.where(first, own[...], theirs), jnp.where(first, theirs, own[...]))

    def store(k, new):
        for ref, value in zip(outs[3 * k : 3 * k + 3], new):
            ref[...] = value

    parts = []
    for half in halves:
        for e in range(count):
            rows = half[e * depth : (e + 1) * depth]
            g_e[:, len(parts), :] = rows[:, :lanes]
            parts.append(rows[:, lanes:])
    store(0, adamw(w_e[...], g_e[...], m_e[...], v_e[...]))
    store(1, adamw(w_r[...], jnp.stack(parts), m_r[...], v_r[...]))

    n_bias = 8 * count // 2
    small, small_got = sent[n_own:, :], got[n_own:, :]
    bias = [lanes_in(x[0:n_bias]) for x in (small, small_got)]
    width = bias[0].shape[1]
    spot = lax.broadcasted_iota(jnp.int32, (width, lanes), 0)
    lane = lax.broadcasted_iota(jnp.int32, (width, lanes), 1)
    pick = (spot == hid * lanes + lane).astype(F32).astype(BF)
    mine, other = [dot(x, pick, 1, 0) for x in bias]
    lo, hi = jnp.where(first, mine, other), jnp.where(first, other, mine)
    g_b = jnp.stack(
        [jnp.concatenate([x[k * count : (k + 1) * count] for x in (lo, hi)], axis=0) for k in range(2)]
    )
    store(2, adamw(w_b[...], g_b, m_b[...], v_b[...]))

    g_s = lanes_in(add_low(small[n_bias:], small_got[n_bias:]))
    spot = lax.broadcasted_iota(jnp.int32, (depth, width), 0)
    lane = lax.broadcasted_iota(jnp.int32, (depth, width), 1)
    pick = (lane == row * depth + spot).astype(F32).astype(BF)
    g_s = dot(pick, g_s, 1, 1)[:, : w_s.shape[1]]
    store(3, adamw(w_s[...], g_s, m_s[...], v_s[...]))


def update(at, own, sent, got, *params):
    outs = []
    for k in range(4):
        outs += [(params[3 * k].shape, F32)] * 3
    return kernel_call(
        update_kernel,
        tuple(outs),
        ((params[0].shape, F32),),
        16,
        2.4,
        1,
        at, own, sent, got, *params,
    )


def logit_order():
    order = np.zeros((GROWS, 128), np.float32)
    for t in range(TASKS):
        for k in range(SELECT):
            for b in range(BITS):
                order[(b * SELECT + k) * TPAD + t, (t * SELECT + k) * BITS + b] = 1.0
            at = (BITS * SELECT + k) * TPAD + t
            order[at, TASKS * SELECT * BITS + t * SELECT + k] = 1.0
    return order


def per_device(
    n_rows,
    n_hid,
    features,
    w_expand,
    w_reduce,
    biases,
    w_select,
    grad_mix,
    m_expand,
    v_expand,
    m_reduce,
    v_reduce,
    m_biases,
    v_biases,
    m_select,
    v_select,
):
    d_loc, experts, h_loc = w_expand.shape
    width = d_loc * n_rows
    mine_n = experts // 2
    chunk = mine_n // 2
    row = lax.axis_index("rows")
    hid_at = lax.axis_index("hid")
    core = hid_at % 2

    bits = n_rows.bit_length() - 1
    masks = [1 << b for b in range(bits)]
    side = (0, 2)
    sibling = ((0, 1), (0, 1))
    dims = [side] + [(m, 0) for m in masks]
    if n_rows == 8:
        way = ((3, 2, 0, 1), (3, 2, 1, 0))
        back_way = ((2, 3, 0, 1), (1, 2, 3, 0))
    else:
        way = back_way = (tuple(range(len(dims))),) * 2

    def swap(x, hops):
        pairs = []
        for r in range(n_rows):
            for h in range(n_hid):
                mr, mh = hops[h % 2]
                pairs.append((r * n_hid + h, (r ^ mr) * n_hid + (h ^ mh)))
        return lax.ppermute(x, ("rows", "hid"), pairs)

    def hops(step):
        return tuple(dims[way[k][step]] for k in range(2))

    def back_hops(step):
        return tuple(dims[back_way[k][step]] for k in range(2))

    def table_of(pair):
        if n_rows != 8:
            return (tuple(range(16)),) * 2
        both = []
        for order in pair:
            spots = []
            for q in range(8):
                for s in range(2):
                    on = [s] + [(q >> b) & 1 for b in range(3)]
                    spots.append(sum(on[d] << order.index(d) for d in range(4)))
            both.append(tuple(spots))
        return tuple(both)

    order = jnp.asarray(logit_order(), BF)
    at = jnp.stack([core, row, hid_at]).astype(jnp.int32)

    def split_experts(x, axis):
        mine = lax.dynamic_slice_in_dim(x, core * mine_n, mine_n, axis)
        other = lax.dynamic_slice_in_dim(x, (1 - core) * mine_n, mine_n, axis)
        return mine, other

    def tie(x, *after):
        return lax.optimization_barrier((x, after))[0]

    part = n_rows // 8

    def canonical(lo, hi):
        w = jnp.concatenate([lo, hi], axis=0).reshape(8, part, 2, 2, chunk, d_loc, 2 * h_loc)
        w = jnp.transpose(w, (0, 2, 3, 4, 1, 5, 6)).reshape(2, -1, 2 * h_loc)
        return w[0], w[1]

    def uncanonical(lo, hi):
        if n_rows == 8:
            return lo, hi
        w = jnp.concatenate([lo, hi], axis=0).reshape(8, 2, 2, chunk, part, d_loc, 2 * h_loc)
        w = jnp.transpose(w, (0, 4, 1, 2, 3, 5, 6)).reshape(2, -1, 2 * h_loc)
        return w[0], w[1]

    w_r_view = jnp.transpose(w_reduce, (0, 2, 1))
    packed = pack(at, w_expand, w_r_view, biases, w_select, d_loc % 16 == 0)
    sel, b_own = packed[:2]
    if d_loc % 16 == 0:
        w_mine, w_other = packed[2:]
    else:
        w_mine, w_other = split_experts(
            jnp.stack([jnp.transpose(w_expand, (1, 0, 2)), w_r_view]).astype(BF), 1
        )
    w_recv = swap(w_other, sibling)
    n_b = b_own.shape[0]
    (b_own,) = join((((0, 0, n_b), (1, 0, n_b)),), b_own, swap(b_own, sibling))
    x_own = features
    g_own = jnp.transpose(grad_mix, (1, 0, 2))
    x_recv = swap(tie(x_own, w_recv), sibling)
    g_recv = swap(tie(g_own, w_recv), sibling)

    steps = len(dims)
    ride = n_rows == 8
    if ride:
        n = chunk * d_loc * 2
        a_msg, b_msg = chip_messages(w_mine, w_recv, sel)
        a_got = swap(a_msg, hops(0))
        (a_msg,) = join((((0, 0, n), (1, 0, n), (0, n, d_loc), (1, n, d_loc)),), a_msg, a_got)
        b_got = swap(tie(b_msg, a_got), hops(0))
        a_got = swap(a_msg, hops(1))
        xt, gt, perm, to_q = turn(masks, at, x_own, x_recv, g_own, g_recv, (a_msg,))
        n *= 2
        tail = tuple((k, n, 2 * d_loc) for k in range(2)) + ((2, 0, 4 * experts),)
        (a_msg,) = join(
            (((0, 0, n), (1, 0, n)) + tail,), a_msg, a_got, b_own, after=(perm,)
        )
        a_got = swap(a_msg, hops(2))
        both = lambda x, y, after: join(
            (((0, 0, x.shape[0]), (1, 0, x.shape[0])),), x, y, after=after
        )[0]
        b_msg = both(b_msg, b_got, (a_msg,))
        b_got = swap(b_msg, hops(1))
        n *= 2
        a_lo, riders = join(
            (
                ((0, 0, n), (1, 0, n)),
                ((0, n, 4 * d_loc), (1, n, 4 * d_loc), (1, n + 4 * d_loc, 4 * experts)),
            ),
            a_msg, a_got,
        )
        a_hi = swap(a_lo, hops(3))
        turned = swap(riders, sibling)
        b_msg = both(b_msg, b_got, (a_lo,))
        b_got = swap(b_msg, hops(2))
    else:
        xt, gt, perm, to_q = turn(masks, at, x_own, x_recv, g_own, g_recv, (sel,))
        chip = jnp.concatenate([w_mine, w_recv], axis=3)
        bufs = [chip[None, :, :chunk], chip[None, :, chunk:]]
        for step in range(steps):
            gots = [swap(buf, hops(step)) for buf in bufs]
            if step + 1 < steps:
                bufs = [jnp.concatenate(pair, axis=0) for pair in zip(bufs, gots)]
        for m in masks:
            sel = jnp.concatenate([sel, swap(sel, ((m, 0), (m, 0)))], axis=0)
        riders = turned = jnp.concatenate([sel, swap(b_own, (side, side))], axis=0)
        (a_lo, a_hi), (b_lo, b_hi) = [canonical(*pair) for pair in zip(bufs, gots)]

    cc_a, gates, logits, selp, gb1_a, b0, b1 = prep(
        masks, ride, at, order, riders, turned, b_own, xt, gt
    )

    spots, back = table_of(way), table_of(back_way)
    cc_b, gb1_b = late(gates, gt, (b0,))
    if ride:
        b_lo = both(b_msg, b_got, (gb1_b,))
        b_hi = swap(b_lo, hops(3))
    first = critical(spots, back, at, a_lo, a_hi, xt, cc_a, b0, (b_lo,))
    a_lo, a_msg = uncanonical(first[0], first[1])
    a_got = swap(a_msg, back_hops(steps - 1))
    second = critical(
        spots, back, at, b_lo, b_hi, xt, cc_b, b0, (first[0],), (first[6], gb1_a, gb1_b, to_q, perm)
    )
    b_lo, b_msg = second[:2]
    if not ride:
        n = b_lo.shape[0]
        b_lo, b_msg = uncanonical(b_lo, b_msg[:n])
        b_msg = jnp.concatenate([b_msg, second[1][n:]], axis=0)
    b_got = swap(b_msg, back_hops(steps - 1))
    ys_a, gl_a = outer(0, at, first[5], first[2], gt, logits, b1, after=(second[0],))
    a_lo, a_msg = fold(a_lo.shape[:1], a_lo, a_msg, a_got, after=(gl_a,))
    a_got = swap(a_msg, back_hops(steps - 2))
    ys_b, gls, gsel = outer(
        1, at, second[5], second[2], gt, logits, b1, order, (gl_a, xt, perm), (a_lo,)
    )
    gsel_got = swap(gsel, back_hops(steps - 1))
    b_lo, b_msg = fold(b_lo.shape[:1], b_lo, b_msg, b_got, (gsel, gsel_got), (a_got,))
    b_got = swap(b_msg, back_hops(steps - 2))
    a_lo, a_msg = fold(a_lo.shape[:1], a_lo, a_msg, a_got, after=(b_lo,))
    a_got = swap(a_msg, back_hops(steps - 3))
    ends = ((first[4], first[3], ys_a), (second[4], second[3], ys_b))
    n_own = x_own.shape[0]
    mix_other = mix(n_own, n_own, *ends, selp, gls, gates, (a_lo, b_lo))
    mix_recv = swap(mix_other, sibling)
    b_lo, b_msg = fold(b_lo.shape[:1], b_lo, b_msg, b_got, after=(mix_other,))
    b_got = swap(b_msg, back_hops(steps - 3))
    mix_own = mix(0, n_own, *ends, selp, gls, gates, (b_lo,))
    mixed, grad_features, token = final(masks, at, mix_own, mix_recv, (b_lo,))
    for step in reversed(range(1, steps - 3)):
        a_lo, a_msg = fold(a_lo.shape[:1], a_lo, a_msg, a_got)
        b_lo, b_msg = fold(b_lo.shape[:1], b_lo, b_msg, b_got)
        a_got, b_got = swap(a_msg, back_hops(step)), swap(b_msg, back_hops(step))
    lo, msg = pair_fold(a_lo, a_msg, a_got, b_lo, b_msg, b_got, (token,))
    got = swap(msg, back_hops(0))
    own, msg = last_fold(lo, msg, got)
    got = swap(msg, sibling)
    mixed = jnp.transpose(mixed, (1, 0, 2))

    flip = lambda x: jnp.transpose(x, (0, 2, 1))
    new = list(
        update(
            at, own, msg, got,
            w_expand, m_expand, v_expand,
            w_r_view, flip(m_reduce), flip(v_reduce),
            biases, m_biases, v_biases,
            w_select, m_select, v_select,
        )
    )
    new[3:6] = [flip(x) for x in new[3:6]]
    return (mixed, grad_features, *new)


def solution(mesh):
    row_split = P(("rows", "hid"), None)
    task_split = P(("rows", "hid"), None, None)
    expand = P("rows", None, "hid")
    reduce = P(None, "hid", "rows")
    bias = P(None, None, "hid")
    select = P("rows", None)
    return jax.shard_map(
        functools.partial(per_device, mesh.shape["rows"], mesh.shape["hid"]),
        mesh=mesh,
        in_specs=(
            row_split, expand, reduce, bias, select, task_split,
            expand, expand, reduce, reduce, bias, bias, select, select,
        ),
        out_specs=(
            task_split, row_split,
            expand, expand, expand,
            reduce, reduce, reduce,
            bias, bias, bias,
            select, select, select,
        ),
        check_vma=False,
    )
```

```python
import functools

import jax
import jax.numpy as jnp
import numpy as np
from jax import lax
from jax.experimental import pallas as pl
from jax.experimental.pallas import tpu as pltpu
from jax.sharding import PartitionSpec as P

TASKS = 3
SELECT = 4
BITS = 4
STEP = 5
GAMMA = 2.0
RATE = 0.05
DECAY = 0.01
EPSILON = 1e-08
BETA_ONE = 0.5
BETA_TWO = 0.5

BF = jnp.bfloat16
F32 = jnp.float32
HIGHEST = lax.Precision.HIGHEST
TPAD = 8
GROUPS = BITS * SELECT + SELECT
GROWS = GROUPS * TPAD
ONES = 16
TILE = 256
WIDE = 1024
MIB = 1 << 20
FLOPS_MICRO = 1.2e10


def dot(a, b, ca, cb, precision=None):
    return lax.dot_general(
        a, b, (((ca,), (cb,)), ((), ())), preferred_element_type=F32, precision=precision
    )


def params(mib):
    return pltpu.CompilerParams(vmem_limit_bytes=mib * MIB)


def kernel_call(body, outs, scratch, mib, micros, smem, *args, after=(), far=0, sems=0):
    in_vmem = pl.BlockSpec(memory_space=pltpu.VMEM)
    in_smem = pl.BlockSpec(memory_space=pltpu.SMEM)
    anywhere = pl.BlockSpec(memory_space=pl.ANY)
    n_in, n_after = len(args), len(after)

    def kernel(*refs):
        body(*refs[:n_in], *refs[n_in + n_after :])

    return pl.pallas_call(
        kernel,
        out_shape=tuple(jax.ShapeDtypeStruct(shape, kind) for shape, kind in outs),
        in_specs=[in_smem] * smem + [in_vmem] * (len(args) - smem) + [anywhere] * len(after),
        out_specs=(anywhere,) * far + (in_vmem,) * (len(outs) - far),
        scratch_shapes=[pltpu.VMEM(shape, kind) for shape, kind in scratch]
        + ([pltpu.SemaphoreType.DMA((sems or far,))] if far else []),
        compiler_params=params(mib),
        cost_estimate=pl.CostEstimate(
            flops=int(micros * FLOPS_MICRO), bytes_accessed=0, transcendentals=0
        ),
    )(*args, *after)


def gate_parts(z_of, a_of, high):
    smooth, clipped = {}, {}
    for k in range(SELECT):
        for b in range(BITS):
            v = jnp.clip(z_of(b, k), -0.5 * GAMMA, 0.5 * GAMMA)
            clipped[b, k] = v
            smooth[b, k] = v * (1.5 / GAMMA - 2.0 / GAMMA**3 * v * v) + 0.5
    a = [a_of(k) for k in range(SELECT)]
    top = functools.reduce(jnp.maximum, a)
    ex = [jnp.exp(v - top) for v in a]
    inv = 1.0 / functools.reduce(jnp.add, ex)
    alpha = [v * inv for v in ex]
    last = BITS - 1
    f_high = [
        high * smooth[last, k] + (1.0 - high) * (1.0 - smooth[last, k]) for k in range(SELECT)
    ]
    return alpha, smooth, clipped, f_high


def fac(smooth, b, k, bit):
    return smooth[b, k] if bit else 1.0 - smooth[b, k]


def part_of(i, tile):
    return pl.ds(pl.multiple_of(i * tile, tile), tile)


def places(masks, at, width):
    row, hid = at[1], at[2]
    depth = width // (1 << len(masks))

    def d_of(spot):
        block, out = spot // depth, row
        for b, m in enumerate(masks):
            out = out ^ (((block >> b) & 1) * m)
        return out * depth + spot % depth

    def q_of(spot):
        lanes = width // 4
        return (hid ^ (spot // lanes)) * lanes + spot % lanes

    return d_of, q_of


def turn_kernel(masks, at, xo, xr, go, gr, xt, gt, perm, to_q):
    rows, width = xo.shape
    d_of, q_of = places(masks, at, width)
    up = lax.broadcasted_iota(jnp.int32, (width, width), 0)
    across = lax.broadcasted_iota(jnp.int32, (width, width), 1)
    perm[...] = (d_of(up) == across).astype(F32).astype(BF)
    to_q[...] = (q_of(up) == across).astype(F32).astype(BF)
    xt[width : width + ONES, :] = jnp.ones((ONES, xt.shape[1]), BF)
    tile = min(WIDE, rows)
    for x, g, start in ((xo, go, 0), (xr, gr, rows)):
        for i in range(rows // tile):
            here = slice(i * tile, (i + 1) * tile)
            out = slice(start + i * tile, start + (i + 1) * tile)
            xt[0:width, out] = dot(perm[...], x[here, :], 1, 1).astype(BF)
            for t in range(TASKS):
                gt[t, :, out] = dot(perm[...], g[t, here, :], 1, 1).astype(BF)


def turn(masks, at, x_own, x_recv, g_own, g_recv, after):
    rows, width = x_own.shape
    total = 2 * rows
    return kernel_call(
        functools.partial(turn_kernel, masks),
        (
            ((width + ONES, total), BF),
            ((TASKS, width, total), BF),
            ((width, width), BF),
            ((width, width), BF),
        ),
        (),
        12,
        3.5,
        1,
        at, x_own, x_recv, g_own, g_recv,
        after=after,
    )


def prep_kernel(
    masks, ride, at, order, riders, turned, b_own, xt, gt,
    cc_a, gates, logits, selp, gb1, b0, b1, sel,
):
    core = at[0]
    high = core.astype(F32)
    _, width, total = gt.shape
    tile = min(WIDE, total)
    d_of, q_of = places(masks, at, width)
    up = lax.broadcasted_iota(jnp.int32, (width, width), 0)
    across = lax.broadcasted_iota(jnp.int32, (width, width), 1)
    one = lambda same: same.astype(F32)
    n_b = b_own.shape[0] // 2
    if ride:
        depth = width // 8
        for q in range(8):
            spot = (q >> 2) + 2 * (q >> 1 & 1) + 4 * (q & 1)
            rows = slice(spot * depth, (spot + 1) * depth)
            sel[q * depth : (q + 1) * depth, :] = jnp.where(core == 1, riders[rows, :], turned[rows, :])
        side = [
            jnp.where(
                core == 0,
                riders[width + k * n_b : width + (k + 1) * n_b, :],
                turned[width + (1 - k) * n_b : width + (2 - k) * n_b, :],
            )
            for k in range(2)
        ]
    else:
        sel[...] = riders[0:width, :]
        side = [riders[width + k * n_b : width + (k + 1) * n_b, :] for k in range(2)]
    pieces = []
    for block in [b_own[k * n_b : (k + 1) * n_b, :] for k in range(2)] + side:
        block = block.astype(F32)
        pieces.append(block[:, : width // 4] + block[:, width // 4 :])
    take = lambda x, k: jnp.where(core == 0, x[16 * k : 16 * k + 8], x[16 * k + 8 : 16 * k + 16])
    bias = [jnp.concatenate([take(x, k) for x in pieces], axis=1) for k in range(2)]
    b0[...] = dot(one(up == across), 0.5 * bias[0], 1, 1, HIGHEST)
    b1[...] = dot(one(d_of(up) == q_of(across)), bias[1], 1, 1, HIGHEST)
    selp[...] = dot(order[...], sel[...], 1, 1).astype(BF)
    gb1[...] = jnp.zeros_like(gb1)

    @pl.loop(0, total // tile)
    def _(i):
        part = part_of(i, tile)
        lg = dot(selp[...], xt[0:width, part], 1, 0)
        logits[:, part] = lg

        def z_of(b, k):
            at = (b * SELECT + k) * TPAD
            return lg[at : at + TPAD]

        def a_of(k):
            at = (BITS * SELECT + k) * TPAD
            return lg[at : at + TPAD]

        alpha, smooth, _, f_high = gate_parts(z_of, a_of, high)
        gate = [None] * 8
        for k in range(SELECT):
            base = alpha[k] * f_high[k]
            for e2 in range(2):
                w2 = base * fac(smooth, 2, k, e2)
                for e1 in range(2):
                    w1 = w2 * fac(smooth, 1, k, e1)
                    for e0 in range(2):
                        e = 4 * e2 + 2 * e1 + e0
                        w0 = w1 * fac(smooth, 0, k, e0)
                        gate[e] = w0 if gate[e] is None else gate[e] + w0
        for e in range(8):
            gates[e, :, part] = gate[e]
        combine(gate[0:4], gt, part, cc_a, gb1)


def combine(gate, gt, part, cc, gb1):
    ones = jnp.ones((8, part.size), BF)
    low = [[g[t : t + 1].astype(BF) for t in range(TASKS)] for g in gate]
    for e in range(4):
        c = low[e][0] * gt[0, :, part]
        for t in range(1, TASKS):
            c = c + low[e][t] * gt[t, :, part]
        cc[e, :, part] = c
        gb1[e] += dot(ones, c, 1, 1)


def late_kernel(gates, gt, cc, gb1):
    total = gt.shape[2]
    tile = min(WIDE, total)
    gb1[...] = jnp.zeros_like(gb1)

    @pl.loop(0, total // tile)
    def _(i):
        part = part_of(i, tile)
        combine([gates[4 + e, :, part] for e in range(4)], gt, part, cc, gb1)


def late(gates, gt, after):
    _, width, total = gt.shape
    return kernel_call(
        late_kernel,
        (((4, width, total), BF), ((4, 8, width), F32)),
        (),
        12,
        2.0,
        0,
        gates, gt,
        after=after,
    )


def prep(masks, ride, at, order, riders, turned, b_own, xt, gt):
    _, width, total = gt.shape
    return kernel_call(
        functools.partial(prep_kernel, masks, ride),
        (
            ((4, width, total), BF),
            ((8, TPAD, total), F32),
            ((GROWS, total), F32),
            ((GROWS, width), BF),
            ((4, 8, width), F32),
            ((width, 8), F32),
            ((width, 8), F32),
        ),
        (((width, 128), BF),),
        14,
        5.0,
        1,
        at, order, riders, turned, b_own, xt, gt,
    )


def lanes_out(x):
    return jnp.concatenate([x[:, :128], x[:, 128:]], axis=0)


def lanes_in(x):
    rows = x.shape[0] // 2
    return jnp.concatenate([x[:rows], x[rows:]], axis=1)


def critical_kernel(second, spots, back, *refs):
    if second:
        (at_core, w_lo, w_hi, xt, cc, b0, gb0_a, gb1_a, gb1_b, to_q, perm,
         g_lo, g_hi, hid, gp, e_all, r_all, acc_e, acc_r) = refs
    else:
        (at_core, w_lo, w_hi, xt, cc, b0,
         g_lo, g_hi, hid, gp, e_all, r_all, gb0, acc_e, acc_r) = refs
    core = at_core[0]
    chunk, width, total = cc.shape
    lanes = w_lo.shape[1]
    hidden = 2 * lanes
    blocks = 8
    depth = width // blocks
    first = chunk if second else 0

    def each_block(table, lo, hi, visit):
        for q in range(blocks):
            for side in range(2):
                at = jnp.where(core == 0, table[0][2 * q + side], table[1][2 * q + side])
                rows = slice(q * depth, (q + 1) * depth)

                def cols(e, side=side):
                    return slice(e * hidden + side * lanes, e * hidden + (side + 1) * lanes)

                @pl.when(at < blocks)
                def _():
                    visit(lo, at, rows, cols)

                @pl.when(at >= blocks)
                def _():
                    visit(hi, at - blocks, rows, cols)

    def unpack(ref, at, rows, cols):
        for e in range(chunk):
            for which, out in ((0, e_all), (1, r_all)):
                spot = pl.multiple_of(((at * 2 + which) * chunk + e) * depth, depth)
                out[rows, cols(e)] = ref[pl.ds(spot, depth), :]

    each_block(spots, w_lo, w_hi, unpack)

    e_t = [(e_all[:, e * hidden : (e + 1) * hidden] * 0.5).T for e in range(chunk)]
    r = [(r_all[:, e * hidden : (e + 1) * hidden] * 0.5).T for e in range(chunk)]
    parts = [slice(i, i + TILE) for i in range(0, total, TILE)]

    def products(e, part):
        return dot(e_t[e], xt[0:width, part], 1, 0), dot(r[e], cc[e, :, part], 1, 0)

    def finish(e, part, u, gh):
        u = u + b0[:, first + e : first + e + 1]
        t = jnp.tanh(u)
        plus = 1.0 + t
        h = u * plus
        hid[e, :, part] = h.astype(BF)
        gp[e, :, part] = (gh * (plus + h * (1.0 - t))).astype(BF)
        if part is parts[-1]:
            cols = slice(e * hidden, (e + 1) * hidden)
            acc_e[:, cols] = dot(xt[...], gp[e], 1, 1)
            acc_r[:, cols] = dot(cc[e], hid[e], 1, 1)

    held = None
    for e in range(chunk):
        for part in parts:
            ready = (e, part, *products(e, part))
            if held:
                finish(*held)
            held = ready
    finish(*held)
    sums = [acc_e[width : width + 1, e * hidden : (e + 1) * hidden] for e in range(chunk)]

    def pack(ref, at, rows, cols):
        for e in range(chunk):
            ref[pl.ds(pl.multiple_of((at * 2 * chunk + e) * depth, depth), depth), :] = acc_e[
                rows, cols(e)
            ].astype(BF)
            ref[
                pl.ds(pl.multiple_of(((at * 2 + 1) * chunk + e) * depth, depth), depth), :
            ] = acc_r[rows, cols(e)].astype(BF)

    each_block(back, g_lo, g_hi, pack)
    sums = jnp.concatenate(sums, axis=0)
    if second:
        mine = jnp.concatenate([gb0_a[...], sums], axis=0).astype(BF)
        outer = jnp.concatenate(
            [x[e, 0:1] for x in (gb1_a, gb1_b) for e in range(chunk)], axis=0
        ).astype(BF)
        both = jnp.concatenate(
            [dot(mine, to_q[...], 1, 0), dot(outer, perm[...], 1, 0)], axis=0
        ).astype(BF)
        g_hi[2 * chunk * width :, :] = lanes_out(both)
    else:
        gb0[...] = sums


def critical(spots, back, at, w_lo, w_hi, xt, cc, b0, after, more=None):
    chunk, width, total = cc.shape
    rows, lanes = w_lo.shape
    hidden = 2 * lanes
    outs = [
        ((rows, lanes), BF),
        ((rows + (8 * chunk if more else 0), lanes), BF),
        ((chunk, hidden, total), BF),
        ((chunk, hidden, total), BF),
        ((width, chunk * hidden), BF),
        ((width, chunk * hidden), BF),
    ]
    if not more:
        outs.append(((chunk, hidden), F32))
    return kernel_call(
        functools.partial(critical_kernel, more is not None, spots, back),
        tuple(outs),
        (((width + ONES, chunk * hidden), F32), ((width, chunk * hidden), F32)),
        16,
        7.6,
        1,
        at, w_lo, w_hi, xt, cc, b0, *(more or ()),
        after=after,
    )


def add_low(a, b):
    return (a.astype(F32) + b.astype(F32)).astype(BF)


def fold_kernel(rows, n_small, n_tail, lo, sent, got, *refs):
    small, tail, (keep, msg) = refs[:n_small], refs[n_small : n_small + n_tail], refs[-2:]
    at = to = 0
    for size in rows:
        half = size // 2
        keep[to : to + half, :] = add_low(lo[at : at + half, :], got[at : at + half, :])
        msg[to : to + half, :] = add_low(lo[at + half : at + size, :], got[at + half : at + size, :])
        at, to = at + size, to + half
    more = sent.shape[0] - at
    if more:
        msg[to : to + more, :] = add_low(sent[at:, :], got[at:, :])
        to += more
    if small:
        msg[to:, :] = add_low(small[0][...], small[1][...])


def fold(rows, lo, sent, got, small=(), after=()):
    total = sum(rows)
    end = sent.shape[0] - total // 2 + (small[0].shape[0] if small else 0)
    return kernel_call(
        functools.partial(fold_kernel, rows, len(small), 0),
        (((total // 2, lo.shape[1]), BF), ((end, lo.shape[1]), BF)),
        (),
        8,
        0.3,
        0,
        lo, sent, got, *small,
        after=after,
    )


def pair_fold_kernel(a_lo, a_got, b_lo, b_sent, b_got, a_sent, keep, msg):
    half_b, half_a = b_lo.shape[0] // 2, a_lo.shape[0] // 2
    both = ((b_lo, b_got, half_b, 0), (a_lo, a_got, half_a, half_b))
    for lo, got, half, to in both:
        keep[to : to + half, :] = add_low(lo[0:half, :], got[0:half, :])
        msg[to : to + half, :] = add_low(lo[half : 2 * half, :], got[half : 2 * half, :])
    msg[half_a + half_b :, :] = add_low(b_sent[2 * half_b :, :], b_got[2 * half_b :, :])


def pair_fold(a_lo, a_sent, a_got, b_lo, b_sent, b_got, after=()):
    rows, lanes = a_lo.shape
    return kernel_call(
        pair_fold_kernel,
        (((rows, lanes), BF), ((b_sent.shape[0], lanes), BF)),
        (),
        8,
        0.3,
        0,
        a_lo, a_got, b_lo, b_sent, b_got, a_sent,
        after=after,
    )


def last_fold_kernel(lo, sent, got, own, msg):
    half = lo.shape[1] // 2
    size = lo.shape[0] // 2
    rows = size // 2
    for i, at in enumerate((size, 0)):
        e, r = [
            lo[k : k + rows, :].astype(F32) + got[k : k + rows, :].astype(F32)
            for k in (at, at + rows)
        ]
        here = slice(i * rows, (i + 1) * rows)
        own[here, :] = jnp.concatenate([e[:, :half], r[:, :half]], axis=1)
        msg[here, :] = jnp.concatenate([e[:, half:], r[:, half:]], axis=1).astype(BF)
    msg[size:, :] = add_low(sent[2 * size :, :], got[2 * size :, :])


def last_fold(lo, sent, got):
    rows, lanes = lo.shape
    small = sent.shape[0] - rows
    return kernel_call(
        last_fold_kernel,
        (((rows // 2, lanes), F32), ((rows // 2 + small, lanes), BF)),
        (),
        8,
        0.3,
        0,
        lo, sent, got,
    )


def outer_kernel(chunk_at, *refs):
    if chunk_at:
        at_core, order, r_all, hid, gt, logits, b1, gl_in, xt, perm, ys, gls, gsel, acc = refs
        acc[...] = jnp.zeros_like(acc)
    else:
        at_core, r_all, hid, gt, logits, b1, ys, gls = refs
    high = at_core[0].astype(F32)
    sign = 2.0 * high - 1.0
    count, hidden, total = hid.shape
    width = gt.shape[1]
    tile = min(WIDE, total)

    @pl.loop(0, total // tile)
    def _(i):
        part = part_of(i, tile)
        gg = []
        for e in range(count):
            y = dot(r_all[:, e * hidden : (e + 1) * hidden], hid[e, :, part], 1, 0)
            at = chunk_at * count + e
            y = y + b1[:, at : at + 1]
            low = y.astype(BF)
            ys[e, :, part] = low
            sums = []
            for t in range(TASKS):
                p = None
                for d in range(0, width, 32):
                    q = gt[t, d : d + 32, part] * low[d : d + 32]
                    p = q if p is None else p + q
                sums.append(jnp.sum(p.astype(F32), axis=0, keepdims=True))
            gg.append(jnp.concatenate(sums + [jnp.zeros((TPAD - TASKS, tile), F32)], axis=0))
        gl = gate_back(
            lambda b, k: logits[(b * SELECT + k) * TPAD : (b * SELECT + k + 1) * TPAD, part],
            lambda k: logits[
                (BITS * SELECT + k) * TPAD : (BITS * SELECT + k + 1) * TPAD, part
            ],
            gg, chunk_at, high, sign,
        )
        if chunk_at:
            gl = (gl + gl_in[:, part]).astype(BF)
            acc[...] += dot(gl, xt[0:width, part], 1, 1)
        gls[:, part] = gl

    if chunk_at:
        turned = dot(order[:, 0:64], acc[...].astype(BF), 0, 0).astype(BF)
        gsel[...] = lanes_out(dot(turned, perm[...], 1, 0)).astype(BF)


def outer(chunk_at, at, r_all, hid, gt, logits, b1, order=None, more=(), after=()):
    count, _, total = hid.shape
    width = gt.shape[1]
    outs = [((count, width, total), BF), ((GROWS, total), BF if chunk_at else F32)]
    if chunk_at:
        outs.append(((order.shape[1], 128), BF))
        args = (at, order, r_all, hid, gt, logits, b1, *more)
    else:
        args = (at, r_all, hid, gt, logits, b1)
    return kernel_call(
        functools.partial(outer_kernel, chunk_at),
        tuple(outs),
        (((GROWS, width), F32),) if chunk_at else (),
        16,
        4.3,
        1,
        *args,
        after=after,
    )


def mix_kernel(start, e_a, gp_a, y_a, e_b, gp_b, y_b, selp, gls, gates, out):
    chunk, hidden, _ = gp_a.shape
    _, width, rows = out.shape
    tile, depth = 512, 16

    @pl.loop(0, rows // tile)
    def _(i):
        here, part = part_of(i, tile), part_of(i + start // tile, tile)
        v = dot(e_a[...], gp_a[:, :, part].reshape(chunk * hidden, tile), 1, 0)
        v = v + dot(e_b[...], gp_b[:, :, part].reshape(chunk * hidden, tile), 1, 0)
        out[TASKS, :, here] = (v + dot(selp[...], gls[:, part], 0, 0)).astype(BF)
        for d in range(width // depth):
            block = slice(d * depth, (d + 1) * depth)
            sums = [None] * TASKS
            for e in range(2 * chunk):
                y = (y_a if e < chunk else y_b)[e % chunk, block, part].astype(F32)
                for t in range(TASKS):
                    m = gates[e, t : t + 1, part] * y
                    sums[t] = m if e == 0 else sums[t] + m
            for t in range(TASKS):
                out[t, block, here] = sums[t].astype(BF)


def mix(start, rows, first, second, selp, gls, gates, after):
    chunk, width, total = first[2].shape
    (out,) = kernel_call(
        functools.partial(mix_kernel, start),
        (((TASKS + 1, width, rows), BF),),
        (),
        16,
        4.0,
        0,
        *first, *second, selp, gls, gates,
        after=after,
    )
    return out


def gate_back(z_of, a_of, gg, e2, high, sign):
    alpha, smooth, clipped, f_high = gate_parts(z_of, a_of, high)
    out = [None] * GROUPS
    d_alpha = []
    for k in range(SELECT):
        f = [[fac(smooth, b, k, bit) for bit in range(2)] for b in range(BITS - 1)]
        low = [f[0][0] * gg[2 * e1] + f[0][1] * gg[2 * e1 + 1] for e1 in range(2)]
        dif = [gg[2 * e1 + 1] - gg[2 * e1] for e1 in range(2)]
        mid = f[1][0] * low[0] + f[1][1] * low[1]
        t0 = f[2][e2] * mid
        d2 = mid if e2 else -mid
        d1 = f[2][e2] * (low[1] - low[0])
        d0 = f[2][e2] * (f[1][0] * dif[0] + f[1][1] * dif[1])
        d_alpha.append(f_high[k] * t0)
        scale = alpha[k] * f_high[k]
        for b, d in enumerate((scale * d0, scale * d1, scale * d2, alpha[k] * sign * t0)):
            v = clipped[b, k]
            out[b * SELECT + k] = d * (1.5 / GAMMA - 6.0 / GAMMA**3 * v * v)
    total = functools.reduce(jnp.add, [a * d for a, d in zip(alpha, d_alpha)])
    for k in range(SELECT):
        out[BITS * SELECT + k] = alpha[k] * (d_alpha[k] - total)
    return jnp.concatenate(out, axis=0)


def final_kernel(masks, at, own, recv, mixed, gf, token, buf, sems):
    token[...] = jnp.zeros_like(token)
    width = buf.shape[2]
    d_of, _ = places(masks, at, width)
    up = lax.broadcasted_iota(jnp.int32, (width, width), 0)
    across = lax.broadcasted_iota(jnp.int32, (width, width), 1)
    perm = (d_of(up) == across).astype(F32).astype(BF)
    copies = []
    for t in range(TASKS + 1):
        s = (own[t].astype(F32) + recv[t].astype(F32)).astype(BF)
        buf[t] = dot(s, perm, 0, 0).astype(BF)
        to = mixed.at[t] if t < TASKS else gf
        copies.append(pltpu.make_async_copy(buf.at[t], to, sems.at[t]))
        copies[-1].start()
    for copy in copies:
        copy.wait()


def final(masks, at, own, recv, after):
    _, width, rows = own.shape
    return kernel_call(
        functools.partial(final_kernel, masks),
        (((TASKS, rows, width), BF), ((rows, width), BF), ((8, 128), F32)),
        (((TASKS + 1, rows, width), BF),),
        16,
        0.1,
        1,
        at, own, recv,
        after=after,
        far=2,
        sems=TASKS + 1,
    )


def adamw(weight, grad, first, second):
    first = BETA_ONE * first + (1.0 - BETA_ONE) * grad
    second = BETA_TWO * second + (1.0 - BETA_TWO) * grad * grad
    mhat = first / (1.0 - BETA_ONE**STEP)
    vhat = second / (1.0 - BETA_TWO**STEP)
    weight = weight - RATE * (mhat / (jnp.sqrt(vhat) + EPSILON) + DECAY * weight)
    return (first, second, weight)


def pack_kernel(with_w, core, w_e, w_r, w_b, w_s, sel, bias, *refs):
    first = core[0] == 0
    sel[...] = jnp.zeros_like(sel)
    sel[:, 0 : w_s.shape[1]] = w_s[...].astype(BF)
    experts, lanes = w_b.shape[1:]
    for k in range(2):
        high = w_b[k].astype(BF)
        low = (w_b[k] - high.astype(F32)).astype(BF)
        bias[k * experts : (k + 1) * experts, :] = jnp.concatenate(
            [high.astype(F32), low.astype(F32)], axis=1
        ).astype(BF)
    if with_w:
        mine, other = refs
        count = experts // 2
        for e in range(count):
            for which in range(2):
                lo, hi = (
                    (w_r[e], w_r[e + count]) if which else (w_e[:, e, :], w_e[:, e + count, :])
                )
                mine[which, e] = jnp.where(first, lo, hi).astype(BF)
                other[which, e] = jnp.where(first, hi, lo).astype(BF)


def pack(core, w_e, w_r, w_b, w_s, with_w):
    experts, depth, lanes = w_r.shape
    half = (2, experts // 2, depth, lanes)
    outs = [((depth, 2 * lanes), BF), ((2 * experts, 2 * lanes), BF)]
    if with_w:
        outs += [(half, BF), (half, BF)]
    block = lambda shape: pl.BlockSpec(shape, lambda i: (0,) * len(shape))
    return pl.pallas_call(
        functools.partial(pack_kernel, with_w),
        grid=(1,),
        out_shape=tuple(jax.ShapeDtypeStruct(shape, kind) for shape, kind in outs),
        in_specs=[pl.BlockSpec(memory_space=pltpu.SMEM)]
        + [block(x.shape) for x in (w_e, w_r, w_b, w_s)],
        out_specs=tuple(block(shape) for shape, _ in outs),
        compiler_params=params(8),
    )(core, *(pltpu.with_memory_space_constraint(x, pltpu.HBM) for x in (w_e, w_r, w_b, w_s)))


def join_kernel(plan, n_in, *refs):
    ins, outs = refs[:n_in], refs[n_in:]
    for out, pieces in zip(outs, plan):
        to = 0
        for k, start, rows in pieces:
            out[to : to + rows, :] = ins[k][start : start + rows, :]
            to += rows


def join(plan, *ins, after=()):
    lanes = ins[0].shape[1]
    return kernel_call(
        functools.partial(join_kernel, plan, len(ins)),
        tuple(((sum(p[2] for p in pieces), lanes), BF) for pieces in plan),
        (),
        8,
        0.3,
        0,
        *ins,
        after=after,
    )


def chip_kernel(mine, recv, sel, a_msg, b_msg):
    _, count, depth, lanes = mine.shape
    half = count // 2
    for which in range(2):
        for e in range(count):
            msg = a_msg if e < half else b_msg
            to = (which * half + e % half) * depth
            msg[to : to + depth, :] = jnp.concatenate([mine[which, e], recv[which, e]], axis=1)
    a_msg[2 * half * depth :, :] = sel[...]


def chip_messages(mine, recv, sel):
    _, count, depth, lanes = mine.shape
    rows = count * depth
    return kernel_call(
        chip_kernel,
        (((rows + sel.shape[0], 2 * lanes), BF), ((rows, 2 * lanes), BF)),
        (),
        8,
        0.3,
        0,
        mine, recv, sel,
    )


def update_kernel(
    at, own, sent, got, w_e, m_e, v_e, w_r, m_r, v_r, w_b, m_b, v_b, w_s, m_s, v_s, *refs
):
    outs, (g_e,) = refs[:-1], refs[-1:]
    core, row, hid = at[0], at[1], at[2]
    first = core == 0
    experts, depth, lanes = w_r.shape
    count = experts // 2
    n_own = own.shape[0]
    theirs = got[0:n_own, :].astype(F32)
    halves = (jnp.where(first, own[...], theirs), jnp.where(first, theirs, own[...]))

    def store(k, new):
        for ref, value in zip(outs[3 * k : 3 * k + 3], new):
            ref[...] = value

    parts = []
    for half in halves:
        for e in range(count):
            rows = half[e * depth : (e + 1) * depth]
            g_e[:, len(parts), :] = rows[:, :lanes]
            parts.append(rows[:, lanes:])
    store(0, adamw(w_e[...], g_e[...], m_e[...], v_e[...]))
    store(1, adamw(w_r[...], jnp.stack(parts), m_r[...], v_r[...]))

    n_bias = 8 * count // 2
    small, small_got = sent[n_own:, :], got[n_own:, :]
    bias = [lanes_in(x[0:n_bias]) for x in (small, small_got)]
    width = bias[0].shape[1]
    spot = lax.broadcasted_iota(jnp.int32, (width, lanes), 0)
    lane = lax.broadcasted_iota(jnp.int32, (width, lanes), 1)
    pick = (spot == hid * lanes + lane).astype(F32).astype(BF)
    mine, other = [dot(x, pick, 1, 0) for x in bias]
    lo, hi = jnp.where(first, mine, other), jnp.where(first, other, mine)
    g_b = jnp.stack(
        [jnp.concatenate([x[k * count : (k + 1) * count] for x in (lo, hi)], axis=0) for k in range(2)]
    )
    store(2, adamw(w_b[...], g_b, m_b[...], v_b[...]))

    g_s = lanes_in(add_low(small[n_bias:], small_got[n_bias:]))
    spot = lax.broadcasted_iota(jnp.int32, (depth, width), 0)
    lane = lax.broadcasted_iota(jnp.int32, (depth, width), 1)
    pick = (lane == row * depth + spot).astype(F32).astype(BF)
    g_s = dot(pick, g_s, 1, 1)[:, : w_s.shape[1]]
    store(3, adamw(w_s[...], g_s, m_s[...], v_s[...]))


def update(at, own, sent, got, *params):
    outs = []
    for k in range(4):
        outs += [(params[3 * k].shape, F32)] * 3
    return kernel_call(
        update_kernel,
        tuple(outs),
        ((params[0].shape, F32),),
        16,
        2.4,
        1,
        at, own, sent, got, *params,
    )


def logit_order():
    order = np.zeros((GROWS, 128), np.float32)
    for t in range(TASKS):
        for k in range(SELECT):
            for b in range(BITS):
                order[(b * SELECT + k) * TPAD + t, (t * SELECT + k) * BITS + b] = 1.0
            at = (BITS * SELECT + k) * TPAD + t
            order[at, TASKS * SELECT * BITS + t * SELECT + k] = 1.0
    return order


def per_device(
    n_rows,
    n_hid,
    features,
    w_expand,
    w_reduce,
    biases,
    w_select,
    grad_mix,
    m_expand,
    v_expand,
    m_reduce,
    v_reduce,
    m_biases,
    v_biases,
    m_select,
    v_select,
):
    d_loc, experts, h_loc = w_expand.shape
    width = d_loc * n_rows
    mine_n = experts // 2
    chunk = mine_n // 2
    row = lax.axis_index("rows")
    hid_at = lax.axis_index("hid")
    core = hid_at % 2

    bits = n_rows.bit_length() - 1
    masks = [1 << b for b in range(bits)]
    side = (0, 2)
    sibling = ((0, 1), (0, 1))
    dims = [side] + [(m, 0) for m in masks]
    if n_rows == 8:
        way = ((3, 2, 0, 1), (3, 2, 1, 0))
        late_way = ((0, 3, 2, 1), (1, 3, 2, 0))
        back_way = ((2, 3, 0, 1), (1, 2, 3, 0))
    else:
        way = late_way = back_way = (tuple(range(len(dims))),) * 2

    def swap(x, hops):
        pairs = []
        for r in range(n_rows):
            for h in range(n_hid):
                mr, mh = hops[h % 2]
                pairs.append((r * n_hid + h, (r ^ mr) * n_hid + (h ^ mh)))
        return lax.ppermute(x, ("rows", "hid"), pairs)

    def hops(step):
        return tuple(dims[way[k][step]] for k in range(2))

    def late_hops(step):
        return tuple(dims[late_way[k][step]] for k in range(2))

    def back_hops(step):
        return tuple(dims[back_way[k][step]] for k in range(2))

    def table_of(pair):
        if n_rows != 8:
            return (tuple(range(16)),) * 2
        both = []
        for order in pair:
            spots = []
            for q in range(8):
                for s in range(2):
                    on = [s] + [(q >> b) & 1 for b in range(3)]
                    spots.append(sum(on[d] << order.index(d) for d in range(4)))
            both.append(tuple(spots))
        return tuple(both)

    order = jnp.asarray(logit_order(), BF)
    at = jnp.stack([core, row, hid_at]).astype(jnp.int32)

    def split_experts(x, axis):
        mine = lax.dynamic_slice_in_dim(x, core * mine_n, mine_n, axis)
        other = lax.dynamic_slice_in_dim(x, (1 - core) * mine_n, mine_n, axis)
        return mine, other

    def tie(x, *after):
        return lax.optimization_barrier((x, after))[0]

    part = n_rows // 8

    def canonical(lo, hi):
        w = jnp.concatenate([lo, hi], axis=0).reshape(8, part, 2, 2, chunk, d_loc, 2 * h_loc)
        w = jnp.transpose(w, (0, 2, 3, 4, 1, 5, 6)).reshape(2, -1, 2 * h_loc)
        return w[0], w[1]

    def uncanonical(lo, hi):
        if n_rows == 8:
            return lo, hi
        w = jnp.concatenate([lo, hi], axis=0).reshape(8, 2, 2, chunk, part, d_loc, 2 * h_loc)
        w = jnp.transpose(w, (0, 4, 1, 2, 3, 5, 6)).reshape(2, -1, 2 * h_loc)
        return w[0], w[1]

    w_r_view = jnp.transpose(w_reduce, (0, 2, 1))
    packed = pack(at, w_expand, w_r_view, biases, w_select, d_loc % 16 == 0)
    sel, b_own = packed[:2]
    if d_loc % 16 == 0:
        w_mine, w_other = packed[2:]
    else:
        w_mine, w_other = split_experts(
            jnp.stack([jnp.transpose(w_expand, (1, 0, 2)), w_r_view]).astype(BF), 1
        )
    w_recv = swap(w_other, sibling)
    n_b = b_own.shape[0]
    (b_own,) = join((((0, 0, n_b), (1, 0, n_b)),), b_own, swap(b_own, sibling))
    x_own = features
    g_own = jnp.transpose(grad_mix, (1, 0, 2))
    x_recv = swap(tie(x_own, w_recv), sibling)
    g_recv = swap(tie(g_own, w_recv), sibling)

    steps = len(dims)
    ride = n_rows == 8
    if ride:
        n = chunk * d_loc * 2
        a_msg, b_msg = chip_messages(w_mine, w_recv, sel)
        a_got = swap(a_msg, hops(0))
        (a_msg,) = join((((0, 0, n), (1, 0, n), (0, n, d_loc), (1, n, d_loc)),), a_msg, a_got)
        b_got = swap(b_msg, late_hops(0))
        a_got = swap(a_msg, hops(1))
        xt, gt, perm, to_q = turn(masks, at, x_own, x_recv, g_own, g_recv, (a_msg,))
        n *= 2
        tail = tuple((k, n, 2 * d_loc) for k in range(2)) + ((2, 0, 4 * experts),)
        (a_msg,) = join(
            (((0, 0, n), (1, 0, n)) + tail,), a_msg, a_got, b_own, after=(perm,)
        )
        a_got = swap(a_msg, hops(2))
        both = lambda x, y, after: join(
            (((0, 0, x.shape[0]), (1, 0, x.shape[0])),), x, y, after=after
        )[0]
        b_msg = both(b_msg, b_got, (a_msg,))
        b_got = swap(b_msg, late_hops(1))
        n *= 2
        a_lo, riders = join(
            (
                ((0, 0, n), (1, 0, n)),
                ((0, n, 4 * d_loc), (1, n, 4 * d_loc), (1, n + 4 * d_loc, 4 * experts)),
            ),
            a_msg, a_got,
        )
        a_hi = swap(a_lo, hops(3))
        turned = swap(riders, sibling)
        b_msg = both(b_msg, b_got, (a_lo,))
        b_got = swap(b_msg, late_hops(2))
    else:
        xt, gt, perm, to_q = turn(masks, at, x_own, x_recv, g_own, g_recv, (sel,))
        chip = jnp.concatenate([w_mine, w_recv], axis=3)
        bufs = [chip[None, :, :chunk], chip[None, :, chunk:]]
        for step in range(steps):
            gots = [swap(buf, hops(step)) for buf in bufs]
            if step + 1 < steps:
                bufs = [jnp.concatenate(pair, axis=0) for pair in zip(bufs, gots)]
        for m in masks:
            sel = jnp.concatenate([sel, swap(sel, ((m, 0), (m, 0)))], axis=0)
        riders = turned = jnp.concatenate([sel, swap(b_own, (side, side))], axis=0)
        (a_lo, a_hi), (b_lo, b_hi) = [canonical(*pair) for pair in zip(bufs, gots)]

    cc_a, gates, logits, selp, gb1_a, b0, b1 = prep(
        masks, ride, at, order, riders, turned, b_own, xt, gt
    )

    spots, back = table_of(way), table_of(back_way)
    cc_b, gb1_b = late(gates, gt, (b0,))
    if ride:
        b_lo = both(b_msg, b_got, (gb1_b,))
        b_hi = swap(b_lo, late_hops(3))
    first = critical(spots, back, at, a_lo, a_hi, xt, cc_a, b0, (b_lo,))
    a_lo, a_msg = uncanonical(first[0], first[1])
    a_got = swap(a_msg, back_hops(steps - 1))
    second = critical(
        table_of(late_way), back, at, b_lo, b_hi, xt, cc_b, b0, (first[0],), (first[6], gb1_a, gb1_b, to_q, perm)
    )
    b_lo, b_msg = second[:2]
    if not ride:
        n = b_lo.shape[0]
        b_lo, b_msg = uncanonical(b_lo, b_msg[:n])
        b_msg = jnp.concatenate([b_msg, second[1][n:]], axis=0)
    b_got = swap(b_msg, back_hops(steps - 1))
    ys_a, gl_a = outer(0, at, first[5], first[2], gt, logits, b1, after=(second[0],))
    a_lo, a_msg = fold(a_lo.shape[:1], a_lo, a_msg, a_got, after=(gl_a,))
    a_got = swap(a_msg, back_hops(steps - 2))
    ys_b, gls, gsel = outer(
        1, at, second[5], second[2], gt, logits, b1, order, (gl_a, xt, perm), (a_lo,)
    )
    gsel_got = swap(gsel, back_hops(steps - 1))
    a_lo, a_msg = fold(a_lo.shape[:1], a_lo, a_msg, a_got, after=(gsel,))
    a_got = swap(a_msg, back_hops(steps - 3))
    b_lo, b_msg = fold(b_lo.shape[:1], b_lo, b_msg, b_got, (gsel, gsel_got), (a_lo,))
    b_got = swap(b_msg, back_hops(steps - 2))
    ends = ((first[4], first[3], ys_a), (second[4], second[3], ys_b))
    n_own = x_own.shape[0]
    mix_other = mix(n_own, n_own, *ends, selp, gls, gates, (a_lo, b_lo))
    mix_recv = swap(mix_other, sibling)
    b_lo, b_msg = fold(b_lo.shape[:1], b_lo, b_msg, b_got, after=(mix_other,))
    b_got = swap(b_msg, back_hops(steps - 3))
    mix_own = mix(0, n_own, *ends, selp, gls, gates, (b_lo,))
    mixed, grad_features, token = final(masks, at, mix_own, mix_recv, (b_lo,))
    for step in reversed(range(1, steps - 3)):
        a_lo, a_msg = fold(a_lo.shape[:1], a_lo, a_msg, a_got)
        b_lo, b_msg = fold(b_lo.shape[:1], b_lo, b_msg, b_got)
        a_got, b_got = swap(a_msg, back_hops(step)), swap(b_msg, back_hops(step))
    lo, msg = pair_fold(a_lo, a_msg, a_got, b_lo, b_msg, b_got, (token,))
    got = swap(msg, back_hops(0))
    own, msg = last_fold(lo, msg, got)
    got = swap(msg, sibling)
    mixed = jnp.transpose(mixed, (1, 0, 2))

    flip = lambda x: jnp.transpose(x, (0, 2, 1))
    new = list(
        update(
            at, own, msg, got,
            w_expand, m_expand, v_expand,
            w_r_view, flip(m_reduce), flip(v_reduce),
            biases, m_biases, v_biases,
            w_select, m_select, v_select,
        )
    )
    new[3:6] = [flip(x) for x in new[3:6]]
    return (mixed, grad_features, *new)


def solution(mesh):
    row_split = P(("rows", "hid"), None)
    task_split = P(("rows", "hid"), None, None)
    expand = P("rows", None, "hid")
    reduce = P(None, "hid", "rows")
    bias = P(None, None, "hid")
    select = P("rows", None)
    return jax.shard_map(
        functools.partial(per_device, mesh.shape["rows"], mesh.shape["hid"]),
        mesh=mesh,
        in_specs=(
            row_split, expand, reduce, bias, select, task_split,
            expand, expand, reduce, reduce, bias, bias, select, select,
        ),
        out_specs=(
            task_split, row_split,
            expand, expand, expand,
            reduce, reduce, reduce,
            bias, bias, bias,
            select, select, select,
        ),
        check_vma=False,
    )
```

```python
import functools

import jax
import jax.numpy as jnp
import numpy as np
from jax import lax
from jax.experimental import pallas as pl
from jax.experimental.pallas import tpu as pltpu
from jax.sharding import PartitionSpec as P

TASKS = 3
SELECT = 4
BITS = 4
STEP = 5
GAMMA = 2.0
RATE = 0.05
DECAY = 0.01
EPSILON = 1e-08
BETA_ONE = 0.5
BETA_TWO = 0.5

BF = jnp.bfloat16
F32 = jnp.float32
HIGHEST = lax.Precision.HIGHEST
TPAD = 8
GROUPS = BITS * SELECT + SELECT
GROWS = GROUPS * TPAD
ONES = 16
TILE = 256
WIDE = 1024
MIB = 1 << 20
FLOPS_MICRO = 1.2e10


def dot(a, b, ca, cb, precision=None):
    return lax.dot_general(
        a, b, (((ca,), (cb,)), ((), ())), preferred_element_type=F32, precision=precision
    )


def params(mib):
    return pltpu.CompilerParams(vmem_limit_bytes=mib * MIB)


def kernel_call(body, outs, scratch, mib, micros, smem, *args, after=(), far=0, sems=0):
    in_vmem = pl.BlockSpec(memory_space=pltpu.VMEM)
    in_smem = pl.BlockSpec(memory_space=pltpu.SMEM)
    anywhere = pl.BlockSpec(memory_space=pl.ANY)
    n_in, n_after = len(args), len(after)

    def kernel(*refs):
        body(*refs[:n_in], *refs[n_in + n_after :])

    return pl.pallas_call(
        kernel,
        out_shape=tuple(jax.ShapeDtypeStruct(shape, kind) for shape, kind in outs),
        in_specs=[in_smem] * smem + [in_vmem] * (len(args) - smem) + [anywhere] * len(after),
        out_specs=(anywhere,) * far + (in_vmem,) * (len(outs) - far),
        scratch_shapes=[pltpu.VMEM(shape, kind) for shape, kind in scratch]
        + ([pltpu.SemaphoreType.DMA((sems or far,))] if far else []),
        compiler_params=params(mib),
        cost_estimate=pl.CostEstimate(
            flops=int(micros * FLOPS_MICRO), bytes_accessed=0, transcendentals=0
        ),
    )(*args, *after)


def gate_parts(z_of, a_of, high):
    smooth, clipped = {}, {}
    for k in range(SELECT):
        for b in range(BITS):
            v = jnp.clip(z_of(b, k), -0.5 * GAMMA, 0.5 * GAMMA)
            clipped[b, k] = v
            smooth[b, k] = v * (1.5 / GAMMA - 2.0 / GAMMA**3 * v * v) + 0.5
    a = [a_of(k) for k in range(SELECT)]
    top = functools.reduce(jnp.maximum, a)
    ex = [jnp.exp(v - top) for v in a]
    inv = 1.0 / functools.reduce(jnp.add, ex)
    alpha = [v * inv for v in ex]
    last = BITS - 1
    f_high = [
        high * smooth[last, k] + (1.0 - high) * (1.0 - smooth[last, k]) for k in range(SELECT)
    ]
    return alpha, smooth, clipped, f_high


def fac(smooth, b, k, bit):
    return smooth[b, k] if bit else 1.0 - smooth[b, k]


def part_of(i, tile):
    return pl.ds(pl.multiple_of(i * tile, tile), tile)


def places(masks, at, width):
    row, hid = at[1], at[2]
    depth = width // (1 << len(masks))

    def d_of(spot):
        block, out = spot // depth, row
        for b, m in enumerate(masks):
            out = out ^ (((block >> b) & 1) * m)
        return out * depth + spot % depth

    def q_of(spot):
        lanes = width // 4
        return (hid ^ (spot // lanes)) * lanes + spot % lanes

    return d_of, q_of


def turn_kernel(masks, at, xo, xr, go, gr, xt, gt, perm, to_q):
    rows, width = xo.shape
    d_of, q_of = places(masks, at, width)
    up = lax.broadcasted_iota(jnp.int32, (width, width), 0)
    across = lax.broadcasted_iota(jnp.int32, (width, width), 1)
    perm[...] = (d_of(up) == across).astype(F32).astype(BF)
    to_q[...] = (q_of(up) == across).astype(F32).astype(BF)
    xt[width : width + ONES, :] = jnp.ones((ONES, xt.shape[1]), BF)
    tile = min(WIDE, rows)
    for x, g, start in ((xo, go, 0), (xr, gr, rows)):
        for i in range(rows // tile):
            here = slice(i * tile, (i + 1) * tile)
            out = slice(start + i * tile, start + (i + 1) * tile)
            xt[0:width, out] = dot(perm[...], x[here, :], 1, 1).astype(BF)
            for t in range(TASKS):
                gt[t, :, out] = dot(perm[...], g[t, here, :], 1, 1).astype(BF)


def turn(masks, at, x_own, x_recv, g_own, g_recv, after):
    rows, width = x_own.shape
    total = 2 * rows
    return kernel_call(
        functools.partial(turn_kernel, masks),
        (
            ((width + ONES, total), BF),
            ((TASKS, width, total), BF),
            ((width, width), BF),
            ((width, width), BF),
        ),
        (),
        12,
        3.5,
        1,
        at, x_own, x_recv, g_own, g_recv,
        after=after,
    )


def prep_kernel(
    masks, ride, at, order, riders, turned, b_own, xt, gt,
    cc_a, gates, logits, selp, gb1, b0, b1, sel,
):
    core = at[0]
    high = core.astype(F32)
    _, width, total = gt.shape
    tile = min(WIDE, total)
    d_of, q_of = places(masks, at, width)
    up = lax.broadcasted_iota(jnp.int32, (width, width), 0)
    across = lax.broadcasted_iota(jnp.int32, (width, width), 1)
    one = lambda same: same.astype(F32)
    n_b = b_own.shape[0] // 2
    if ride:
        depth = width // 8
        for q in range(8):
            spot = (q >> 2) + 2 * (q >> 1 & 1) + 4 * (q & 1)
            rows = slice(spot * depth, (spot + 1) * depth)
            sel[q * depth : (q + 1) * depth, :] = jnp.where(core == 1, riders[rows, :], turned[rows, :])
        side = [
            jnp.where(
                core == 0,
                riders[width + k * n_b : width + (k + 1) * n_b, :],
                turned[width + (1 - k) * n_b : width + (2 - k) * n_b, :],
            )
            for k in range(2)
        ]
    else:
        sel[...] = riders[0:width, :]
        side = [riders[width + k * n_b : width + (k + 1) * n_b, :] for k in range(2)]
    pieces = []
    for block in [b_own[k * n_b : (k + 1) * n_b, :] for k in range(2)] + side:
        block = block.astype(F32)
        pieces.append(block[:, : width // 4] + block[:, width // 4 :])
    take = lambda x, k: jnp.where(core == 0, x[16 * k : 16 * k + 8], x[16 * k + 8 : 16 * k + 16])
    bias = [jnp.concatenate([take(x, k) for x in pieces], axis=1) for k in range(2)]
    b0[...] = dot(one(up == across), 0.5 * bias[0], 1, 1, HIGHEST)
    b1[...] = dot(one(d_of(up) == q_of(across)), bias[1], 1, 1, HIGHEST)
    selp[...] = dot(order[...], sel[...], 1, 1).astype(BF)
    gb1[...] = jnp.zeros_like(gb1)

    @pl.loop(0, total // tile)
    def _(i):
        part = part_of(i, tile)
        lg = dot(selp[...], xt[0:width, part], 1, 0)
        logits[:, part] = lg

        def z_of(b, k):
            at = (b * SELECT + k) * TPAD
            return lg[at : at + TPAD]

        def a_of(k):
            at = (BITS * SELECT + k) * TPAD
            return lg[at : at + TPAD]

        alpha, smooth, _, f_high = gate_parts(z_of, a_of, high)
        gate = [None] * 8
        for k in range(SELECT):
            base = alpha[k] * f_high[k]
            for e2 in range(2):
                w2 = base * fac(smooth, 2, k, e2)
                for e1 in range(2):
                    w1 = w2 * fac(smooth, 1, k, e1)
                    for e0 in range(2):
                        e = 4 * e2 + 2 * e1 + e0
                        w0 = w1 * fac(smooth, 0, k, e0)
                        gate[e] = w0 if gate[e] is None else gate[e] + w0
        for e in range(8):
            gates[e, :, part] = gate[e]
        combine(gate[0:4], gt, part, cc_a, gb1)


def combine(gate, gt, part, cc, gb1):
    ones = jnp.ones((8, part.size), BF)
    low = [[g[t : t + 1].astype(BF) for t in range(TASKS)] for g in gate]
    for e in range(4):
        c = low[e][0] * gt[0, :, part]
        for t in range(1, TASKS):
            c = c + low[e][t] * gt[t, :, part]
        cc[e, :, part] = c
        gb1[e] += dot(ones, c, 1, 1)


def late_kernel(gates, gt, cc, gb1):
    total = gt.shape[2]
    tile = min(WIDE, total)
    gb1[...] = jnp.zeros_like(gb1)

    @pl.loop(0, total // tile)
    def _(i):
        part = part_of(i, tile)
        combine([gates[4 + e, :, part] for e in range(4)], gt, part, cc, gb1)


def late(gates, gt, after):
    _, width, total = gt.shape
    return kernel_call(
        late_kernel,
        (((4, width, total), BF), ((4, 8, width), F32)),
        (),
        12,
        2.0,
        0,
        gates, gt,
        after=after,
    )


def prep(masks, ride, at, order, riders, turned, b_own, xt, gt):
    _, width, total = gt.shape
    return kernel_call(
        functools.partial(prep_kernel, masks, ride),
        (
            ((4, width, total), BF),
            ((8, TPAD, total), F32),
            ((GROWS, total), F32),
            ((GROWS, width), BF),
            ((4, 8, width), F32),
            ((width, 8), F32),
            ((width, 8), F32),
        ),
        (((width, 128), BF),),
        14,
        5.0,
        1,
        at, order, riders, turned, b_own, xt, gt,
    )


def lanes_out(x):
    return jnp.concatenate([x[:, :128], x[:, 128:]], axis=0)


def lanes_in(x):
    rows = x.shape[0] // 2
    return jnp.concatenate([x[:rows], x[rows:]], axis=1)


def critical_kernel(second, spots, back, *refs):
    if second:
        (at_core, w_lo, w_hi, xt, cc, b0, gb0_a, gb1_a, gb1_b, to_q, perm,
         g_lo, g_hi, hid, gp, e_all, r_all, acc_e, acc_r) = refs
    else:
        (at_core, w_lo, w_hi, xt, cc, b0,
         g_lo, g_hi, hid, gp, e_all, r_all, gb0, acc_e, acc_r) = refs
    core = at_core[0]
    chunk, width, total = cc.shape
    lanes = w_lo.shape[1]
    hidden = 2 * lanes
    blocks = 8
    depth = width // blocks
    first = chunk if second else 0

    def each_block(table, lo, hi, visit):
        for q in range(blocks):
            for side in range(2):
                at = jnp.where(core == 0, table[0][2 * q + side], table[1][2 * q + side])
                rows = slice(q * depth, (q + 1) * depth)

                def cols(e, side=side):
                    return slice(e * hidden + side * lanes, e * hidden + (side + 1) * lanes)

                @pl.when(at < blocks)
                def _():
                    visit(lo, at, rows, cols)

                @pl.when(at >= blocks)
                def _():
                    visit(hi, at - blocks, rows, cols)

    def unpack(ref, at, rows, cols):
        for e in range(chunk):
            for which, out in ((0, e_all), (1, r_all)):
                spot = pl.multiple_of(((at * 2 + which) * chunk + e) * depth, depth)
                out[rows, cols(e)] = ref[pl.ds(spot, depth), :]

    each_block(spots, w_lo, w_hi, unpack)

    e_t = [(e_all[:, e * hidden : (e + 1) * hidden] * 0.5).T for e in range(chunk)]
    r = [(r_all[:, e * hidden : (e + 1) * hidden] * 0.5).T for e in range(chunk)]
    parts = [slice(i, i + TILE) for i in range(0, total, TILE)]

    def products(e, part):
        return dot(e_t[e], xt[0:width, part], 1, 0), dot(r[e], cc[e, :, part], 1, 0)

    def finish(e, part, u, gh):
        u = u + b0[:, first + e : first + e + 1]
        t = jnp.tanh(u)
        plus = 1.0 + t
        h = u * plus
        hid[e, :, part] = h.astype(BF)
        gp[e, :, part] = (gh * (plus + h * (1.0 - t))).astype(BF)
        if part is parts[-1]:
            cols = slice(e * hidden, (e + 1) * hidden)
            acc_e[:, cols] = dot(xt[...], gp[e], 1, 1)
            acc_r[:, cols] = dot(cc[e], hid[e], 1, 1)

    held = None
    for e in range(chunk):
        for part in parts:
            ready = (e, part, *products(e, part))
            if held:
                finish(*held)
            held = ready
    finish(*held)
    sums = [acc_e[width : width + 1, e * hidden : (e + 1) * hidden] for e in range(chunk)]

    def pack(ref, at, rows, cols):
        for e in range(chunk):
            ref[pl.ds(pl.multiple_of((at * 2 * chunk + e) * depth, depth), depth), :] = acc_e[
                rows, cols(e)
            ].astype(BF)
            ref[
                pl.ds(pl.multiple_of(((at * 2 + 1) * chunk + e) * depth, depth), depth), :
            ] = acc_r[rows, cols(e)].astype(BF)

    each_block(back, g_lo, g_hi, pack)
    sums = jnp.concatenate(sums, axis=0)
    if second:
        mine = jnp.concatenate([gb0_a[...], sums], axis=0).astype(BF)
        outer = jnp.concatenate(
            [x[e, 0:1] for x in (gb1_a, gb1_b) for e in range(chunk)], axis=0
        ).astype(BF)
        both = jnp.concatenate(
            [dot(mine, to_q[...], 1, 0), dot(outer, perm[...], 1, 0)], axis=0
        ).astype(BF)
        g_hi[2 * chunk * width :, :] = lanes_out(both)
    else:
        gb0[...] = sums


def critical(spots, back, at, w_lo, w_hi, xt, cc, b0, after, more=None):
    chunk, width, total = cc.shape
    rows, lanes = w_lo.shape
    hidden = 2 * lanes
    outs = [
        ((rows, lanes), BF),
        ((rows + (8 * chunk if more else 0), lanes), BF),
        ((chunk, hidden, total), BF),
        ((chunk, hidden, total), BF),
        ((width, chunk * hidden), BF),
        ((width, chunk * hidden), BF),
    ]
    if not more:
        outs.append(((chunk, hidden), F32))
    return kernel_call(
        functools.partial(critical_kernel, more is not None, spots, back),
        tuple(outs),
        (((width + ONES, chunk * hidden), F32), ((width, chunk * hidden), F32)),
        16,
        7.6,
        1,
        at, w_lo, w_hi, xt, cc, b0, *(more or ()),
        after=after,
    )


def add_low(a, b):
    return (a.astype(F32) + b.astype(F32)).astype(BF)


def fold_kernel(rows, n_small, n_tail, lo, sent, got, *refs):
    small, tail, (keep, msg) = refs[:n_small], refs[n_small : n_small + n_tail], refs[-2:]
    at = to = 0
    for size in rows:
        half = size // 2
        keep[to : to + half, :] = add_low(lo[at : at + half, :], got[at : at + half, :])
        msg[to : to + half, :] = add_low(lo[at + half : at + size, :], got[at + half : at + size, :])
        at, to = at + size, to + half
    more = sent.shape[0] - at
    if more:
        msg[to : to + more, :] = add_low(sent[at:, :], got[at:, :])
        to += more
    if small:
        msg[to:, :] = add_low(small[0][...], small[1][...])


def fold(rows, lo, sent, got, small=(), after=()):
    total = sum(rows)
    end = sent.shape[0] - total // 2 + (small[0].shape[0] if small else 0)
    return kernel_call(
        functools.partial(fold_kernel, rows, len(small), 0),
        (((total // 2, lo.shape[1]), BF), ((end, lo.shape[1]), BF)),
        (),
        8,
        0.3,
        0,
        lo, sent, got, *small,
        after=after,
    )


def pair_fold_kernel(a_lo, a_got, b_lo, b_sent, b_got, a_sent, keep, msg):
    half_b, half_a = b_lo.shape[0] // 2, a_lo.shape[0] // 2
    both = ((b_lo, b_got, half_b, 0), (a_lo, a_got, half_a, half_b))
    for lo, got, half, to in both:
        keep[to : to + half, :] = add_low(lo[0:half, :], got[0:half, :])
        msg[to : to + half, :] = add_low(lo[half : 2 * half, :], got[half : 2 * half, :])
    msg[half_a + half_b :, :] = add_low(b_sent[2 * half_b :, :], b_got[2 * half_b :, :])


def pair_fold(a_lo, a_sent, a_got, b_lo, b_sent, b_got, after=()):
    rows, lanes = a_lo.shape
    return kernel_call(
        pair_fold_kernel,
        (((rows, lanes), BF), ((b_sent.shape[0], lanes), BF)),
        (),
        8,
        0.3,
        0,
        a_lo, a_got, b_lo, b_sent, b_got, a_sent,
        after=after,
    )


def last_fold_kernel(lo, sent, got, own, msg):
    half = lo.shape[1] // 2
    size = lo.shape[0] // 2
    rows = size // 2
    for i, at in enumerate((size, 0)):
        e, r = [
            lo[k : k + rows, :].astype(F32) + got[k : k + rows, :].astype(F32)
            for k in (at, at + rows)
        ]
        here = slice(i * rows, (i + 1) * rows)
        own[here, :] = jnp.concatenate([e[:, :half], r[:, :half]], axis=1)
        msg[here, :] = jnp.concatenate([e[:, half:], r[:, half:]], axis=1).astype(BF)
    msg[size:, :] = add_low(sent[2 * size :, :], got[2 * size :, :])


def last_fold(lo, sent, got):
    rows, lanes = lo.shape
    small = sent.shape[0] - rows
    return kernel_call(
        last_fold_kernel,
        (((rows // 2, lanes), F32), ((rows // 2 + small, lanes), BF)),
        (),
        8,
        0.3,
        0,
        lo, sent, got,
    )


def outer_kernel(chunk_at, *refs):
    if chunk_at:
        at_core, order, r_all, hid, gt, logits, b1, gl_in, xt, perm, ys, gls, gsel, acc = refs
        acc[...] = jnp.zeros_like(acc)
    else:
        at_core, r_all, hid, gt, logits, b1, ys, gls = refs
    high = at_core[0].astype(F32)
    sign = 2.0 * high - 1.0
    count, hidden, total = hid.shape
    width = gt.shape[1]
    tile = min(WIDE, total)

    @pl.loop(0, total // tile)
    def _(i):
        part = part_of(i, tile)
        gg = []
        for e in range(count):
            y = dot(r_all[:, e * hidden : (e + 1) * hidden], hid[e, :, part], 1, 0)
            at = chunk_at * count + e
            y = y + b1[:, at : at + 1]
            low = y.astype(BF)
            ys[e, :, part] = low
            sums = []
            for t in range(TASKS):
                p = None
                for d in range(0, width, 32):
                    q = gt[t, d : d + 32, part] * low[d : d + 32]
                    p = q if p is None else p + q
                sums.append(jnp.sum(p.astype(F32), axis=0, keepdims=True))
            gg.append(jnp.concatenate(sums + [jnp.zeros((TPAD - TASKS, tile), F32)], axis=0))
        gl = gate_back(
            lambda b, k: logits[(b * SELECT + k) * TPAD : (b * SELECT + k + 1) * TPAD, part],
            lambda k: logits[
                (BITS * SELECT + k) * TPAD : (BITS * SELECT + k + 1) * TPAD, part
            ],
            gg, chunk_at, high, sign,
        )
        if chunk_at:
            gl = (gl + gl_in[:, part]).astype(BF)
            acc[...] += dot(gl, xt[0:width, part], 1, 1)
        gls[:, part] = gl

    if chunk_at:
        turned = dot(order[:, 0:64], acc[...].astype(BF), 0, 0).astype(BF)
        gsel[...] = lanes_out(dot(turned, perm[...], 1, 0)).astype(BF)


def outer(chunk_at, at, r_all, hid, gt, logits, b1, order=None, more=(), after=()):
    count, _, total = hid.shape
    width = gt.shape[1]
    outs = [((count, width, total), BF), ((GROWS, total), BF if chunk_at else F32)]
    if chunk_at:
        outs.append(((order.shape[1], 128), BF))
        args = (at, order, r_all, hid, gt, logits, b1, *more)
    else:
        args = (at, r_all, hid, gt, logits, b1)
    return kernel_call(
        functools.partial(outer_kernel, chunk_at),
        tuple(outs),
        (((GROWS, width), F32),) if chunk_at else (),
        16,
        4.3,
        1,
        *args,
        after=after,
    )


def mix_kernel(start, e_a, gp_a, y_a, e_b, gp_b, y_b, selp, gls, gates, out):
    chunk, hidden, _ = gp_a.shape
    _, width, rows = out.shape
    tile, depth = 512, 16

    @pl.loop(0, rows // tile)
    def _(i):
        here, part = part_of(i, tile), part_of(i + start // tile, tile)
        v = dot(e_a[...], gp_a[:, :, part].reshape(chunk * hidden, tile), 1, 0)
        v = v + dot(e_b[...], gp_b[:, :, part].reshape(chunk * hidden, tile), 1, 0)
        out[TASKS, :, here] = (v + dot(selp[...], gls[:, part], 0, 0)).astype(BF)
        for d in range(width // depth):
            block = slice(d * depth, (d + 1) * depth)
            sums = [None] * TASKS
            for e in range(2 * chunk):
                y = (y_a if e < chunk else y_b)[e % chunk, block, part]
                for t in range(TASKS):
                    m = gates[e, t : t + 1, part].astype(BF) * y
                    sums[t] = m if e == 0 else sums[t] + m
            for t in range(TASKS):
                out[t, block, here] = sums[t]


def mix(start, rows, first, second, selp, gls, gates, after):
    chunk, width, total = first[2].shape
    (out,) = kernel_call(
        functools.partial(mix_kernel, start),
        (((TASKS + 1, width, rows), BF),),
        (),
        16,
        4.0,
        0,
        *first, *second, selp, gls, gates,
        after=after,
    )
    return out


def gate_back(z_of, a_of, gg, e2, high, sign):
    alpha, smooth, clipped, f_high = gate_parts(z_of, a_of, high)
    out = [None] * GROUPS
    d_alpha = []
    for k in range(SELECT):
        f = [[fac(smooth, b, k, bit) for bit in range(2)] for b in range(BITS - 1)]
        low = [f[0][0] * gg[2 * e1] + f[0][1] * gg[2 * e1 + 1] for e1 in range(2)]
        dif = [gg[2 * e1 + 1] - gg[2 * e1] for e1 in range(2)]
        mid = f[1][0] * low[0] + f[1][1] * low[1]
        t0 = f[2][e2] * mid
        d2 = mid if e2 else -mid
        d1 = f[2][e2] * (low[1] - low[0])
        d0 = f[2][e2] * (f[1][0] * dif[0] + f[1][1] * dif[1])
        d_alpha.append(f_high[k] * t0)
        scale = alpha[k] * f_high[k]
        for b, d in enumerate((scale * d0, scale * d1, scale * d2, alpha[k] * sign * t0)):
            v = clipped[b, k]
            out[b * SELECT + k] = d * (1.5 / GAMMA - 6.0 / GAMMA**3 * v * v)
    total = functools.reduce(jnp.add, [a * d for a, d in zip(alpha, d_alpha)])
    for k in range(SELECT):
        out[BITS * SELECT + k] = alpha[k] * (d_alpha[k] - total)
    return jnp.concatenate(out, axis=0)


def final_kernel(masks, at, own, recv, mixed, gf, token, buf, sems):
    token[...] = jnp.zeros_like(token)
    width = buf.shape[2]
    d_of, _ = places(masks, at, width)
    up = lax.broadcasted_iota(jnp.int32, (width, width), 0)
    across = lax.broadcasted_iota(jnp.int32, (width, width), 1)
    perm = (d_of(up) == across).astype(F32).astype(BF)
    copies = []
    for t in range(TASKS + 1):
        s = (own[t].astype(F32) + recv[t].astype(F32)).astype(BF)
        buf[t] = dot(s, perm, 0, 0).astype(BF)
        to = mixed.at[t] if t < TASKS else gf
        copies.append(pltpu.make_async_copy(buf.at[t], to, sems.at[t]))
        copies[-1].start()
    for copy in copies:
        copy.wait()


def final(masks, at, own, recv, after):
    _, width, rows = own.shape
    return kernel_call(
        functools.partial(final_kernel, masks),
        (((TASKS, rows, width), BF), ((rows, width), BF), ((8, 128), F32)),
        (((TASKS + 1, rows, width), BF),),
        16,
        0.1,
        1,
        at, own, recv,
        after=after,
        far=2,
        sems=TASKS + 1,
    )


def adamw(weight, grad, first, second):
    first = BETA_ONE * first + (1.0 - BETA_ONE) * grad
    second = BETA_TWO * second + (1.0 - BETA_TWO) * grad * grad
    mhat = first / (1.0 - BETA_ONE**STEP)
    vhat = second / (1.0 - BETA_TWO**STEP)
    weight = weight - RATE * (mhat / (jnp.sqrt(vhat) + EPSILON) + DECAY * weight)
    return (first, second, weight)


def pack_kernel(with_w, core, w_e, w_r, w_b, w_s, sel, bias, *refs):
    first = core[0] == 0
    sel[...] = jnp.zeros_like(sel)
    sel[:, 0 : w_s.shape[1]] = w_s[...].astype(BF)
    experts, lanes = w_b.shape[1:]
    for k in range(2):
        high = w_b[k].astype(BF)
        low = (w_b[k] - high.astype(F32)).astype(BF)
        bias[k * experts : (k + 1) * experts, :] = jnp.concatenate(
            [high.astype(F32), low.astype(F32)], axis=1
        ).astype(BF)
    if with_w:
        mine, other = refs
        count = experts // 2
        for e in range(count):
            for which in range(2):
                lo, hi = (
                    (w_r[e], w_r[e + count]) if which else (w_e[:, e, :], w_e[:, e + count, :])
                )
                mine[which, e] = jnp.where(first, lo, hi).astype(BF)
                other[which, e] = jnp.where(first, hi, lo).astype(BF)


def pack(core, w_e, w_r, w_b, w_s, with_w):
    experts, depth, lanes = w_r.shape
    half = (2, experts // 2, depth, lanes)
    outs = [((depth, 2 * lanes), BF), ((2 * experts, 2 * lanes), BF)]
    if with_w:
        outs += [(half, BF), (half, BF)]
    block = lambda shape: pl.BlockSpec(shape, lambda i: (0,) * len(shape))
    return pl.pallas_call(
        functools.partial(pack_kernel, with_w),
        grid=(1,),
        out_shape=tuple(jax.ShapeDtypeStruct(shape, kind) for shape, kind in outs),
        in_specs=[pl.BlockSpec(memory_space=pltpu.SMEM)]
        + [block(x.shape) for x in (w_e, w_r, w_b, w_s)],
        out_specs=tuple(block(shape) for shape, _ in outs),
        compiler_params=params(8),
    )(core, *(pltpu.with_memory_space_constraint(x, pltpu.HBM) for x in (w_e, w_r, w_b, w_s)))


def join_kernel(plan, n_in, *refs):
    ins, outs = refs[:n_in], refs[n_in:]
    for out, pieces in zip(outs, plan):
        to = 0
        for k, start, rows in pieces:
            out[to : to + rows, :] = ins[k][start : start + rows, :]
            to += rows


def join(plan, *ins, after=()):
    lanes = ins[0].shape[1]
    return kernel_call(
        functools.partial(join_kernel, plan, len(ins)),
        tuple(((sum(p[2] for p in pieces), lanes), BF) for pieces in plan),
        (),
        8,
        0.3,
        0,
        *ins,
        after=after,
    )


def chip_kernel(mine, recv, sel, a_msg, b_msg):
    _, count, depth, lanes = mine.shape
    half = count // 2
    for which in range(2):
        for e in range(count):
            msg = a_msg if e < half else b_msg
            to = (which * half + e % half) * depth
            msg[to : to + depth, :] = jnp.concatenate([mine[which, e], recv[which, e]], axis=1)
    a_msg[2 * half * depth :, :] = sel[...]


def chip_messages(mine, recv, sel):
    _, count, depth, lanes = mine.shape
    rows = count * depth
    return kernel_call(
        chip_kernel,
        (((rows + sel.shape[0], 2 * lanes), BF), ((rows, 2 * lanes), BF)),
        (),
        8,
        0.3,
        0,
        mine, recv, sel,
    )


def update_kernel(
    at, own, sent, got, w_e, m_e, v_e, w_r, m_r, v_r, w_b, m_b, v_b, w_s, m_s, v_s, *refs
):
    outs, (g_e,) = refs[:-1], refs[-1:]
    core, row, hid = at[0], at[1], at[2]
    first = core == 0
    experts, depth, lanes = w_r.shape
    count = experts // 2
    n_own = own.shape[0]
    theirs = got[0:n_own, :].astype(F32)
    halves = (jnp.where(first, own[...], theirs), jnp.where(first, theirs, own[...]))

    def store(k, new):
        for ref, value in zip(outs[3 * k : 3 * k + 3], new):
            ref[...] = value

    parts = []
    for half in halves:
        for e in range(count):
            rows = half[e * depth : (e + 1) * depth]
            g_e[:, len(parts), :] = rows[:, :lanes]
            parts.append(rows[:, lanes:])
    store(0, adamw(w_e[...], g_e[...], m_e[...], v_e[...]))
    store(1, adamw(w_r[...], jnp.stack(parts), m_r[...], v_r[...]))

    n_bias = 8 * count // 2
    small, small_got = sent[n_own:, :], got[n_own:, :]
    bias = [lanes_in(x[0:n_bias]) for x in (small, small_got)]
    width = bias[0].shape[1]
    spot = lax.broadcasted_iota(jnp.int32, (width, lanes), 0)
    lane = lax.broadcasted_iota(jnp.int32, (width, lanes), 1)
    pick = (spot == hid * lanes + lane).astype(F32).astype(BF)
    mine, other = [dot(x, pick, 1, 0) for x in bias]
    lo, hi = jnp.where(first, mine, other), jnp.where(first, other, mine)
    g_b = jnp.stack(
        [jnp.concatenate([x[k * count : (k + 1) * count] for x in (lo, hi)], axis=0) for k in range(2)]
    )
    store(2, adamw(w_b[...], g_b, m_b[...], v_b[...]))

    g_s = lanes_in(add_low(small[n_bias:], small_got[n_bias:]))
    spot = lax.broadcasted_iota(jnp.int32, (depth, width), 0)
    lane = lax.broadcasted_iota(jnp.int32, (depth, width), 1)
    pick = (lane == row * depth + spot).astype(F32).astype(BF)
    g_s = dot(pick, g_s, 1, 1)[:, : w_s.shape[1]]
    store(3, adamw(w_s[...], g_s, m_s[...], v_s[...]))


def update(at, own, sent, got, *params):
    outs = []
    for k in range(4):
        outs += [(params[3 * k].shape, F32)] * 3
    return kernel_call(
        update_kernel,
        tuple(outs),
        ((params[0].shape, F32),),
        16,
        2.4,
        1,
        at, own, sent, got, *params,
    )


def logit_order():
    order = np.zeros((GROWS, 128), np.float32)
    for t in range(TASKS):
        for k in range(SELECT):
            for b in range(BITS):
                order[(b * SELECT + k) * TPAD + t, (t * SELECT + k) * BITS + b] = 1.0
            at = (BITS * SELECT + k) * TPAD + t
            order[at, TASKS * SELECT * BITS + t * SELECT + k] = 1.0
    return order


def per_device(
    n_rows,
    n_hid,
    features,
    w_expand,
    w_reduce,
    biases,
    w_select,
    grad_mix,
    m_expand,
    v_expand,
    m_reduce,
    v_reduce,
    m_biases,
    v_biases,
    m_select,
    v_select,
):
    d_loc, experts, h_loc = w_expand.shape
    width = d_loc * n_rows
    mine_n = experts // 2
    chunk = mine_n // 2
    row = lax.axis_index("rows")
    hid_at = lax.axis_index("hid")
    core = hid_at % 2

    bits = n_rows.bit_length() - 1
    masks = [1 << b for b in range(bits)]
    side = (0, 2)
    sibling = ((0, 1), (0, 1))
    dims = [side] + [(m, 0) for m in masks]
    if n_rows == 8:
        way = ((3, 2, 0, 1), (3, 2, 1, 0))
        late_way = ((0, 3, 2, 1), (1, 3, 2, 0))
        back_way = ((2, 3, 0, 1), (1, 2, 3, 0))
    else:
        way = late_way = back_way = (tuple(range(len(dims))),) * 2

    def swap(x, hops):
        pairs = []
        for r in range(n_rows):
            for h in range(n_hid):
                mr, mh = hops[h % 2]
                pairs.append((r * n_hid + h, (r ^ mr) * n_hid + (h ^ mh)))
        return lax.ppermute(x, ("rows", "hid"), pairs)

    def hops(step):
        return tuple(dims[way[k][step]] for k in range(2))

    def late_hops(step):
        return tuple(dims[late_way[k][step]] for k in range(2))

    def back_hops(step):
        return tuple(dims[back_way[k][step]] for k in range(2))

    def table_of(pair):
        if n_rows != 8:
            return (tuple(range(16)),) * 2
        both = []
        for order in pair:
            spots = []
            for q in range(8):
                for s in range(2):
                    on = [s] + [(q >> b) & 1 for b in range(3)]
                    spots.append(sum(on[d] << order.index(d) for d in range(4)))
            both.append(tuple(spots))
        return tuple(both)

    order = jnp.asarray(logit_order(), BF)
    at = jnp.stack([core, row, hid_at]).astype(jnp.int32)

    def split_experts(x, axis):
        mine = lax.dynamic_slice_in_dim(x, core * mine_n, mine_n, axis)
        other = lax.dynamic_slice_in_dim(x, (1 - core) * mine_n, mine_n, axis)
        return mine, other

    def tie(x, *after):
        return lax.optimization_barrier((x, after))[0]

    part = n_rows // 8

    def canonical(lo, hi):
        w = jnp.concatenate([lo, hi], axis=0).reshape(8, part, 2, 2, chunk, d_loc, 2 * h_loc)
        w = jnp.transpose(w, (0, 2, 3, 4, 1, 5, 6)).reshape(2, -1, 2 * h_loc)
        return w[0], w[1]

    def uncanonical(lo, hi):
        if n_rows == 8:
            return lo, hi
        w = jnp.concatenate([lo, hi], axis=0).reshape(8, 2, 2, chunk, part, d_loc, 2 * h_loc)
        w = jnp.transpose(w, (0, 4, 1, 2, 3, 5, 6)).reshape(2, -1, 2 * h_loc)
        return w[0], w[1]

    w_r_view = jnp.transpose(w_reduce, (0, 2, 1))
    packed = pack(at, w_expand, w_r_view, biases, w_select, d_loc % 16 == 0)
    sel, b_own = packed[:2]
    if d_loc % 16 == 0:
        w_mine, w_other = packed[2:]
    else:
        w_mine, w_other = split_experts(
            jnp.stack([jnp.transpose(w_expand, (1, 0, 2)), w_r_view]).astype(BF), 1
        )
    w_recv = swap(w_other, sibling)
    n_b = b_own.shape[0]
    (b_own,) = join((((0, 0, n_b), (1, 0, n_b)),), b_own, swap(b_own, sibling))
    x_own = features
    g_own = jnp.transpose(grad_mix, (1, 0, 2))
    x_recv = swap(tie(x_own, w_recv), sibling)
    g_recv = swap(tie(g_own, w_recv), sibling)

    steps = len(dims)
    ride = n_rows == 8
    if ride:
        n = chunk * d_loc * 2
        a_msg, b_msg = chip_messages(w_mine, w_recv, sel)
        a_got = swap(a_msg, hops(0))
        (a_msg,) = join((((0, 0, n), (1, 0, n), (0, n, d_loc), (1, n, d_loc)),), a_msg, a_got)
        b_got = swap(b_msg, late_hops(0))
        a_got = swap(a_msg, hops(1))
        xt, gt, perm, to_q = turn(masks, at, x_own, x_recv, g_own, g_recv, (a_msg,))
        n *= 2
        tail = tuple((k, n, 2 * d_loc) for k in range(2)) + ((2, 0, 4 * experts),)
        (a_msg,) = join(
            (((0, 0, n), (1, 0, n)) + tail,), a_msg, a_got, b_own, after=(perm,)
        )
        a_got = swap(a_msg, hops(2))
        both = lambda x, y, after: join(
            (((0, 0, x.shape[0]), (1, 0, x.shape[0])),), x, y, after=after
        )[0]
        b_msg = both(b_msg, b_got, (a_msg,))
        b_got = swap(b_msg, late_hops(1))
        n *= 2
        a_lo, riders = join(
            (
                ((0, 0, n), (1, 0, n)),
                ((0, n, 4 * d_loc), (1, n, 4 * d_loc), (1, n + 4 * d_loc, 4 * experts)),
            ),
            a_msg, a_got,
        )
        a_hi = swap(a_lo, hops(3))
        turned = swap(riders, sibling)
        b_msg = both(b_msg, b_got, (a_lo,))
        b_got = swap(b_msg, late_hops(2))
    else:
        xt, gt, perm, to_q = turn(masks, at, x_own, x_recv, g_own, g_recv, (sel,))
        chip = jnp.concatenate([w_mine, w_recv], axis=3)
        bufs = [chip[None, :, :chunk], chip[None, :, chunk:]]
        for step in range(steps):
            gots = [swap(buf, hops(step)) for buf in bufs]
            if step + 1 < steps:
                bufs = [jnp.concatenate(pair, axis=0) for pair in zip(bufs, gots)]
        for m in masks:
            sel = jnp.concatenate([sel, swap(sel, ((m, 0), (m, 0)))], axis=0)
        riders = turned = jnp.concatenate([sel, swap(b_own, (side, side))], axis=0)
        (a_lo, a_hi), (b_lo, b_hi) = [canonical(*pair) for pair in zip(bufs, gots)]

    cc_a, gates, logits, selp, gb1_a, b0, b1 = prep(
        masks, ride, at, order, riders, turned, b_own, xt, gt
    )

    spots, back = table_of(way), table_of(back_way)
    cc_b, gb1_b = late(gates, gt, (b0,))
    if ride:
        b_lo = both(b_msg, b_got, (gb1_b,))
        b_hi = swap(b_lo, late_hops(3))
    first = critical(spots, back, at, a_lo, a_hi, xt, cc_a, b0, (b_lo,))
    a_lo, a_msg = uncanonical(first[0], first[1])
    a_got = swap(a_msg, back_hops(steps - 1))
    second = critical(
        table_of(late_way), back, at, b_lo, b_hi, xt, cc_b, b0, (first[0],), (first[6], gb1_a, gb1_b, to_q, perm)
    )
    b_lo, b_msg = second[:2]
    if not ride:
        n = b_lo.shape[0]
        b_lo, b_msg = uncanonical(b_lo, b_msg[:n])
        b_msg = jnp.concatenate([b_msg, second[1][n:]], axis=0)
    b_got = swap(b_msg, back_hops(steps - 1))
    ys_a, gl_a = outer(0, at, first[5], first[2], gt, logits, b1, after=(second[0],))
    a_lo, a_msg = fold(a_lo.shape[:1], a_lo, a_msg, a_got, after=(gl_a,))
    a_got = swap(a_msg, back_hops(steps - 2))
    ys_b, gls, gsel = outer(
        1, at, second[5], second[2], gt, logits, b1, order, (gl_a, xt, perm), (a_lo,)
    )
    gsel_got = swap(gsel, back_hops(steps - 1))
    a_lo, a_msg = fold(a_lo.shape[:1], a_lo, a_msg, a_got, after=(gsel,))
    a_got = swap(a_msg, back_hops(steps - 3))
    b_lo, b_msg = fold(b_lo.shape[:1], b_lo, b_msg, b_got, (gsel, gsel_got), (a_lo,))
    b_got = swap(b_msg, back_hops(steps - 2))
    ends = ((first[4], first[3], ys_a), (second[4], second[3], ys_b))
    n_own = x_own.shape[0]
    mix_other = mix(n_own, n_own, *ends, selp, gls, gates, (a_lo, b_lo))
    mix_recv = swap(mix_other, sibling)
    b_lo, b_msg = fold(b_lo.shape[:1], b_lo, b_msg, b_got, after=(mix_other,))
    b_got = swap(b_msg, back_hops(steps - 3))
    mix_own = mix(0, n_own, *ends, selp, gls, gates, (b_lo,))
    mixed, grad_features, token = final(masks, at, mix_own, mix_recv, (b_lo,))
    for step in reversed(range(1, steps - 3)):
        a_lo, a_msg = fold(a_lo.shape[:1], a_lo, a_msg, a_got)
        b_lo, b_msg = fold(b_lo.shape[:1], b_lo, b_msg, b_got)
        a_got, b_got = swap(a_msg, back_hops(step)), swap(b_msg, back_hops(step))
    lo, msg = pair_fold(a_lo, a_msg, a_got, b_lo, b_msg, b_got, (token,))
    got = swap(msg, back_hops(0))
    own, msg = last_fold(lo, msg, got)
    got = swap(msg, sibling)
    mixed = jnp.transpose(mixed, (1, 0, 2))

    flip = lambda x: jnp.transpose(x, (0, 2, 1))
    new = list(
        update(
            at, own, msg, got,
            w_expand, m_expand, v_expand,
            w_r_view, flip(m_reduce), flip(v_reduce),
            biases, m_biases, v_biases,
            w_select, m_select, v_select,
        )
    )
    new[3:6] = [flip(x) for x in new[3:6]]
    return (mixed, grad_features, *new)


def solution(mesh):
    row_split = P(("rows", "hid"), None)
    task_split = P(("rows", "hid"), None, None)
    expand = P("rows", None, "hid")
    reduce = P(None, "hid", "rows")
    bias = P(None, None, "hid")
    select = P("rows", None)
    return jax.shard_map(
        functools.partial(per_device, mesh.shape["rows"], mesh.shape["hid"]),
        mesh=mesh,
        in_specs=(
            row_split, expand, reduce, bias, select, task_split,
            expand, expand, reduce, reduce, bias, bias, select, select,
        ),
        out_specs=(
            task_split, row_split,
            expand, expand, expand,
            reduce, reduce, reduce,
            bias, bias, bias,
            select, select, select,
        ),
        check_vma=False,
    )
```
